32 devices in a mesh: dp: 8 (over z, y), tensor: 4 (over x, core).
Axes of the slice: x: 2, y: 2, z: 4, core: 2. Of those that a mesh axis runs over, the one named last changes fastest.
Arguments:
- band_patches: bfloat16 [64, 13, 256, 768], P('dp', None, 'tensor'), may hold values from -6 to 6
- band_counts: int32 [64], P('dp'), may hold values from 4 to 13
- visible_index: int32 [64, 64], P('dp'), may hold values from 0 to 255, as said below
- enc_attn_gain: float32 [768], replicated, may hold values from 0.5 to 1.5
- enc_attn_shift: float32 [768], replicated, may hold values from -1.75 to 1.75
- enc_qkv_weight: bfloat16 [3, 768, 768], P(None, 'tensor'), may hold values from -0.21875 to 0.21875
- enc_out_weight: bfloat16 [768, 768], P('tensor'), may hold values from -1.75 to 1.75
- enc_out_bias: float32 [768], replicated, may hold values from -1.75 to 1.75
- enc_mlp_gain: float32 [768], replicated, may hold values from 0.5 to 1.5
- enc_mlp_shift: float32 [768], replicated, may hold values from -1.75 to 1.75
- enc_up_weight: bfloat16 [768, 3072], P(None, 'tensor'), may hold values from -0.21875 to 0.21875
- enc_up_bias: float32 [3072], P('tensor'), may hold values from -3 to 3
- enc_down_weight: bfloat16 [3072, 768], P('tensor'), may hold values from -0.109375 to 0.109375
- enc_down_bias: float32 [768], replicated, may hold values from -1.75 to 1.75
- proj_weight: bfloat16 [768, 512], replicated, may hold values from -0.21875 to 0.21875
- proj_bias: float32 [512], replicated, may hold values from -1.75 to 1.75
- mask_token: float32 [512], replicated, may hold values from -6 to 6
- dec_attn_gain: float32 [512], replicated, may hold values from 0.5 to 1.5
- dec_attn_shift: float32 [512], replicated, may hold values from -1.75 to 1.75
- dec_qkv_weight: bfloat16 [3, 256, 512], P(None, 'tensor'), may hold values from -0.25 to 0.25
- dec_out_weight: bfloat16 [256, 512], P('tensor'), may hold values from -6 to 6
- dec_out_bias: float32 [512], replicated, may hold values from -1.75 to 1.75
- dec_mlp_gain: float32 [512], replicated, may hold values from 0.5 to 1.5
- dec_mlp_shift: float32 [512], replicated, may hold values from -1.75 to 1.75
- dec_up_weight: bfloat16 [512, 2048], P(None, 'tensor'), may hold values from -0.25 to 0.25
- dec_up_bias: float32 [2048], replicated, may hold values from -3 to 3
- dec_down_weight: bfloat16 [2048, 512], P('tensor'), may hold values from -0.125 to 0.125
- dec_down_bias: float32 [512], replicated, may hold values from -1.75 to 1.75
- cotangent: bfloat16 [64, 256, 512], P('dp'), may hold values from -8 to 8
Outputs:
- decoded: float32 [64, 256, 512], P('dp', None, 'tensor')
- band_grad: float32 [64, 13, 256, 768], P('dp', None, 'tensor')
- grad_enc_attn_gain: float32 [768], P('dp')
- grad_enc_attn_shift: float32 [768], P('dp')
- grad_enc_qkv_weight: float32 [3, 768, 768], P(None, 'tensor', 'dp')
- grad_enc_out_weight: float32 [768, 768], P('tensor', 'dp')
- grad_enc_out_bias: float32 [768], P('dp')
- grad_enc_mlp_gain: float32 [768], P('dp')
- grad_enc_mlp_shift: float32 [768], P('dp')
- grad_enc_up_weight: float32 [768, 3072], P('dp', 'tensor')
- grad_enc_up_bias: float32 [3072], P(('tensor', 'dp'))
- grad_enc_down_weight: float32 [3072, 768], P('tensor', 'dp')
- grad_enc_down_bias: float32 [768], P('dp')
- grad_proj_weight: float32 [768, 512], P('dp')
- grad_proj_bias: float32 [512], P('dp')
- grad_mask_token: float32 [512], P('dp')
- grad_dec_attn_gain: float32 [512], P('dp')
- grad_dec_attn_shift: float32 [512], P('dp')
- grad_dec_qkv_weight: float32 [3, 256, 512], P(None, 'tensor', 'dp')
- grad_dec_out_weight: float32 [256, 512], P('tensor', 'dp')
- grad_dec_out_bias: float32 [512], P('dp')
- grad_dec_mlp_gain: float32 [512], P('dp')
- grad_dec_mlp_shift: float32 [512], P('dp')
- grad_dec_up_weight: float32 [512, 2048], P('dp', 'tensor')
- grad_dec_up_bias: float32 [2048], P(('tensor', 'dp'))
- grad_dec_down_weight: float32 [2048, 512], P('tensor', 'dp')
- grad_dec_down_bias: float32 [512], P('dp')
The draws below stay inside these ranges and needn't reach their ends.
Inputs may be any that keep to these rules, and one draw needn't show every extreme that they name: `visible_index`: each row holds 64 different patch numbers in rising order.
All inputs are finite; a program needn't handle non-finite values.
Results may differ from the reference program's by a relative error of at most 0.029.
Values may be sent and summed in bfloat16 or wider, within the bound.
No kernel may reach another device: no remote copies, remote signals or barrier semaphores. Data moves between devices by JAX's collectives and lax.ppermute only.
A program may use at most 192 MiB of HBM per device.

```python
import functools
import math
import jax
import jax.numpy as jnp
from jax import lax

D_ENC = 768
HEADS_ENC = 12
HEAD = 64
FF_ENC = 3072
D_DEC = 512
HEADS_DEC = 4
FF_DEC = 2048
PATCHES = 256
BANDS = 13
VISIBLE = 64
CHIPS = 64


def draw_visible_index(key, part):
    key = jax.random.fold_in(key, 7)
    chip_keys = jax.random.split(key, CHIPS)
    orders = jax.vmap(lambda single: jax.random.permutation(single, PATCHES))(chip_keys)
    return jnp.sort(orders[:, :VISIBLE], axis=1).astype(jnp.int32)


def place_ends(values, own_key, least, largest):
    extent = values.shape
    spot = [jax.random.randint(jax.random.fold_in(own_key, axis), (), 0, extent[axis]) for axis in range(len(extent))]
    values = values.at[tuple(spot)].set(least)
    longest = extent.index(max(extent))
    spot[longest] = (spot[longest] + 1) % extent[longest]
    return values.at[tuple(spot)].set(largest)


def raised(result, key, source, target, blocks, factor):
    owner, partner = [(jnp.arange(result.shape[position]) // (result.shape[position] // blocks)).reshape([-1 if axis == position else 1 for axis in range(result.ndim)]) for position in (source, target)]
    chosen = jax.random.permutation(key, blocks)[partner]
    strong = (owner == chosen) | (owner == (partner + blocks // 2) % blocks)
    return jnp.where(strong, factor * result, result)


def block_levels(rng, dims, cuts, smallest, top_value):
    def one(axis_at, parts):
        heights = jax.random.uniform(jax.random.fold_in(jax.random.fold_in(rng, 6), axis_at), (parts,), jnp.float32, smallest / len(cuts), top_value / len(cuts))
        return jnp.repeat(jnp.exp(heights), dims[axis_at] // parts).reshape((-1,) + (1,) * (len(dims) - axis_at - 1))

    factor_of = one(*cuts[0])
    for cut in cuts[1:]:
        factor_of = factor_of * one(*cut)
    return factor_of


def normal_values(own_key, extent, spread, most, cuts=(), dtype=jnp.bfloat16):
    entries = spread * jax.random.normal(own_key, extent, jnp.float32)
    if cuts:
        entries = entries * block_levels(own_key, extent, cuts, -0.22, 0.18)
    return jnp.clip(entries, -most, most).astype(dtype)


def bell_draw_with(own_key, dims, deviation, reach, cuts, heavy, held_as=jnp.bfloat16):
    entries = deviation * jax.random.normal(own_key, dims, jnp.float32)
    if cuts:
        entries = entries * block_levels(own_key, dims, cuts, -0.22, 0.18)
    return jnp.clip(raised(entries, jax.random.fold_in(own_key, 3), *heavy), -reach, reach).astype(held_as)


def setup_inputs(seed: int = 0) -> dict:
    arg_keys = jax.random.split(jax.random.key(seed), 30)
    return {
        "band_patches": normal_values(arg_keys[0], (CHIPS, BANDS, PATCHES, D_ENC), 1.0, 6.0, ((0, 8), (2, 4))),
        "band_counts": place_ends(jax.random.randint(arg_keys[1], (CHIPS,), 4, BANDS + 1), jax.random.fold_in(arg_keys[1], 1), 4, BANDS).astype(jnp.int32),
        "visible_index": draw_visible_index(jax.random.fold_in(arg_keys[29], 71), 0),
        "enc_attn_gain": jnp.clip(1.0 + 0.1 * jax.random.normal(arg_keys[3], (D_ENC,), jnp.float32), 0.5, 1.5),
        "enc_attn_shift": normal_values(arg_keys[4], (D_ENC,), 0.3, 1.75, (), jnp.float32),
        "enc_qkv_weight": normal_values(arg_keys[5], (3, HEADS_ENC * HEAD, D_ENC), D_ENC ** -0.5, 0.21875, ((1, 4),)),
        "enc_out_weight": normal_values(arg_keys[6], (HEADS_ENC * HEAD, D_ENC), (HEADS_ENC * HEAD // VISIBLE) ** -0.5, 1.75, ((0, 4),)),
        "enc_out_bias": normal_values(arg_keys[7], (D_ENC,), 0.3, 1.75, (), jnp.float32),
        "enc_mlp_gain": jnp.clip(1.0 + 0.1 * jax.random.normal(arg_keys[8], (D_ENC,), jnp.float32), 0.5, 1.5),
        "enc_mlp_shift": normal_values(arg_keys[9], (D_ENC,), 0.3, 1.75, (), jnp.float32),
        "enc_up_weight": normal_values(arg_keys[10], (D_ENC, FF_ENC), D_ENC ** -0.5, 0.21875, ((1, 4),)),
        "enc_up_bias": normal_values(arg_keys[11], (FF_ENC,), 0.5, 3.0, ((0, 4),), jnp.float32),
        "enc_down_weight": normal_values(arg_keys[12], (FF_ENC, D_ENC), FF_ENC ** -0.5, 0.109375, ((0, 4),)),
        "enc_down_bias": normal_values(arg_keys[13], (D_ENC,), 0.3, 1.75, (), jnp.float32),
        "proj_weight": normal_values(arg_keys[14], (D_ENC, D_DEC), D_ENC ** -0.5, 0.21875),
        "proj_bias": normal_values(arg_keys[15], (D_DEC,), 0.3, 1.75, (), jnp.float32),
        "mask_token": normal_values(arg_keys[16], (D_DEC,), 1.0, 6.0, (), jnp.float32),
        "dec_attn_gain": jnp.clip(1.0 + 0.1 * jax.random.normal(arg_keys[17], (D_DEC,), jnp.float32), 0.5, 1.5),
        "dec_attn_shift": normal_values(arg_keys[18], (D_DEC,), 0.3, 1.75, (), jnp.float32),
        "dec_qkv_weight": normal_values(arg_keys[19], (3, HEADS_DEC * HEAD, D_DEC), D_DEC ** -0.5, 0.25, ((1, 4),)),
        "dec_out_weight": normal_values(arg_keys[20], (HEADS_DEC * HEAD, D_DEC), (max(HEADS_DEC * HEAD // PATCHES, 1)) ** -0.5, 6.0, ((0, 4),)),
        "dec_out_bias": normal_values(arg_keys[21], (D_DEC,), 0.3, 1.75, (), jnp.float32),
        "dec_mlp_gain": jnp.clip(1.0 + 0.1 * jax.random.normal(arg_keys[22], (D_DEC,), jnp.float32), 0.5, 1.5),
        "dec_mlp_shift": normal_values(arg_keys[23], (D_DEC,), 0.3, 1.75, (), jnp.float32),
        "dec_up_weight": normal_values(arg_keys[24], (D_DEC, FF_DEC), D_DEC ** -0.5, 0.25, ((1, 4),)),
        "dec_up_bias": normal_values(arg_keys[25], (FF_DEC,), 0.5, 3.0, (), jnp.float32),
        "dec_down_weight": normal_values(arg_keys[26], (FF_DEC, D_DEC), FF_DEC ** -0.5, 0.125, ((0, 4),)),
        "dec_down_bias": normal_values(arg_keys[27], (D_DEC,), 0.3, 1.75, (), jnp.float32),
        "cotangent": bell_draw_with(arg_keys[28], (CHIPS, PATCHES, D_DEC), 1.0, 8.0, ((0, 8),), (0, 2, 8, 2.0)),
    }


@jax.custom_vjp
def low(v):
    return lax.optimization_barrier(v.astype(jnp.bfloat16)).astype(jnp.float32)

@jax.custom_vjp
def low_back(v):
    return v

def low_keep(v):
    return (low(v), None)

def low_pass(kept, grad):
    return (grad,)

def back_keep(v):
    return (v, None)

def back_low(kept, grad):
    return (low(grad),)
low.defvjp(low_keep, low_pass)
low_back.defvjp(back_keep, back_low)
EPSILON = 1e-05
HIGHEST = lax.Precision.HIGHEST

def round_both(values):
    return low(low_back(values))

def layer_norm(stream, gain, shift):
    center = stream - lax.optimization_barrier(jnp.mean(stream, -1, keepdims=True))
    inverse = lax.rsqrt(lax.optimization_barrier(jnp.mean(center * center, -1, keepdims=True)) + EPSILON)
    return center * inverse * gain + shift

def sincos_table(count, width):
    places = lax.broadcasted_iota(jnp.float32, (count, width // 2), 0)
    orders = lax.broadcasted_iota(jnp.float32, (count, width // 2), 1)
    angles = places * jnp.exp(orders * (-math.log(10000.0) / (width // 2)))
    return jnp.concatenate([jnp.sin(angles), jnp.cos(angles)], 1)

def ref_block(stream, params):
    attn_gain, attn_shift, qkv_weight, out_weight, out_bias, mlp_gain, mlp_shift, up_weight, up_bias, down_weight, down_bias = params
    chip_count, length, _ = stream.shape
    inner_width = qkv_weight.shape[1]
    normed = low(layer_norm(stream, attn_gain, attn_shift))
    qkv = round_both(jnp.einsum('csd,tid->csti', normed, qkv_weight, precision=HIGHEST))
    shaped = qkv.reshape(chip_count, length, 3, inner_width // HEAD, HEAD)
    queries = shaped[:, :, 0]
    keyset = shaped[:, :, 1]
    valset = shaped[:, :, 2]
    scores = low_back(jnp.einsum('cqhe,ckhe->chqk', queries, keyset, precision=HIGHEST) * HEAD ** (-0.5))
    prob_low = low(jax.nn.softmax(scores, -1))
    mixed_rows = round_both(jnp.einsum('chqk,ckhe->cqhe', prob_low, valset, precision=HIGHEST))
    mixed_rows = mixed_rows.reshape(chip_count, length, inner_width)
    middle = stream + low_back(jnp.einsum('csi,id->csd', mixed_rows, out_weight, precision=HIGHEST)) + out_bias
    mlp_normed = low(layer_norm(middle, mlp_gain, mlp_shift))
    hidden = low_back(jnp.einsum('csd,df->csf', mlp_normed, up_weight, precision=HIGHEST)) + up_bias
    activation = low(jax.nn.gelu(hidden, approximate=False))
    return middle + low_back(jnp.einsum('csf,fd->csd', activation, down_weight, precision=HIGHEST)) + down_bias

def forward(band_values, enc_params, proj_params, dec_params, band_counts, visible_index):
    proj_weight, proj_bias, mask_token = proj_params
    chip_count = band_values.shape[0]
    band_used = (lax.broadcasted_iota(jnp.int32, (chip_count, band_values.shape[1]), 1) < band_counts[:, None]).astype(jnp.float32)
    counts_float = band_counts.astype(jnp.float32)[:, None, None]
    band_mean = low(jnp.einsum('cb,cbpd->cpd', band_used, band_values, precision=HIGHEST) / counts_float)
    tokens = jnp.take_along_axis(band_mean, visible_index[:, :, None], axis=1)
    enc_out = ref_block(tokens, enc_params)
    enc_low = low(enc_out)
    latent = low_back(jnp.einsum('cvd,de->cve', enc_low, proj_weight, precision=HIGHEST)) + proj_bias
    patches = band_values.shape[2]
    dec_width = proj_weight.shape[1]
    chip_rows = lax.broadcasted_iota(jnp.int32, visible_index.shape, 0)
    base = jnp.broadcast_to(mask_token, (chip_count, patches, dec_width))
    decoder_in = base.at[chip_rows, visible_index].set(latent) + sincos_table(patches, dec_width)
    return ref_block(decoder_in, dec_params)

def reference(band_patches, band_counts, visible_index, enc_attn_gain, enc_attn_shift, enc_qkv_weight, enc_out_weight, enc_out_bias, enc_mlp_gain, enc_mlp_shift, enc_up_weight, enc_up_bias, enc_down_weight, enc_down_bias, proj_weight, proj_bias, mask_token, dec_attn_gain, dec_attn_shift, dec_qkv_weight, dec_out_weight, dec_out_bias, dec_mlp_gain, dec_mlp_shift, dec_up_weight, dec_up_bias, dec_down_weight, dec_down_bias, cotangent):
    as_float = lambda values: values.astype(jnp.float32)
    enc_params = tuple((as_float(item) for item in (enc_attn_gain, enc_attn_shift, enc_qkv_weight, enc_out_weight, enc_out_bias, enc_mlp_gain, enc_mlp_shift, enc_up_weight, enc_up_bias, enc_down_weight, enc_down_bias)))
    proj_params = tuple((as_float(item) for item in (proj_weight, proj_bias, mask_token)))
    dec_params = tuple((as_float(item) for item in (dec_attn_gain, dec_attn_shift, dec_qkv_weight, dec_out_weight, dec_out_bias, dec_mlp_gain, dec_mlp_shift, dec_up_weight, dec_up_bias, dec_down_weight, dec_down_bias)))
    bound = functools.partial(forward, band_counts=band_counts, visible_index=visible_index)
    decoded, pullback = jax.vjp(bound, as_float(band_patches), enc_params, proj_params, dec_params)
    band_grad, enc_grads, proj_grads, dec_grads = pullback(as_float(cotangent))
    return (decoded, band_grad, enc_grads[0], enc_grads[1], enc_grads[2], enc_grads[3], enc_grads[4], enc_grads[5], enc_grads[6], enc_grads[7], enc_grads[8], enc_grads[9], enc_grads[10], proj_grads[0], proj_grads[1], proj_grads[2], dec_grads[0], dec_grads[1], dec_grads[2], dec_grads[3], dec_grads[4], dec_grads[5], dec_grads[6], dec_grads[7], dec_grads[8], dec_grads[9], dec_grads[10])
```

```python
import functools
import math

import jax
import jax.numpy as jnp
from jax import lax
from jax.experimental import pallas as pl
from jax.experimental.pallas import tpu as pltpu
from jax.sharding import PartitionSpec as P

HEAD = 64
EPSILON = 1e-05
SCALE = HEAD ** (-0.5)
VMEM_BYTES = 52 * 1024 * 1024
F32 = jnp.float32
LOW = jnp.bfloat16
NN = (((1,), (0,)), ((), ()))
NT = (((1,), (1,)), ((), ()))
TN = (((0,), (0,)), ((), ()))
VEC_ROWS = 16


def dot(left, right, dims=NN):
    return lax.dot_general(left, right, dims, preferred_element_type=F32)


def col_sum(values):
    return jnp.sum(values, 0, keepdims=True)


def norm_parts(stream):
    center = stream - jnp.mean(stream, -1, keepdims=True)
    inverse = lax.rsqrt(jnp.mean(center * center, -1, keepdims=True) + EPSILON)
    return center * inverse, inverse


def norm_back(grad, xhat, inverse, gain):
    scaled = grad * gain
    mean_q = jnp.mean(scaled, -1, keepdims=True)
    mean_qx = jnp.mean(scaled * xhat, -1, keepdims=True)
    return inverse * (scaled - mean_q - xhat * mean_qx)


def gelu_parts(hidden):
    phi = 0.5 + 0.5 * lax.erf(hidden * (0.5**0.5))
    density = jnp.exp(hidden * hidden * -0.5) * (1.0 / math.sqrt(2.0 * math.pi))
    return hidden * phi, phi + hidden * density


def softmax_rows(scores):
    weights = jnp.exp(scores - jnp.max(scores, -1, keepdims=True))
    return weights * (1.0 / jnp.sum(weights, -1, keepdims=True))


def same_chip(rows, length):
    first = lax.broadcasted_iota(jnp.int32, (rows, rows), 0) // length
    second = lax.broadcasted_iota(jnp.int32, (rows, rows), 1) // length
    return first == second


def attend(queries, keyset, mask):
    scores = dot(queries, keyset, NT) * SCALE
    if mask is not None:
        scores = jnp.where(mask, scores, -1e30)
    return softmax_rows(scores)


def attend_back(probs, queries, keyset, valset, grad_mixed):
    grad_probs = dot(grad_mixed, valset, NT)
    grad_values = dot(probs.astype(LOW), grad_mixed, TN)
    grad_scores = probs * (grad_probs - jnp.sum(grad_probs * probs, -1, keepdims=True))
    score_low = grad_scores.astype(LOW)
    grad_queries = dot(score_low, keyset) * SCALE
    grad_keys = dot(score_low, queries, TN) * SCALE
    return grad_queries.astype(LOW), grad_keys.astype(LOW), grad_values.astype(LOW)


def call(body, out_shape, args, scalars=(), flops=0, name=None):
    specs = [pl.BlockSpec(memory_space=pltpu.SMEM) for _ in scalars]
    specs += [pl.BlockSpec(memory_space=pltpu.VMEM) for _ in args]
    moved = sum(math.prod(a.shape) * a.dtype.itemsize for a in list(args) + list(out_shape))
    return pl.pallas_call(
        body,
        out_shape=out_shape,
        in_specs=specs,
        out_specs=[pl.BlockSpec(memory_space=pltpu.VMEM) for _ in out_shape],
        compiler_params=pltpu.CompilerParams(vmem_limit_bytes=VMEM_BYTES),
        cost_estimate=pl.CostEstimate(flops=flops, bytes_accessed=moved, transcendentals=0),
        name=name,
    )(*scalars, *args)


def bit_reverse(value, bits):
    result = 0
    for place in range(bits):
        result = result | (((value >> place) & 1) << (bits - 1 - place))
    return result


def put_block(keep, send, lead, place, half, rows, columns, values):
    @pl.when(place < half)
    def _():
        keep[lead + (place, rows, columns)] = values

    @pl.when(place >= half)
    def _():
        send[lead + (place - half, rows, columns)] = values


def band_mean_kernel(place_ref, count_ref, bands_ref, visible_ref, out_ref, *, own_chips):
    spot, rank = chip_of(pl.program_id(0), place_ref[0], own_chips), place_ref[0]
    count = count_ref[spot]
    own = bands_ref.shape[2]
    total = bands_ref[0, 0].astype(F32)
    for band in range(1, bands_ref.shape[1]):
        used = jnp.where(band < count, 1.0, 0.0).astype(F32)
        total = total + bands_ref[0, band].astype(F32) * used
    mean = (total / count.astype(F32)).astype(LOW)
    patch = lax.broadcasted_iota(jnp.int32, (visible_ref.shape[1], own), 1) + rank * own
    chosen = jnp.where(visible_ref[0] == patch, 1.0, 0.0).astype(LOW)
    out_ref[0] = dot(chosen, mean).astype(LOW)


def chip_of(step, rank, own_chips):
    part, index = step // own_chips, step % own_chips
    apart = 2 * (part % 2) + part // 2
    return (rank ^ apart) * own_chips + index


def band_mean(place, counts, bands, visible, own_chips):
    chips, band_count, own, width = bands.shape
    length = visible.shape[1]
    grid_spec = pltpu.PrefetchScalarGridSpec(
        num_scalar_prefetch=2,
        grid=(chips,),
        in_specs=[
            pl.BlockSpec(
                (1, band_count, own, width), lambda g, p, c: (chip_of(g, p[0], own_chips), 0, 0, 0)
            ),
            pl.BlockSpec((1, length, 1), lambda g, p, c: (chip_of(g, p[0], own_chips), 0, 0)),
        ],
        out_specs=pl.BlockSpec((1, length, width), lambda g, p, c: (g, 0, 0)),
    )
    return pl.pallas_call(
        functools.partial(band_mean_kernel, own_chips=own_chips),
        grid_spec=grid_spec,
        out_shape=jax.ShapeDtypeStruct((chips, length, width), LOW),
        compiler_params=pltpu.CompilerParams(vmem_limit_bytes=VMEM_BYTES),
        cost_estimate=pl.CostEstimate(
            flops=bands.size, bytes_accessed=2 * bands.size, transcendentals=0
        ),
        name="band_mean",
    )(place, counts, bands, visible[:, :, None])


def enc_attn_kernel(
    tok_a, tok_b, gain, shift, qkv_w, out_w, part_a, part_b, normed_ref, qkv_ref, mixed_ref, *, length
):
    rows = tok_a.shape[0]
    inner = out_w.shape[0]
    mask = same_chip(rows, length)
    for group, (tok, part) in enumerate(((tok_a, part_a), (tok_b, part_b))):
        span = slice(group * rows, (group + 1) * rows)
        xhat, _ = norm_parts(tok[...].astype(F32))
        normed = (xhat * gain[...] + shift[...]).astype(LOW)
        normed_ref[span] = normed
        qkv = dot(normed, qkv_w[...], NT).astype(LOW)
        qkv_ref[span] = qkv
        heads = []
        for head in range(inner // HEAD):
            at = [qkv[:, k * inner + head * HEAD : k * inner + (head + 1) * HEAD] for k in range(3)]
            probs = attend(at[0], at[1], mask)
            heads.append(dot(probs.astype(LOW), at[2]).astype(LOW))
        mixed = jnp.concatenate(heads, 1)
        mixed_ref[span] = mixed
        part[...] = dot(mixed, out_w[...]).astype(LOW)


def enc_mlp_kernel(
    tok_a, tok_b, sum_a, sum_b, out_bias, gain, shift, up_w, up_bias, down_w,
    part_a, part_b, normed_ref, act_ref, slope_ref,
):
    rows = tok_a.shape[0]
    groups = ((tok_a, sum_a, part_a), (tok_b, sum_b, part_b))
    for group, (tok, total, part) in enumerate(groups):
        span = slice(group * rows, (group + 1) * rows)
        middle = tok[...].astype(F32) + total[...].astype(F32) + out_bias[...]
        xhat, _ = norm_parts(middle)
        normed = (xhat * gain[...] + shift[...]).astype(LOW)
        normed_ref[span] = normed
        activation, slope = gelu_parts(dot(normed, up_w[...]) + up_bias[...])
        act_low = activation.astype(LOW)
        act_ref[span] = act_low
        slope_ref[span] = slope.astype(LOW)
        part[...] = dot(act_low, down_w[...]).astype(LOW)


def enc_mlp_back_kernel(
    lat_a, lat_b, proj_w, slope_ref, up_w, down_w,
    part_a, part_b, out_a, out_b, low_ref, hidden_ref, vec_ref,
):
    rows = lat_a.shape[0]
    down_sum, up_sum = 0.0, 0.0
    groups = ((lat_a, out_a, part_a), (lat_b, out_b, part_b))
    for group, (lat, out, part) in enumerate(groups):
        span = slice(group * rows, (group + 1) * rows)
        grad_out = dot(lat[...], proj_w[...], NT)
        out[...] = grad_out
        grad_low = grad_out.astype(LOW)
        low_ref[span] = grad_low
        grad_hidden = dot(grad_low, down_w[...], NT) * slope_ref[span].astype(F32)
        hidden_low = grad_hidden.astype(LOW)
        hidden_ref[span] = hidden_low
        down_sum = down_sum + col_sum(grad_out)
        up_sum = up_sum + col_sum(grad_hidden)
        part[...] = dot(hidden_low, up_w[...], NT).astype(LOW)
    vec_ref[...] = jnp.concatenate(
        [down_sum, up_sum, jnp.zeros((vec_ref.shape[0] - 2, down_sum.shape[1]), F32)], 0
    )


def enc_mlp_weights_kernel(
    place_ref, normed_ref, hidden_ref, low_ref, act_ref, lat_a, lat_b, enc_a, enc_b, keep, send
):
    half = keep.shape[0]
    blocks, bits = 2 * half, (2 * half).bit_length() - 1
    width, hidden = normed_ref.shape[1], hidden_ref.shape[1]
    proj_own = keep.shape[2] - 2 * hidden
    own = pl.ds(pl.multiple_of(place_ref[0] * proj_own, proj_own), proj_own)
    up = dot(normed_ref[...], hidden_ref[...], TN).astype(LOW)
    down = dot(low_ref[...], act_ref[...], TN).astype(LOW)
    proj = (dot(enc_a[...], lat_a[:, own], TN) + dot(enc_b[...], lat_b[:, own], TN)).astype(LOW)
    piece = width // blocks
    for block in range(blocks):
        at = slice(block * piece, (block + 1) * piece)
        values = jnp.concatenate([up[at], down[at], proj[at]], 1)
        place = place_ref[1] ^ bit_reverse(block, bits)
        put_block(keep, send, (), place, half, slice(0, piece), slice(None), values)


def enc_attn_back_kernel(
    tok_a, tok_b, sum_a, sum_b, out_bias, mlp_gain, out_a, out_b, back_a, back_b,
    qkv_ref, qkv_w, out_w, part_a, part_b, mid_a, mid_b, low_ref, grad_qkv_ref, vec_ref, *, length
):
    rows = tok_a.shape[0]
    inner = out_w.shape[0]
    mask = same_chip(rows, length)
    sums = [0.0] * 5
    groups = (
        (tok_a, sum_a, out_a, back_a, part_a, mid_a),
        (tok_b, sum_b, out_b, back_b, part_b, mid_b),
    )
    for group, (tok, total, out, back, part, mid) in enumerate(groups):
        span = slice(group * rows, (group + 1) * rows)
        stream = tok[...].astype(F32)
        xhat, inverse = norm_parts(stream + total[...].astype(F32) + out_bias[...])
        grad = back[...].astype(F32)
        sums[0] = sums[0] + col_sum(grad * xhat)
        sums[1] = sums[1] + col_sum(grad)
        grad_middle = out[...] + norm_back(grad, xhat, inverse, mlp_gain[...])
        mid[...] = grad_middle
        sums[2] = sums[2] + col_sum(grad_middle)
        middle_low = grad_middle.astype(LOW)
        low_ref[span] = middle_low
        grad_mixed = dot(middle_low, out_w[...], NT).astype(LOW)
        grads = ([], [], [])
        for head in range(inner // HEAD):
            at = [
                qkv_ref[span, k * inner + head * HEAD : k * inner + (head + 1) * HEAD]
                for k in range(3)
            ]
            probs = attend(at[0], at[1], mask)
            found = attend_back(probs, *at, grad_mixed[:, head * HEAD : (head + 1) * HEAD])
            for kind in range(3):
                grads[kind].append(found[kind])
        grad_qkv = jnp.concatenate(grads[0] + grads[1] + grads[2], 1)
        grad_qkv_ref[span] = grad_qkv
        partial = dot(grad_qkv, qkv_w[...])
        part[...] = partial.astype(LOW)
        xhat, _ = norm_parts(stream)
        sums[3] = sums[3] + col_sum(partial * xhat)
        sums[4] = sums[4] + col_sum(partial)
    vec_ref[...] = jnp.concatenate(
        sums + [jnp.zeros((vec_ref.shape[0] - 5, sums[0].shape[1]), F32)], 0
    )


def enc_attn_weights_kernel(
    place_ref, normed_ref, grad_qkv_ref, low_ref, mixed_ref, vec_mlp, vec_attn, keep, send
):
    half = keep.shape[0]
    blocks, bits = 2 * half, (2 * half).bit_length() - 1
    width = normed_ref.shape[1]
    qkv = dot(normed_ref[...], grad_qkv_ref[...], TN).astype(LOW)
    out = dot(low_ref[...], mixed_ref[...], TN).astype(LOW)
    vectors = jnp.concatenate([vec_mlp[...], vec_attn[...]], 0)
    piece = width // blocks
    first = keep.shape[1] - VEC_ROWS
    for block in range(blocks):
        at = slice(block * piece, (block + 1) * piece)
        place = place_ref[1] ^ bit_reverse(block, bits)
        values = jnp.concatenate([qkv[at], out[at]], 1)
        put_block(keep, send, (), place, half, slice(0, piece), slice(None), values)
        put_block(
            keep, send, (), place, half, slice(first, first + VEC_ROWS), slice(0, piece),
            vectors[:, at].astype(LOW),
        )


def band_grad_kernel(
    place_ref, count_ref, tok_ref, back_ref, mid_ref, gain, visible_ref, out_ref, *, own_chips
):
    rank = place_ref[0]
    count = count_ref[chip_of(pl.program_id(0), rank, own_chips)]
    xhat, inverse = norm_parts(tok_ref[0].astype(F32))
    grad = mid_ref[0] + norm_back(back_ref[0].astype(F32), xhat, inverse, gain[...])
    grad = grad / count.astype(F32)
    own, length = out_ref.shape[2], visible_ref.shape[2]
    patch = lax.broadcasted_iota(jnp.int32, (own, length), 0) + rank * own
    chosen = jnp.where(visible_ref[0] == patch, 1.0, 0.0).astype(LOW)
    high = grad.astype(LOW)
    rest = (grad - high.astype(F32)).astype(LOW)
    spread = dot(chosen, high) + dot(chosen, rest)
    for band in range(out_ref.shape[1]):
        used = jnp.where(band < count, 1.0, 0.0).astype(F32)
        out_ref[0, band] = spread * used


def band_grad_call(place, counts, tokens, back, mid, gain, visible, bands, own_chips):
    chips, band_count, own, width = bands
    length = visible.shape[1]
    by_step = pl.BlockSpec((1, length, width), lambda g, p, c: (g, 0, 0))
    grid_spec = pltpu.PrefetchScalarGridSpec(
        num_scalar_prefetch=2,
        grid=(chips,),
        in_specs=[
            by_step,
            by_step,
            by_step,
            pl.BlockSpec((1, width), lambda g, p, c: (0, 0)),
            pl.BlockSpec((1, 1, length), lambda g, p, c: (chip_of(g, p[0], own_chips), 0, 0)),
        ],
        out_specs=pl.BlockSpec(
            (1, band_count, own, width), lambda g, p, c: (chip_of(g, p[0], own_chips), 0, 0, 0)
        ),
    )
    return pl.pallas_call(
        functools.partial(band_grad_kernel, own_chips=own_chips),
        grid_spec=grid_spec,
        out_shape=jax.ShapeDtypeStruct(bands, F32),
        compiler_params=pltpu.CompilerParams(vmem_limit_bytes=VMEM_BYTES),
        cost_estimate=pl.CostEstimate(
            flops=0, bytes_accessed=4 * math.prod(bands), transcendentals=0
        ),
        name="band_grad",
    )(place, counts, tokens, back, mid, gain, visible[:, None, :])


def dec_kernel(
    place_ref, enc_low, proj_w, proj_bias, mask_token, position, visible_col, visible_row,
    attn_gain, attn_shift, out_bias, mlp_gain, mlp_shift, up_bias, down_bias,
    w0, w1, w2, w3, cotangent,
    decoded_keep, decoded_send, grad_latent_ref, n1_ref, n2_ref, gml_ref, act_ref, hid_ref,
    gqkv_ref, mixed_ref, vec_ref, upvec_ref,
    slope_scr, prob_scr,
):
    weights = (w0, w1, w2, w3)
    patches, width = position.shape
    kinds = 3 * HEAD
    inner = kinds + HEAD
    units = up_bias.shape[2]
    up_at, down_at = slice(inner, inner + width), slice(inner + width, inner + width + units)
    step = pl.program_id(0)
    latent = dot(enc_low[0], proj_w[...]) + proj_bias[...]
    length = latent.shape[0]
    hit = lax.broadcasted_iota(jnp.int32, (patches, length), 0) == visible_row[0]
    chosen = jnp.where(hit, 1.0, 0.0).astype(LOW)
    is_visible = jnp.sum(jnp.where(hit, 1.0, 0.0), 1, keepdims=True)
    high = latent.astype(LOW)
    rest = (latent - high.astype(F32)).astype(LOW)
    stream = dot(chosen, high) + dot(chosen, rest)
    stream = stream + (1.0 - is_visible) * mask_token[...] + position[...]
    xhat1, inverse1 = norm_parts(stream)
    n1 = (xhat1 * attn_gain[...] + attn_shift[...]).astype(LOW)
    n1_ref[...] = n1
    qkvs, mixed = [], []
    for part, weight in enumerate(weights):
        qkv = dot(n1, weight[0:kinds], NT).astype(LOW)
        at = [qkv[:, k * HEAD : (k + 1) * HEAD] for k in range(3)]
        probs = attend(at[0], at[1], None)
        prob_scr[part] = probs
        mixed_one = dot(probs.astype(LOW), at[2]).astype(LOW)
        mixed_ref[part] = mixed_one
        qkvs.append(at)
        mixed.append(mixed_one)
    out_all = jnp.concatenate([weight[kinds:inner] for weight in weights], 0)
    middle = stream + dot(jnp.concatenate(mixed, 1), out_all) + out_bias[...]
    xhat2, inverse2 = norm_parts(middle)
    n2 = (xhat2 * mlp_gain[...] + mlp_shift[...]).astype(LOW)
    n2_ref[...] = n2
    total = middle + down_bias[...]
    for part, weight in enumerate(weights):
        activation, slope = gelu_parts(dot(n2, weight[up_at]) + up_bias[part])
        act_low = activation.astype(LOW)
        act_ref[part] = act_low
        slope_scr[part] = slope.astype(LOW)
        total = total + dot(act_low, weight[down_at])
    parts = len(weights)
    column = width // parts
    for part in range(parts):
        values = total[:, part * column : (part + 1) * column].astype(LOW)
        apart = place_ref[0] ^ part

        @pl.when(apart % 2 == 0)
        def _(values=values, apart=apart):
            decoded_keep[apart // 2, 0] = values

        @pl.when(apart % 2 == 1)
        def _(values=values, apart=apart):
            decoded_send[apart // 2, 0] = values

    grad_low = cotangent[0]
    grad_out = grad_low.astype(F32)
    grad_n2 = 0.0
    up_sums = []
    for part, weight in enumerate(weights):
        grad_hidden = dot(grad_low, weight[down_at], NT) * slope_scr[part].astype(F32)
        hidden_low = grad_hidden.astype(LOW)
        hid_ref[part] = hidden_low
        up_sums.append(col_sum(grad_hidden))
        grad_n2 = grad_n2 + dot(hidden_low, weight[up_at], NT)
    grad_middle = grad_out + norm_back(grad_n2, xhat2, inverse2, mlp_gain[...])
    mlp_gain_sum, mlp_shift_sum = col_sum(grad_n2 * xhat2), col_sum(grad_n2)
    middle_low = grad_middle.astype(LOW)
    gml_ref[...] = middle_low
    grad_mixed = dot(middle_low, out_all, NT).astype(LOW)
    grad_n1 = 0.0
    for part, weight in enumerate(weights):
        own = grad_mixed[:, part * HEAD : (part + 1) * HEAD]
        grad_qkv = jnp.concatenate(attend_back(prob_scr[part], *qkvs[part], own), 1)
        gqkv_ref[part] = grad_qkv
        grad_n1 = grad_n1 + dot(grad_qkv, weight[0:kinds])
    grad_stream = grad_middle + norm_back(grad_n1, xhat1, inverse1, attn_gain[...])
    pick = lax.broadcasted_iota(jnp.int32, (length, patches), 1) == visible_col[0]
    grad_latent_ref[0] = dot(
        jnp.where(pick, 1.0, 0.0).astype(LOW), grad_stream.astype(LOW)
    ).astype(LOW)
    seen_sum = col_sum(grad_stream * is_visible)
    vectors = jnp.concatenate(
        [
            col_sum(grad_n1 * xhat1),
            col_sum(grad_n1),
            col_sum(grad_middle),
            mlp_gain_sum,
            mlp_shift_sum,
            col_sum(grad_out),
            seen_sum,
            col_sum(grad_stream) - seen_sum,
        ],
        0,
    )
    ups = jnp.concatenate(up_sums + [jnp.zeros((4, units), F32)], 0)

    @pl.when(step == 0)
    def _():
        vec_ref[...] = vectors
        upvec_ref[...] = ups

    @pl.when(step > 0)
    def _():
        vec_ref[...] += vectors
        upvec_ref[...] += ups


def dec_call(place, enc_low, small, position, visible, up_bias, weights, cotangent):
    chips, length, enc_width = enc_low.shape
    patches, width = position.shape
    parts, units = up_bias.shape[0], up_bias.shape[2]
    rows = chips * patches
    column = width // parts
    proj_w, proj_bias, mask_token, rest = small

    def whole(array):
        dims = array.ndim
        return pl.BlockSpec(array.shape, lambda i, p: (0,) * dims)

    def by_chip(shape):
        return pl.BlockSpec((1,) + shape[1:], lambda i, p: (i, 0, 0))

    def by_rows(columns):
        return pl.BlockSpec((patches, columns), lambda i, p: (i, 0))

    def by_part(columns):
        return pl.BlockSpec((parts, patches, columns), lambda i, p: (0, i, 0))

    visible_col, visible_row = visible[:, :, None], visible[:, None, :]
    whole_args = [proj_w, proj_bias, mask_token, position]
    args = [enc_low, *whole_args, visible_col, visible_row, *rest[:5], up_bias, rest[5], *weights]
    specs = [by_chip(enc_low.shape)] + [whole(a) for a in whole_args]
    specs += [by_chip(visible_col.shape), by_chip(visible_row.shape)]
    specs += [whole(a) for a in args[7:]]
    args.append(cotangent)
    specs.append(by_chip(cotangent.shape))
    half = parts // 2
    decoded_spec = pl.BlockSpec((half, 1, patches, column), lambda i, p: (0, i, 0, 0))
    shape = jax.ShapeDtypeStruct
    out_shape = [
        shape((half, chips, patches, column), LOW),
        shape((half, chips, patches, column), LOW),
        shape((chips, length, width), LOW),
        shape((rows, width), LOW),
        shape((rows, width), LOW),
        shape((rows, width), LOW),
        shape((parts, rows, units), LOW),
        shape((parts, rows, units), LOW),
        shape((parts, rows, 3 * HEAD), LOW),
        shape((parts, rows, HEAD), LOW),
        shape((8, width), F32),
        shape((8, units), F32),
    ]
    out_specs = [
        decoded_spec,
        decoded_spec,
        pl.BlockSpec((1, length, width), lambda i, p: (i, 0, 0)),
        by_rows(width),
        by_rows(width),
        by_rows(width),
        by_part(units),
        by_part(units),
        by_part(3 * HEAD),
        by_part(HEAD),
        pl.BlockSpec((8, width), lambda i, p: (0, 0)),
        pl.BlockSpec((8, units), lambda i, p: (0, 0)),
    ]
    return pl.pallas_call(
        dec_kernel,
        grid_spec=pltpu.PrefetchScalarGridSpec(
            num_scalar_prefetch=1,
            grid=(chips,),
            in_specs=specs,
            out_specs=out_specs,
            scratch_shapes=[
                pltpu.VMEM((parts, patches, units), LOW),
                pltpu.VMEM((parts, patches, patches), F32),
            ],
        ),
        out_shape=out_shape,
        compiler_params=pltpu.CompilerParams(vmem_limit_bytes=VMEM_BYTES),
        cost_estimate=pl.CostEstimate(
            flops=12 * rows * width * units * parts // 2, bytes_accessed=1 << 24, transcendentals=0
        ),
        name="decoder",
    )(place, *args)


def dec_weights_kernel(
    place_ref, n1_ref, n2_ref, gml_ref, cot_ref, act_ref, hid_ref, gqkv_ref, mixed_ref,
    vec_ref, upvec_ref, out_ref, *, first
):
    blocks = out_ref.shape[1]
    bits = blocks.bit_length() - 1
    width = n1_ref.shape[1]
    up = dot(n2_ref[...], hid_ref[0], TN).astype(LOW)
    down = dot(cot_ref[...], act_ref[0], TN).astype(LOW)
    qkv = dot(n1_ref[...], gqkv_ref[0], TN).astype(LOW)
    out = dot(gml_ref[...], mixed_ref[0], TN).astype(LOW)
    which = first + 2 * pl.program_id(0)
    vectors = jnp.concatenate(
        [
            vec_ref[...],
            upvec_ref[pl.ds(which, 1)],
            jnp.zeros((VEC_ROWS - 9, width), F32),
        ],
        0,
    ).astype(LOW)
    piece = width // blocks
    start = out_ref.shape[2] - VEC_ROWS
    for block in range(blocks):
        at = slice(block * piece, (block + 1) * piece)
        place = place_ref[1] ^ bit_reverse(block, bits)
        values = jnp.concatenate([up[at], down[at], qkv[at], out[at]], 1)
        out_ref[0, place, 0:piece] = values
        out_ref[0, place, start : start + VEC_ROWS, 0:piece] = vectors[:, at]


def dec_weights(place, saved, vectors, blocks, first):
    n1, n2, gml, cot, act, hid, gqkv, mixed = saved
    rows, width = n1.shape
    units = act.shape[2]
    piece = width // blocks
    padded = -(-piece // 16) * 16 + VEC_ROWS
    columns = 2 * units + 4 * HEAD

    def whole(array):
        dims = array.ndim
        return pl.BlockSpec(array.shape, lambda g, p: (0,) * dims)

    def by_part(array):
        return pl.BlockSpec((1,) + array.shape[1:], lambda g, p: (first + 2 * g, 0, 0))

    return pl.pallas_call(
        functools.partial(dec_weights_kernel, first=first),
        grid_spec=pltpu.PrefetchScalarGridSpec(
            num_scalar_prefetch=1,
            grid=(2,),
            in_specs=[whole(a) for a in (n1, n2, gml, cot)]
            + [by_part(a) for a in (act, hid, gqkv, mixed)]
            + [whole(a) for a in vectors],
            out_specs=pl.BlockSpec(
                (1, blocks, padded, columns), lambda g, p: (g, 0, 0, 0)
            ),
        ),
        out_shape=jax.ShapeDtypeStruct((2, blocks, padded, columns), LOW),
        compiler_params=pltpu.CompilerParams(vmem_limit_bytes=VMEM_BYTES),
        cost_estimate=pl.CostEstimate(
            flops=4 * rows * width * columns, bytes_accessed=1 << 23, transcendentals=0
        ),
        name="dec_weights_%d" % first,
    )(place, n1, n2, gml, cot, act, hid, gqkv, mixed, *vectors)


def swap(values, axis, apart):
    size = lax.axis_size(axis)
    return lax.ppermute(values, axis, [(i, i ^ apart) for i in range(size)])


def add_low(first, second):
    return (first.astype(F32) + second.astype(F32)).astype(LOW)


def sum_over_tensor(keep, send):
    rows = keep.shape[0]
    own = add_low(keep, swap(send, "tensor", 1))
    other = swap(own, "tensor", 2).reshape(2, rows // 2, -1)
    total = add_low(own.reshape(2, rows // 2, -1), other[::-1]).reshape(keep.shape)
    return total, swap(total, "tensor", 1)


def dp_steps(keep, send, axis="dp"):
    distance = 1
    while True:
        total = keep.astype(F32) + swap(send, axis, distance).astype(F32)
        if total.shape[0] == 1:
            return total[0]
        distance *= 2
        half = total.shape[0] // 2
        keep, send = total[:half], total[half:].astype(LOW)


def gather_low(own):
    first = jnp.concatenate([own, swap(own, "tensor", 2)], 0)
    return first, swap(first, "tensor", 1)


def to_absolute(values, rank):
    values = jnp.where(rank // 2 == 1, values[::-1], values)
    return jnp.where(rank % 2 == 1, values[:, ::-1], values)


def body(
    band_patches,
    band_counts,
    visible_index,
    enc_attn_gain,
    enc_attn_shift,
    enc_qkv_weight,
    enc_out_weight,
    enc_out_bias,
    enc_mlp_gain,
    enc_mlp_shift,
    enc_up_weight,
    enc_up_bias,
    enc_down_weight,
    enc_down_bias,
    proj_weight,
    proj_bias,
    mask_token,
    dec_attn_gain,
    dec_attn_shift,
    dec_qkv_weight,
    dec_out_weight,
    dec_out_bias,
    dec_mlp_gain,
    dec_mlp_shift,
    dec_up_weight,
    dec_up_bias,
    dec_down_weight,
    dec_down_bias,
    cotangent,
):
    parts = lax.axis_size("tensor")
    blocks = lax.axis_size("dp")
    bits = blocks.bit_length() - 1
    rank = lax.axis_index("tensor")
    place = jnp.stack([rank, bit_reverse(lax.axis_index("dp"), bits)]).astype(jnp.int32)
    chips, length = visible_index.shape
    own_chips = chips // parts
    enc_width = band_patches.shape[3]
    patches, dec_width = cotangent.shape[1:]
    enc_inner = enc_out_weight.shape[0]
    enc_units = enc_up_weight.shape[1]
    dec_units = dec_up_weight.shape[1]
    dec_kinds = 3 * dec_out_weight.shape[0]
    rows = chips * length
    shape = jax.ShapeDtypeStruct

    def row(vector):
        return vector.reshape(1, -1)

    w_own = jnp.concatenate(
        [
            dec_qkv_weight.reshape(dec_kinds, dec_width),
            dec_out_weight,
            dec_up_weight,
            dec_down_weight,
        ],
        0,
    )
    w_core = swap(w_own, "tensor", 1)
    w_x = swap(w_own, "tensor", 2)
    w_diag = swap(w_x, "tensor", 1)
    weights = (w_own, w_core, w_x, w_diag)
    up_bias_parts = to_absolute(dec_up_bias.reshape(2, 2, 1, dec_units), rank)
    up_bias_parts = up_bias_parts.reshape(parts, 1, dec_units)

    tokens_part = band_mean(place, band_counts, band_patches, visible_index, own_chips)
    tokens_part = tokens_part.reshape(2, rows // 2, enc_width)
    tok_a, tok_b = sum_over_tensor(tokens_part[0], tokens_part[1])

    half_rows = shape((rows // 2, enc_width), LOW)
    all_rows = shape((rows, enc_width), LOW)
    qkv_w = enc_qkv_weight.reshape(3 * enc_inner, enc_width)
    flops_attn = 2 * rows * enc_width * 4 * enc_inner
    flops_mlp = 4 * rows * enc_width * enc_units
    part_a, part_b, enc_n1, enc_qkv, enc_mixed = call(
        functools.partial(enc_attn_kernel, length=length),
        [half_rows, half_rows, all_rows, shape((rows, 3 * enc_inner), LOW), shape((rows, enc_inner), LOW)],
        [tok_a, tok_b, row(enc_attn_gain), row(enc_attn_shift), qkv_w, enc_out_weight],
        flops=flops_attn,
        name="enc_attn",
    )
    sum_a, sum_b = sum_over_tensor(part_a, part_b)
    hidden_shape = shape((rows, enc_units), LOW)
    part_a, part_b, enc_n2, enc_act, enc_slope = call(
        enc_mlp_kernel,
        [half_rows, half_rows, all_rows, hidden_shape, hidden_shape],
        [
            tok_a, tok_b, sum_a, sum_b, row(enc_out_bias), row(enc_mlp_gain), row(enc_mlp_shift),
            enc_up_weight, row(enc_up_bias), enc_down_weight,
        ],
        flops=flops_mlp,
        name="enc_mlp",
    )
    quarter = rows // 4
    down = add_low(part_a, swap(part_b, "tensor", 1))
    down_x = swap(down[quarter:], "tensor", 2)
    enc_out = (
        tok_a[:quarter].astype(F32)
        + sum_a[:quarter].astype(F32)
        + enc_out_bias
        + down[:quarter].astype(F32)
        + down_x.astype(F32)
        + enc_down_bias
    )
    enc_low = enc_out.astype(LOW)
    enc_low_a, enc_low_b = gather_low(enc_low)

    angles = lax.broadcasted_iota(F32, (patches, dec_width // 2), 0) * jnp.exp(
        lax.broadcasted_iota(F32, (patches, dec_width // 2), 1)
        * (-math.log(10000.0) / (dec_width // 2))
    )
    position = jnp.concatenate([jnp.sin(angles), jnp.cos(angles)], 1)
    own_visible = lax.dynamic_slice_in_dim(visible_index, rank * own_chips, own_chips, 0)
    own_cotangent = lax.dynamic_slice_in_dim(cotangent, rank * own_chips, own_chips, 0)
    small = (
        proj_weight,
        row(proj_bias),
        row(mask_token),
        [
            row(v)
            for v in (
                dec_attn_gain, dec_attn_shift, dec_out_bias, dec_mlp_gain, dec_mlp_shift,
                dec_down_bias,
            )
        ],
    )
    (
        decoded_keep, decoded_send, grad_latent, dec_n1, dec_n2, dec_gml, dec_act, dec_hid,
        dec_gqkv, dec_mixed, dec_vec, dec_upvec,
    ) = dec_call(
        place, enc_low.reshape(own_chips, length, enc_width), small, position, own_visible,
        up_bias_parts, weights, own_cotangent,
    )
    lat_a, lat_b = gather_low(grad_latent.reshape(own_chips * length, dec_width))

    wide_rows = shape((rows // 2, enc_width), F32)
    vec_shape = shape((8, enc_width), F32)
    part_a, part_b, out_a, out_b, enc_gol, enc_hid, vec_mlp = call(
        enc_mlp_back_kernel,
        [half_rows, half_rows, wide_rows, wide_rows, all_rows, hidden_shape, vec_shape],
        [lat_a, lat_b, proj_weight, enc_slope, enc_up_weight, enc_down_weight],
        flops=flops_mlp,
        name="enc_mlp_back",
    )
    back_a, back_b = sum_over_tensor(part_a, part_b)

    saved = (
        dec_n1, dec_n2, dec_gml, own_cotangent.reshape(-1, dec_width), dec_act, dec_hid, dec_gqkv,
        dec_mixed,
    )
    dec_send = dec_weights(place, saved, (dec_vec, dec_upvec), blocks, 1)
    dec_keep = dec_weights(place, saved, (dec_vec, dec_upvec), blocks, 0)
    dec_sum = add_low(dec_keep, swap(dec_send, "tensor", 1))
    dec_sum = add_low(dec_sum[0], swap(dec_sum[1], "tensor", 2))
    dec_share = dp_steps(dec_sum[: blocks // 2], dec_sum[blocks // 2 :])

    enc_piece = enc_width // blocks
    enc_rows = -(-enc_piece // 16) * 16
    proj_own = dec_width // parts
    bundle = shape((blocks // 2, enc_rows, 2 * enc_units + proj_own), LOW)
    mlp_keep, mlp_send = call(
        enc_mlp_weights_kernel,
        [bundle, bundle],
        [enc_n2, enc_hid, enc_gol, enc_act, lat_a, lat_b, enc_low_a, enc_low_b],
        scalars=[place],
        flops=flops_mlp,
        name="enc_mlp_weights",
    )
    mlp_share = dp_steps(mlp_keep, mlp_send)

    part_a, part_b, mid_a, mid_b, enc_gml, enc_gqkv, vec_attn = call(
        functools.partial(enc_attn_back_kernel, length=length),
        [
            half_rows, half_rows, wide_rows, wide_rows, all_rows,
            shape((rows, 3 * enc_inner), LOW), vec_shape,
        ],
        [
            tok_a, tok_b, sum_a, sum_b, row(enc_out_bias), row(enc_mlp_gain), out_a, out_b,
            back_a, back_b, enc_qkv, qkv_w, enc_out_weight,
        ],
        flops=2 * flops_attn,
        name="enc_attn_back",
    )
    grad_a, grad_b = sum_over_tensor(part_a, part_b)
    bundle = shape((blocks // 2, enc_rows + VEC_ROWS, 4 * enc_inner), LOW)
    attn_keep, attn_send = call(
        enc_attn_weights_kernel,
        [bundle, bundle],
        [enc_n1, enc_gqkv, enc_gml, enc_mixed, vec_mlp, vec_attn],
        scalars=[place],
        flops=flops_attn,
        name="enc_attn_weights",
    )
    attn_share = dp_steps(attn_keep, attn_send)

    def in_steps(first, second):
        return jnp.concatenate([first, second], 0).reshape(chips, length, enc_width)

    band_grad = band_grad_call(
        place, band_counts, in_steps(tok_a, tok_b), in_steps(grad_a, grad_b),
        in_steps(mid_a, mid_b), row(enc_attn_gain), visible_index, band_patches.shape, own_chips,
    )

    got = swap(decoded_send, "tensor", 1)
    got_x = swap(jnp.stack([decoded_keep[1], got[1]]), "tensor", 2)
    decoded = to_absolute(jnp.stack([jnp.stack([decoded_keep[0], got[0]]), got_x]), rank)
    decoded = decoded.astype(F32).reshape(chips, patches, -1)

    proj_low = mlp_share[:enc_piece, 2 * enc_units :].astype(LOW)
    proj_core = jnp.stack([proj_low, swap(proj_low, "tensor", 1)])
    proj_all = to_absolute(jnp.stack([proj_core, swap(proj_core, "tensor", 2)]), rank)
    proj_all = proj_all.reshape(parts, enc_piece, proj_own).transpose(1, 0, 2)
    enc_vec = attn_share[enc_rows:, :enc_piece]
    norm_vec = enc_vec[11:13]
    norm_vec = norm_vec + swap(norm_vec, "tensor", 1)
    norm_vec = norm_vec + swap(norm_vec, "tensor", 2)
    enc_qkv_grad = attn_share[:enc_piece, : 3 * enc_inner].T.reshape(3, enc_inner, enc_piece)
    dec_piece = dec_width // blocks
    dec_qkv_grad = dec_share[:dec_piece, 2 * dec_units : 2 * dec_units + dec_kinds].T
    dec_vecs = dec_share[-VEC_ROWS:, :dec_piece]
    return (
        decoded,
        band_grad,
        norm_vec[0],
        norm_vec[1],
        enc_qkv_grad,
        attn_share[:enc_piece, 3 * enc_inner :].T,
        enc_vec[10],
        enc_vec[8],
        enc_vec[9],
        mlp_share[:enc_piece, :enc_units],
        enc_vec[1],
        mlp_share[:enc_piece, enc_units : 2 * enc_units].T,
        enc_vec[0],
        proj_all.reshape(enc_piece, dec_width).astype(F32),
        dec_vecs[6],
        dec_vecs[7],
        dec_vecs[0],
        dec_vecs[1],
        dec_qkv_grad.reshape(3, dec_kinds // 3, dec_piece),
        dec_share[:dec_piece, 2 * dec_units + dec_kinds :].T,
        dec_vecs[2],
        dec_vecs[3],
        dec_vecs[4],
        dec_share[:dec_piece, :dec_units],
        dec_vecs[8],
        dec_share[:dec_piece, dec_units : 2 * dec_units].T,
        dec_vecs[5],
    )


def solution(mesh):
    in_specs = (
        P("dp", None, "tensor", None),
        P("dp"),
        P("dp", None),
        P(),
        P(),
        P(None, "tensor", None),
        P("tensor", None),
        P(),
        P(),
        P(),
        P(None, "tensor"),
        P("tensor"),
        P("tensor", None),
        P(),
        P(),
        P(),
        P(),
        P(),
        P(),
        P(None, "tensor", None),
        P("tensor", None),
        P(),
        P(),
        P(),
        P(None, "tensor"),
        P(),
        P("tensor", None),
        P(),
        P("dp", None, None),
    )
    out_specs = (
        P("dp", None, "tensor"),
        P("dp", None, "tensor", None),
        P("dp"),
        P("dp"),
        P(None, "tensor", "dp"),
        P("tensor", "dp"),
        P("dp"),
        P("dp"),
        P("dp"),
        P("dp", "tensor"),
        P(("tensor", "dp")),
        P("tensor", "dp"),
        P("dp"),
        P("dp", None),
        P("dp"),
        P("dp"),
        P("dp"),
        P("dp"),
        P(None, "tensor", "dp"),
        P("tensor", "dp"),
        P("dp"),
        P("dp"),
        P("dp"),
        P("dp", "tensor"),
        P(("tensor", "dp")),
        P("tensor", "dp"),
        P("dp"),
    )
    return jax.shard_map(body, mesh=mesh, in_specs=in_specs, out_specs=out_specs, check_vma=False)
```

```python
import functools
import math

import jax
import jax.numpy as jnp
from jax import lax
from jax.experimental import pallas as pl
from jax.experimental.pallas import tpu as pltpu
from jax.sharding import PartitionSpec as P

HEAD = 64
EPSILON = 1e-05
SCALE = HEAD ** (-0.5)
VMEM_BYTES = 24 * 1024 * 1024
DEC_VMEM_BYTES = 30 * 1024 * 1024
F32 = jnp.float32
LOW = jnp.bfloat16
NN = (((1,), (0,)), ((), ()))
NT = (((1,), (1,)), ((), ()))
TN = (((0,), (0,)), ((), ()))
VEC_ROWS = 16


def dot(left, right, dims=NN):
    return lax.dot_general(left, right, dims, preferred_element_type=F32)


def col_sum(values):
    return jnp.sum(values, 0, keepdims=True)


def vec(ref):
    return ref[...][None, :]


def norm_parts(stream):
    center = stream - jnp.mean(stream, -1, keepdims=True)
    inverse = lax.rsqrt(jnp.mean(center * center, -1, keepdims=True) + EPSILON)
    return center * inverse, inverse


def norm_back(grad, xhat, inverse, gain):
    scaled = grad * gain
    mean_q = jnp.mean(scaled, -1, keepdims=True)
    mean_qx = jnp.mean(scaled * xhat, -1, keepdims=True)
    return inverse * (scaled - mean_q - xhat * mean_qx)


def gelu_parts(hidden):
    phi = 0.5 + 0.5 * lax.erf(hidden * (0.5**0.5))
    density = jnp.exp(hidden * hidden * -0.5) * (1.0 / math.sqrt(2.0 * math.pi))
    return hidden * phi, phi + hidden * density


def softmax_rows(scores):
    weights = jnp.exp(scores - jnp.max(scores, -1, keepdims=True))
    return weights * (1.0 / jnp.sum(weights, -1, keepdims=True))


def same_chip(rows, length):
    first = lax.broadcasted_iota(jnp.int32, (rows, rows), 0) // length
    second = lax.broadcasted_iota(jnp.int32, (rows, rows), 1) // length
    return first == second


def attend(queries, keyset, mask):
    scores = dot(queries, keyset, NT) * SCALE
    if mask is not None:
        scores = jnp.where(mask, scores, -1e30)
    return softmax_rows(scores)


def attend_back(probs, queries, keyset, valset, grad_mixed):
    grad_probs = dot(grad_mixed, valset, NT)
    grad_values = dot(probs.astype(LOW), grad_mixed, TN)
    grad_scores = probs * (grad_probs - jnp.sum(grad_probs * probs, -1, keepdims=True))
    score_low = grad_scores.astype(LOW)
    grad_queries = dot(score_low, keyset) * SCALE
    grad_keys = dot(score_low, queries, TN) * SCALE
    return grad_queries.astype(LOW), grad_keys.astype(LOW), grad_values.astype(LOW)


class Line:
    def __init__(self):
        self.token = None

    def call(self, body, out_shape, args, scalars=(), after=(), name=None, scratch=(), vmem=VMEM_BYTES):
        after = list(after) + ([] if self.token is None else [self.token])
        specs = [pl.BlockSpec(memory_space=pltpu.SMEM) for _ in scalars]
        specs += [pl.BlockSpec(memory_space=pltpu.VMEM) for _ in args]
        specs += [pl.BlockSpec(memory_space=pl.ANY) for _ in after]
        inputs = len(scalars) + len(args)
        outputs = len(out_shape)
        out_specs = []
        for out in out_shape:
            in_hbm = isinstance(out, InHbm)
            out_specs.append(pl.BlockSpec(memory_space=pltpu.HBM if in_hbm else pltpu.VMEM))
        out_shape = [out.array if isinstance(out, InHbm) else out for out in out_shape]

        def wrapped(*refs):
            outs = refs[inputs + len(after) :]
            outs[outputs][...] = jnp.zeros_like(outs[outputs])
            body(*refs[:inputs], *outs[:outputs], *outs[outputs + 1 :])

        *found, self.token = pl.pallas_call(
            wrapped,
            out_shape=out_shape + [jax.ShapeDtypeStruct((8, 128), F32)],
            in_specs=specs,
            out_specs=out_specs + [pl.BlockSpec(memory_space=pltpu.VMEM)],
            scratch_shapes=list(scratch),
            compiler_params=pltpu.CompilerParams(vmem_limit_bytes=vmem),
            cost_estimate=pl.CostEstimate(flops=1, bytes_accessed=1, transcendentals=0),
            name=name,
        )(*scalars, *args, *after)
        return found


class InHbm:
    def __init__(self, array):
        self.array = array


def bit_reverse(value, bits):
    result = 0
    for place in range(bits):
        result = result | (((value >> place) & 1) << (bits - 1 - place))
    return result


def put_block(keep, send, lead, place, half, rows, columns, values):
    @pl.when(place < half)
    def _():
        keep[lead + (place, rows, columns)] = values

    @pl.when(place >= half)
    def _():
        send[lead + (place - half, rows, columns)] = values


def chip_of(step, rank, own_chips):
    part, index = step // own_chips, step % own_chips
    apart = 2 * (part % 2) + part // 2
    return (rank ^ apart) * own_chips + index


def put_rows(parts, first, values):
    for part in parts:
        if first < part.shape[0]:
            part[first : first + values.shape[0]] = values
            return
        first -= part.shape[0]


def get_rows(parts, first, count):
    found = []
    for part in parts:
        size = part.shape[0]
        if first < size and count > 0:
            taken = min(count, size - first)
            found.append(part[first : first + taken])
            count -= taken
            first = size
        first -= size
    return found[0] if len(found) == 1 else jnp.concatenate(found, 0)


def band_mean_kernel(place_ref, count_ref, bands_ref, visible_ref, *parts, own_chips):
    rank = place_ref[0]
    chips, bands, own, width = bands_ref.shape
    length = visible_ref.shape[1]
    patch = lax.broadcasted_iota(jnp.int32, (own, length), 0) + rank * own
    for step in range(chips):
        spot = chip_of(step, rank, own_chips)
        count = count_ref[spot]
        means = []
        for first in range(0, own, 16):
            span = slice(first, first + 16)
            total = bands_ref[spot, 0, span].astype(F32)
            for band in range(1, bands):
                used = jnp.where(band < count, 1.0, 0.0).astype(F32)
                total = total + bands_ref[spot, band, span].astype(F32) * used
            means.append((total / count.astype(F32)).astype(LOW))
        chosen = visible_ref[pl.ds(spot, 1)] == patch
        chosen = jnp.where(chosen, 1.0, 0.0).astype(LOW)
        values = dot(chosen, jnp.concatenate(means, 0), TN).astype(LOW)
        put_rows(parts, step * length, values)


def enc_attn_kernel(*refs, length):
    tok, (gain, shift, qkv_w, out_w) = refs[:4], refs[4:8]
    parts, (normed_ref, qkv_ref, mixed_ref) = refs[8:11], refs[11:]
    rows = normed_ref.shape[0] // 2
    inner = out_w.shape[0]
    block = 2 * length
    mask = same_chip(block, length)
    for group in range(2):
        span = slice(group * rows, (group + 1) * rows)
        xhat, _ = norm_parts(get_rows(tok, group * rows, rows).astype(F32))
        normed = (xhat * vec(gain) + vec(shift)).astype(LOW)
        normed_ref[span] = normed
        qkv = dot(normed, qkv_w[...], NT).astype(LOW)
        qkv_ref[span] = qkv
        blocks = []
        for first in range(0, rows, block):
            heads = []
            for head in range(inner // HEAD):
                at = [
                    qkv[first : first + block, k * inner + head * HEAD : k * inner + (head + 1) * HEAD]
                    for k in range(3)
                ]
                probs = attend(at[0], at[1], mask)
                heads.append(dot(probs.astype(LOW), at[2]).astype(LOW))
            blocks.append(jnp.concatenate(heads, 1))
        mixed = jnp.concatenate(blocks, 0)
        mixed_ref[span] = mixed
        part = dot(mixed, out_w[...]).astype(LOW)
        for first in range(0, rows, block):
            put_rows(parts, group * rows + first, part[first : first + block])


def enc_mlp_kernel(*refs):
    tok, sums = refs[:4], refs[4:8]
    out_bias, gain, shift, up_w, up_bias, down_w = refs[8:14]
    parts, (normed_ref, act_ref, slope_ref) = refs[14:18], refs[18:]
    rows = normed_ref.shape[0] // 2
    block = rows // 2
    for group in range(2):
        span = slice(group * rows, (group + 1) * rows)
        middle = get_rows(tok, group * rows, rows).astype(F32) + vec(out_bias)
        middle = middle + get_rows(sums, group * rows, rows).astype(F32)
        xhat, _ = norm_parts(middle)
        normed = (xhat * vec(gain) + vec(shift)).astype(LOW)
        normed_ref[span] = normed
        activation, slope = gelu_parts(dot(normed, up_w[...]) + vec(up_bias))
        act_low = activation.astype(LOW)
        act_ref[span] = act_low
        slope_ref[span] = slope.astype(LOW)
        part = dot(act_low, down_w[...]).astype(LOW)
        for first in range(0, rows, block):
            put_rows(parts, group * rows + first, part[first : first + block])


def enc_out_kernel(tok, total, out_bias, own, other, down_bias, low_ref):
    low_ref[...] = (
        tok[...].astype(F32)
        + total[...].astype(F32)
        + vec(out_bias)
        + own[...].astype(F32)
        + other[...].astype(F32)
        + vec(down_bias)
    ).astype(LOW)


def enc_mlp_back_kernel(*refs):
    lat, (proj_w, slope_ref, up_w, down_w) = refs[:4], refs[4:8]
    parts, (out_ref, low_ref, hidden_ref, vec_ref) = refs[8:11], refs[11:]
    rows = out_ref.shape[0] // 2
    block = rows // 2
    down_sum, up_sum = 0.0, 0.0
    for group in range(2):
        span = slice(group * rows, (group + 1) * rows)
        grad_out = dot(get_rows(lat, group * rows, rows), proj_w[...], NT)
        out_ref[span] = grad_out
        grad_low = grad_out.astype(LOW)
        low_ref[span] = grad_low
        grad_hidden = dot(grad_low, down_w[...], NT) * slope_ref[span].astype(F32)
        hidden_low = grad_hidden.astype(LOW)
        hidden_ref[span] = hidden_low
        down_sum = down_sum + col_sum(grad_out)
        up_sum = up_sum + col_sum(grad_hidden)
        part = dot(hidden_low, up_w[...], NT).astype(LOW)
        for first in range(0, rows, block):
            put_rows(parts, group * rows + first, part[first : first + block])
    vec_ref[...] = jnp.concatenate(
        [down_sum, up_sum, jnp.zeros((vec_ref.shape[0] - 2, down_sum.shape[1]), F32)], 0
    )


def enc_mlp_weights_kernel(place_ref, normed_ref, hidden_ref, low_ref, act_ref, keep, send):
    half = keep.shape[0]
    blocks, bits = 2 * half, (2 * half).bit_length() - 1
    width, hidden = normed_ref.shape[1], hidden_ref.shape[1]
    piece = width // blocks
    for kind, (left, right) in enumerate(((normed_ref, hidden_ref), (low_ref, act_ref))):
        found = dot(left[...], right[...], TN)
        columns = slice(kind * hidden, (kind + 1) * hidden)
        for block in range(blocks):
            values = found[block * piece : (block + 1) * piece].astype(LOW)
            place = place_ref[1] ^ bit_reverse(block, bits)
            put_block(keep, send, (), place, half, slice(0, piece), columns, values)


def enc_attn_back_kernel(*refs, length):
    tok, sums, backs = refs[:4], refs[4:8], refs[8:12]
    out_bias, mlp_gain, out_ref, qkv_ref, qkv_w, out_w = refs[12:18]
    parts, (mid_ref, low_ref, grad_qkv_ref, vec_ref) = refs[18:21], refs[21:]
    rows = out_ref.shape[0] // 2
    inner = out_w.shape[0]
    block = 2 * length
    mask = same_chip(block, length)
    found = [0.0] * 5
    for group in range(2):
        span = slice(group * rows, (group + 1) * rows)
        stream = get_rows(tok, group * rows, rows).astype(F32)
        total = get_rows(sums, group * rows, rows).astype(F32)
        xhat, inverse = norm_parts(stream + total + vec(out_bias))
        grad = get_rows(backs, group * rows, rows).astype(F32)
        found[0] = found[0] + col_sum(grad * xhat)
        found[1] = found[1] + col_sum(grad)
        grad_middle = out_ref[span] + norm_back(grad, xhat, inverse, vec(mlp_gain))
        mid_ref[span] = grad_middle
        found[2] = found[2] + col_sum(grad_middle)
        middle_low = grad_middle.astype(LOW)
        low_ref[span] = middle_low
        grad_mixed = dot(middle_low, out_w[...], NT).astype(LOW)
        blocks = []
        for first in range(0, rows, block):
            near = slice(group * rows + first, group * rows + first + block)
            grads = ([], [], [])
            for head in range(inner // HEAD):
                at = [
                    qkv_ref[near, k * inner + head * HEAD : k * inner + (head + 1) * HEAD]
                    for k in range(3)
                ]
                probs = attend(at[0], at[1], mask)
                own = grad_mixed[first : first + block, head * HEAD : (head + 1) * HEAD]
                for kind, values in enumerate(attend_back(probs, *at, own)):
                    grads[kind].append(values)
            blocks.append(jnp.concatenate(grads[0] + grads[1] + grads[2], 1))
        grad_qkv = jnp.concatenate(blocks, 0)
        grad_qkv_ref[span] = grad_qkv
        partial = dot(grad_qkv, qkv_w[...])
        part = partial.astype(LOW)
        for first in range(0, rows, block):
            put_rows(parts, group * rows + first, part[first : first + block])
        xhat, _ = norm_parts(stream)
        found[3] = found[3] + col_sum(partial * xhat)
        found[4] = found[4] + col_sum(partial)
    vec_ref[...] = jnp.concatenate(
        found + [jnp.zeros((vec_ref.shape[0] - 5, found[0].shape[1]), F32)], 0
    )


def enc_attn_weights_kernel(
    place_ref, normed_ref, grad_qkv_ref, low_ref, mixed_ref, vec_mlp, vec_attn, keep, send
):
    half = keep.shape[0]
    blocks, bits = 2 * half, (2 * half).bit_length() - 1
    width = normed_ref.shape[1]
    qkv = dot(normed_ref[...], grad_qkv_ref[...], TN)
    out = dot(low_ref[...], mixed_ref[...], TN)
    vectors = jnp.concatenate([vec_mlp[...], vec_attn[...]], 0)
    piece = width // blocks
    first = keep.shape[1] - VEC_ROWS
    for block in range(blocks):
        at = slice(block * piece, (block + 1) * piece)
        place = place_ref[1] ^ bit_reverse(block, bits)
        values = jnp.concatenate([qkv[at], out[at]], 1).astype(LOW)
        put_block(keep, send, (), place, half, slice(0, piece), slice(None), values)
        put_block(
            keep, send, (), place, half, slice(first, first + VEC_ROWS), slice(0, piece),
            vectors[:, at].astype(LOW),
        )


def band_grad_kernel(place_ref, count_ref, *refs, own_chips):
    tok, backs, (mid_ref, gain, visible_ref) = refs[:4], refs[4:8], refs[8:11]
    out_ref, stage, left = refs[11:]
    rank = place_ref[0]
    chips, bands, own, width = out_ref.shape
    length = visible_ref.shape[1]
    spots = [chip_of(step, rank, own_chips) for step in range(chips)]
    counts = [count_ref[spot] for spot in spots]

    def copy_of(source, step, band):
        return pltpu.make_async_copy(
            stage.at[source], out_ref.at[spots[step], band], left.at[step, band]
        )

    stage[chips] = jnp.zeros((own, width), F32)
    for step in range(chips):

        def blank(band, carry, step=step):
            copy_of(chips, step, band).start()
            return carry

        lax.fori_loop(counts[step], bands, blank, 0)
    patch = lax.broadcasted_iota(jnp.int32, (own, length), 0) + rank * own
    for step in range(chips):
        first = step * length
        xhat, inverse = norm_parts(get_rows(tok, first, length).astype(F32))
        back = get_rows(backs, first, length).astype(F32)
        grad = mid_ref[first : first + length] + norm_back(back, xhat, inverse, vec(gain))
        grad = grad / counts[step].astype(F32)
        chosen = visible_ref[pl.ds(spots[step], 1)] == patch
        chosen = jnp.where(chosen, 1.0, 0.0).astype(LOW)
        high = grad.astype(LOW)
        rest = (grad - high.astype(F32)).astype(LOW)
        stage[step] = dot(chosen, high) + dot(chosen, rest)

        def fill(band, carry, step=step):
            copy_of(step, step, band).start()
            return carry

        lax.fori_loop(0, counts[step], fill, 0)
    for step in range(chips):

        def finish(band, carry, step=step):
            copy_of(step, step, band).wait()
            return carry

        lax.fori_loop(0, bands, finish, 0)


def dec_kernel(
    place_ref, enc_low, proj_w, proj_bias, mask_token, position, visible_ref,
    attn_gain, attn_shift, out_bias, mlp_gain, mlp_shift, down_bias, up_bias,
    w0, w1, w2, w3, cotangent,
    decoded_keep, decoded_send, grad_latent_ref, n1_ref, n2_ref, gml_ref, act_ref, hid_ref,
    gqkv_ref, mixed_ref, vec_ref, upvec_ref,
    slope_scr, prob_scr, qkv_scr,
):
    weights = (w0, w1, w2, w3)
    parts = len(weights)
    chips, length = visible_ref.shape
    patches, width = position.shape
    kinds = 3 * HEAD
    inner = kinds + HEAD
    units = up_bias.shape[0] // parts
    up_at, down_at = slice(inner, inner + width), slice(inner + width, inner + width + units)
    spans = [slice(chip * patches, (chip + 1) * patches) for chip in range(chips)]
    latent = dot(enc_low[...], proj_w[...]) + vec(proj_bias)
    high = latent.astype(LOW)
    rest = (latent - high.astype(F32)).astype(LOW)
    streams, chosen, seen = [], [], []
    for chip in range(chips):
        near = slice(chip * length, (chip + 1) * length)
        hit = lax.broadcasted_iota(jnp.int32, (patches, length), 0) == visible_ref[chip : chip + 1]
        hit = jnp.where(hit, 1.0, 0.0)
        is_visible = jnp.sum(hit, 1, keepdims=True)
        hit = hit.astype(LOW)
        filled = dot(hit, high[near]) + dot(hit, rest[near])
        streams.append(filled + (1.0 - is_visible) * vec(mask_token) + position[...])
        chosen.append(hit)
        seen.append(is_visible)
    stream = jnp.concatenate(streams, 0)
    xhat1, inverse1 = norm_parts(stream)
    n1 = (xhat1 * vec(attn_gain) + vec(attn_shift)).astype(LOW)
    n1_ref[...] = n1
    for part, weight in enumerate(weights):
        qkv_scr[part] = dot(n1, weight[0:kinds], NT).astype(LOW)

    def qkv_of(part, span):
        return [qkv_scr[part, span, k * HEAD : (k + 1) * HEAD] for k in range(3)]

    for part in range(parts):
        for span in spans:
            queries, keyset, valset = qkv_of(part, span)
            probs = attend(queries, keyset, None)
            prob_scr[part, span] = probs
            mixed_ref[part, span] = dot(probs.astype(LOW), valset).astype(LOW)
    out_all = jnp.concatenate([weight[kinds:inner] for weight in weights], 0)
    mixed = jnp.concatenate([mixed_ref[part] for part in range(parts)], 1)
    middle = stream + dot(mixed, out_all) + vec(out_bias)
    xhat2, inverse2 = norm_parts(middle)
    n2 = (xhat2 * vec(mlp_gain) + vec(mlp_shift)).astype(LOW)
    n2_ref[...] = n2
    total = middle + vec(down_bias)
    for part, weight in enumerate(weights):
        spot = pl.multiple_of((place_ref[0] ^ part) * units, units)
        bias = up_bias[pl.ds(spot, units)][None, :]
        activation, slope = gelu_parts(dot(n2, weight[up_at]) + bias)
        act_low = activation.astype(LOW)
        act_ref[part] = act_low
        slope_scr[part] = slope.astype(LOW)
        total = total + dot(act_low, weight[down_at])
    column = width // parts
    half = parts // 2
    for part in range(parts):
        apart = place_ref[0] ^ part
        for chip, span in enumerate(spans):
            values = total[span, part * column : (part + 1) * column].astype(LOW)

            @pl.when(apart % 2 == 0)
            def _(values=values, apart=apart, chip=chip):
                decoded_keep[apart // 2, chip] = values

            @pl.when(apart % 2 == 1)
            def _(values=values, apart=apart, chip=chip):
                decoded_send[apart // 2, chip] = values

    grad_low = cotangent[...]
    grad_out = grad_low.astype(F32)
    grad_n2 = 0.0
    up_sums = []
    for part, weight in enumerate(weights):
        grad_hidden = dot(grad_low, weight[down_at], NT) * slope_scr[part].astype(F32)
        hidden_low = grad_hidden.astype(LOW)
        hid_ref[part] = hidden_low
        up_sums.append(col_sum(grad_hidden))
        grad_n2 = grad_n2 + dot(hidden_low, weight[up_at], NT)
    grad_middle = grad_out + norm_back(grad_n2, xhat2, inverse2, vec(mlp_gain))
    mlp_gain_sum, mlp_shift_sum = col_sum(grad_n2 * xhat2), col_sum(grad_n2)
    middle_low = grad_middle.astype(LOW)
    gml_ref[...] = middle_low
    grad_mixed = dot(middle_low, out_all, NT).astype(LOW)
    grad_n1 = 0.0
    for part, weight in enumerate(weights):
        for span in spans:
            own = grad_mixed[span, part * HEAD : (part + 1) * HEAD]
            found = attend_back(prob_scr[part, span], *qkv_of(part, span), own)
            gqkv_ref[part, span] = jnp.concatenate(found, 1)
        grad_n1 = grad_n1 + dot(gqkv_ref[part], weight[0:kinds])
    grad_stream = grad_middle + norm_back(grad_n1, xhat1, inverse1, vec(attn_gain))
    stream_low = grad_stream.astype(LOW)
    for chip, span in enumerate(spans):
        near = slice(chip * length, (chip + 1) * length)
        grad_latent_ref[near] = dot(chosen[chip], stream_low[span], TN).astype(LOW)
    seen_sum = col_sum(grad_stream * jnp.concatenate(seen, 0))
    vec_ref[...] = jnp.concatenate(
        [
            col_sum(grad_n1 * xhat1),
            col_sum(grad_n1),
            col_sum(grad_middle),
            mlp_gain_sum,
            mlp_shift_sum,
            col_sum(grad_out),
            seen_sum,
            col_sum(grad_stream) - seen_sum,
        ],
        0,
    )
    upvec_ref[...] = jnp.concatenate(up_sums + [jnp.zeros((8 - parts, units), F32)], 0)


def put_quarter(keep, sends, part, place, values):
    if part % 2 == 0:
        keep[part // 2, place] = values
        return
    half = sends[0].shape[0]
    put_block(sends[part - 1], sends[part], (), place, half, slice(None), slice(None), values)


def dec_up_kernel(place_ref, n2_ref, hid_ref, enc_low, latent, keep, *sends):
    parts, _, units = hid_ref.shape
    blocks = keep.shape[1]
    bits = blocks.bit_length() - 1
    width, enc_width = n2_ref.shape[1], enc_low.shape[1]
    piece, enc_piece = width // blocks, enc_width // blocks
    column = latent.shape[1] // parts
    left = n2_ref[...].T
    left_proj = enc_low[...].T
    for part in (1, 3, 0, 2):
        up = dot(left, hid_ref[part])
        spot = pl.multiple_of((place_ref[0] ^ part) * column, column)
        proj = dot(left_proj, latent[:, pl.ds(spot, column)])
        for block in range(blocks):
            first = block * enc_piece
            rest = proj[first + piece : first + enc_piece]
            rest = jnp.concatenate([rest[:, : column // 2], rest[:, column // 2 :]], 0)
            values = jnp.concatenate(
                [
                    up[block * piece : (block + 1) * piece],
                    proj[first : first + piece],
                    rest,
                    jnp.zeros_like(rest),
                ],
                1,
            )
            place = place_ref[1] ^ bit_reverse(block, bits)
            put_quarter(keep, sends, part, place, values.astype(LOW))


def dec_down_kernel(
    place_ref, cot_ref, act_ref, n1_ref, gqkv_ref, gml_ref, mixed_ref, vec_ref, upvec_ref, keep, *sends
):
    parts, _, units = act_ref.shape
    blocks = keep.shape[1]
    bits = blocks.bit_length() - 1
    width = n1_ref.shape[1]
    piece = width // blocks
    left_down, left_qkv, left_out = cot_ref[...].T, n1_ref[...].T, gml_ref[...].T
    blank = jnp.zeros((128 - 9, width), F32)
    for part in (1, 3, 0, 2):
        vectors = jnp.concatenate([vec_ref[...], upvec_ref[part : part + 1], blank], 0).T
        values = jnp.concatenate(
            [
                dot(left_down, act_ref[part]),
                dot(left_qkv, gqkv_ref[part]),
                dot(left_out, mixed_ref[part]),
                vectors,
            ],
            1,
        ).astype(LOW)
        for block in range(blocks):
            place = place_ref[1] ^ bit_reverse(block, bits)
            put_quarter(keep, sends, part, place, values[block * piece : (block + 1) * piece])


def add_kernel(keep, got_0, got_1, out):
    half = got_0.shape[0]
    out[0:half] = (keep[0:half].astype(F32) + got_0[...].astype(F32)).astype(LOW)
    out[half:] = (keep[half:].astype(F32) + got_1[...].astype(F32)).astype(LOW)


def add_two_kernel(far_keep, far_got, near_keep, near_got, far, near):
    far[...] = (far_keep[...].astype(F32) + far_got[...].astype(F32)).astype(LOW)
    near[...] = (near_keep[...].astype(F32) + near_got[...].astype(F32)).astype(LOW)


def add_crossed_kernel(own, other, first, second):
    half = first.shape[0]
    first[...] = (own[0:half].astype(F32) + other[half:].astype(F32)).astype(LOW)
    second[...] = (own[half:].astype(F32) + other[0:half].astype(F32)).astype(LOW)


def assemble_kernel(place_ref, *refs):
    for sources, target in ((refs[0:4], refs[8]), (refs[4:8], refs[9])):
        for apart, source in enumerate(sources):
            rows = source.shape[0]
            spot = pl.multiple_of((place_ref[2] ^ apart) * rows, rows)
            target[pl.ds(spot, rows)] = source[...]


def pick_kernel(place_ref, source, out):
    rows = out.shape[0]
    out[...] = source[pl.ds(pl.multiple_of(place_ref[2] * rows, rows), rows)]


def total_of(arrays, place):
    total = arrays[0][place].astype(F32)
    for array in arrays[1:]:
        total = total + array[place].astype(F32)
    return total


def fold_kernel(*refs):
    arrays, (next_keep, next_send) = refs[:-2], refs[-2:]
    half = next_keep.shape[0]
    for place in range(half):
        next_send[place] = total_of(arrays, half + place).astype(LOW)
        next_keep[place] = total_of(arrays, place).astype(LOW)


def sum_kernel(*refs):
    for place in range(refs[-1].shape[0]):
        refs[-1][place] = total_of(refs[:-1], place).astype(LOW)


def split_kernel(keep, got_0, got_1, got_2, got_3, near_0, near_1, far_0, far_1):
    half = got_0.shape[0]
    pieces = ((0, got_0, near_0), (0, got_1, near_1), (1, got_2, far_0), (1, got_3, far_1))
    for number, (part, got, target) in enumerate(pieces):
        for place in range(half):
            first = keep[part, number % 2 * half + place].astype(F32)
            target[place] = (first + got[place].astype(F32)).astype(LOW)


def split_whole_kernel(keep, got_0, got_1, got_2, got_3, near, far):
    half = got_0.shape[0]
    split_kernel(
        keep, got_0, got_1, got_2, got_3,
        near.at[0:half], near.at[half:], far.at[0:half], far.at[half:],
    )


def enc_mlp_share_kernel(keep, got, up_ref, down_ref):
    piece, units = up_ref.shape
    total = total_of((keep, got), 0)
    up_ref[...] = total[:piece, :units]
    down_ref[...] = total[:piece, units:]


def enc_attn_share_kernel(keep, got, qkv_ref, out_ref, *vectors):
    total = total_of((keep, got), 0)
    inner, piece = out_ref.shape
    qkv_ref[...] = total[:piece, : 3 * inner].T
    out_ref[...] = total[:piece, 3 * inner :].T
    for row, vector in zip((10, 8, 9, 1, 0), vectors[:5], strict=True):
        vector[...] = total[total.shape[0] - VEC_ROWS + row, :piece]
    norms = total[total.shape[0] - VEC_ROWS :, :piece]
    vectors[5][...] = jnp.concatenate([norms[11:13], jnp.zeros((6, piece), F32)], 0)


def dec_up_share_kernel(keep, got, up_ref, proj_ref):
    total = total_of((keep, got), 0)
    piece, units = up_ref.shape
    enc_piece, column = proj_ref.shape
    up_ref[...] = total[:, :units]
    rest = enc_piece - piece
    ends = total[:, units + column : units + column + column // 2]
    ends = jnp.concatenate([ends[:rest], ends[rest:]], 1)
    proj_ref[...] = jnp.concatenate([total[:, units : units + column], ends], 0).astype(LOW)


def dec_down_share_kernel(keep, got, down_ref, qkv_ref, out_ref, *vectors):
    total = total_of((keep, got), 0)
    piece, units = down_ref.shape
    inner = out_ref.shape[0]
    down_ref[...] = total[:, :units]
    qkv_ref[...] = total[:, units : units + 3 * inner].T
    out_ref[...] = total[:, units + 3 * inner : units + 4 * inner].T
    rows = total[:, units + 4 * inner :].T
    for row in range(9):
        vectors[row][...] = rows[row, :piece]


def norm_add_kernel(first, second, out):
    out[...] = first[...] + second[...]


def norm_share_kernel(first, second, gain_ref, shift_ref):
    total = first[...] + second[...]
    gain_ref[...] = total[0]
    shift_ref[...] = total[1]


def proj_kernel(place_ref, own, core, far, out):
    column = own.shape[1]
    for apart, part in enumerate((own[...], core[...], far[0], far[1])):
        spot = pl.multiple_of((place_ref[0] ^ apart) * column, column)
        out[:, pl.ds(spot, column)] = part.astype(F32)


def decoded_kernel(place_ref, keep, got, far, out):
    chips = keep.shape[1]
    for index in range(chips):
        pieces = (keep[0, index], got[0, index], far[0, index], far[1, index])
        for apart, piece in enumerate(pieces):
            out[(place_ref[0] ^ apart) * chips + index] = piece.astype(F32)


def swap(values, axis, apart):
    size = lax.axis_size(axis)
    return lax.ppermute(values, axis, [(i, i ^ apart) for i in range(size)])


class Chain:
    def __init__(self, line, name, keep, send):
        self.line, self.name, self.keep, self.distance, self.step = line, name, list(keep), 1, 0
        self.got = swap(send, "dp", 1)

    def fold(self):
        half = self.places() // 2
        out = jax.ShapeDtypeStruct((half,) + self.got.shape[1:], LOW)
        self.step += 1
        keep, send = self.line.call(
            fold_kernel, [out, out], [*self.keep, self.got], name="%s_fold_%d" % (self.name, self.step)
        )
        self.keep = [keep]
        self.distance *= 2
        self.got = swap(send, "dp", self.distance)

    def places(self):
        return self.got.shape[0]

    def addends(self):
        while self.places() > 1:
            self.fold()
        return [*self.keep, self.got]


def body(
    band_patches,
    band_counts,
    visible_index,
    enc_attn_gain,
    enc_attn_shift,
    enc_qkv_weight,
    enc_out_weight,
    enc_out_bias,
    enc_mlp_gain,
    enc_mlp_shift,
    enc_up_weight,
    enc_up_bias,
    enc_down_weight,
    enc_down_bias,
    proj_weight,
    proj_bias,
    mask_token,
    dec_attn_gain,
    dec_attn_shift,
    dec_qkv_weight,
    dec_out_weight,
    dec_out_bias,
    dec_mlp_gain,
    dec_mlp_shift,
    dec_up_weight,
    dec_up_bias,
    dec_down_weight,
    dec_down_bias,
    cotangent,
):
    parts = lax.axis_size("tensor")
    blocks = lax.axis_size("dp")
    bits = blocks.bit_length() - 1
    rank = lax.axis_index("tensor")
    number = lax.axis_index("dp")
    place = jnp.stack([rank, bit_reverse(number, bits), number % 4]).astype(jnp.int32)
    chips, length = visible_index.shape
    band_total, own_patches = band_patches.shape[1:3]
    own_chips = chips // parts
    enc_width = band_patches.shape[3]
    patches, dec_width = cotangent.shape[1:]
    enc_inner = enc_out_weight.shape[0]
    enc_units = enc_up_weight.shape[1]
    dec_units = dec_up_weight.shape[1]
    dec_inner = dec_out_weight.shape[0]
    dec_kinds = 3 * dec_inner
    rows = chips * length
    shape = jax.ShapeDtypeStruct
    half_rows = shape((rows // 2, enc_width), LOW)
    quarter_rows = shape((rows // 4, enc_width), LOW)
    all_rows = shape((rows, enc_width), LOW)
    wide_rows = shape((rows, enc_width), F32)
    hidden_shape = shape((rows, enc_units), LOW)
    vec_shape = shape((8, enc_width), F32)
    part_shapes = [half_rows, quarter_rows, quarter_rows]

    line = Line()
    call = line.call

    def core(values):
        return swap(values, "tensor", 1)

    def add_cores(parts, name, after=()):
        keep, *sends = parts
        return call(add_kernel, [half_rows], [keep, *map(core, sends)], after=after, name=name)[0]

    def cross(own, name, after=()):
        pair = call(
            add_crossed_kernel, [quarter_rows] * 2, [own, swap(own, "tensor", 2)], after=after, name=name
        )
        return [*pair, *map(core, pair)]

    w_own = jnp.concatenate(
        [
            dec_qkv_weight.reshape(dec_kinds, dec_width),
            dec_out_weight,
            dec_up_weight,
            dec_down_weight,
        ],
        0,
    )
    angles = lax.broadcasted_iota(F32, (patches, dec_width // 2), 0) * jnp.exp(
        lax.broadcasted_iota(F32, (patches, dec_width // 2), 1)
        * (-math.log(10000.0) / (dec_width // 2))
    )
    position = jnp.concatenate([jnp.sin(angles), jnp.cos(angles)], 1)
    own_visible = lax.dynamic_slice_in_dim(visible_index, rank * own_chips, own_chips, 0)
    own_cotangent = lax.dynamic_slice_in_dim(cotangent, rank * own_chips, own_chips, 0)
    own_cotangent = own_cotangent.reshape(-1, dec_width)
    w_core = core(w_own)
    w_rows = w_own.shape[0] // 4
    w_pick = call(
        pick_kernel, [shape((w_rows, dec_width), LOW)], [w_own], scalars=[place], name="enc_pick"
    )[0]
    w_fourths = [swap(w_pick, "tensor", 2)]
    w_fourths.append(swap(w_fourths[0], "dp", 1))
    w_fourths.append(swap(w_fourths[0], "dp", 2))
    w_fourths.append(swap(w_fourths[2], "dp", 1))

    parts_here = call(
        functools.partial(band_mean_kernel, own_chips=own_chips),
        part_shapes,
        [band_patches, visible_index],
        scalars=[place, band_counts],
        name="band_mean",
    )
    own = add_cores(parts_here, "enc_add_tokens", [w_fourths[0]])
    tok = cross(own, "enc_cross_tokens")

    qkv_w = enc_qkv_weight.reshape(3 * enc_inner, enc_width)
    *parts_here, enc_n1, enc_qkv, enc_mixed = call(
        functools.partial(enc_attn_kernel, length=length),
        part_shapes + [all_rows, shape((rows, 3 * enc_inner), LOW), shape((rows, enc_inner), LOW)],
        [*tok, enc_attn_gain, enc_attn_shift, qkv_w, enc_out_weight],
        after=[w_fourths[1], w_fourths[2], position, own_cotangent, own_visible],
        name="enc_attn",
    )
    own = add_cores(parts_here, "enc_add_attn", [w_fourths[3]])
    w_x, w_diag = call(
        assemble_kernel,
        [shape(w_own.shape, LOW)] * 2,
        [*w_fourths, *map(core, w_fourths)],
        scalars=[place],
        name="enc_assemble",
    )
    sums = cross(own, "enc_cross_attn")
    *parts_here, enc_n2, enc_act, enc_slope = call(
        enc_mlp_kernel,
        [quarter_rows] * 4 + [all_rows, hidden_shape, hidden_shape],
        [
            *tok, *sums, enc_out_bias, enc_mlp_gain, enc_mlp_shift,
            enc_up_weight, enc_up_bias, enc_down_weight,
        ],
        name="enc_mlp",
    )
    far, near = call(
        add_two_kernel,
        [quarter_rows] * 2,
        [parts_here[1], core(parts_here[3]), parts_here[0], core(parts_here[2])],
        name="enc_add_mlp",
    )
    enc_low = call(
        enc_out_kernel,
        [quarter_rows],
        [tok[0], sums[0], enc_out_bias, near, swap(far, "tensor", 2), enc_down_bias],
        name="enc_out",
    )[0]

    dec_rows = own_chips * patches
    dec_all = shape((dec_rows, dec_width), LOW)
    dec_hidden = shape((parts, dec_rows, dec_units), LOW)
    dec_column = shape((parts // 2, own_chips, patches, dec_width // parts), LOW)
    (
        decoded_keep, decoded_send, grad_latent, dec_n1, dec_n2, dec_gml, dec_act, dec_hid,
        dec_gqkv, dec_mixed, dec_vec, dec_upvec,
    ) = call(
        dec_kernel,
        [
            dec_column, dec_column, shape((own_chips * length, dec_width), LOW), dec_all, dec_all,
            dec_all, dec_hidden, dec_hidden, shape((parts, dec_rows, 3 * HEAD), LOW),
            shape((parts, dec_rows, HEAD), LOW), shape((8, dec_width), F32), shape((8, dec_units), F32),
        ],
        [
            enc_low, proj_weight, proj_bias, mask_token, position, own_visible, dec_attn_gain,
            dec_attn_shift, dec_out_bias, dec_mlp_gain, dec_mlp_shift, dec_down_bias, dec_up_bias,
            w_own, w_core, w_x, w_diag, own_cotangent,
        ],
        scalars=[place],
        name="decoder",
        vmem=DEC_VMEM_BYTES,
        scratch=[
            pltpu.VMEM((parts, dec_rows, dec_units), LOW),
            pltpu.VMEM((parts, dec_rows, patches), F32),
            pltpu.VMEM((parts, dec_rows, 3 * HEAD), LOW),
        ],
    )
    lat = [grad_latent, swap(grad_latent, "tensor", 2)]
    lat = [*lat, *map(core, lat)]
    decoded_got = core(decoded_send)

    dec_piece = dec_width // blocks
    enc_piece = enc_width // blocks
    enc_rows = -(-enc_piece // 16) * 16
    proj_own = dec_width // parts
    dec_bundle = shape((2, blocks, dec_piece, dec_units + 2 * proj_own), LOW)
    up_keep, *up_sends = call(
        dec_up_kernel,
        [dec_bundle] + [shape((blocks // 2,) + dec_bundle.shape[2:], LOW)] * 4,
        [dec_n2, dec_hid, enc_low, grad_latent],
        scalars=[place],
        name="dec_up",
    )

    *parts_here, enc_out_grad_in, enc_gol, enc_hid, vec_mlp = call(
        enc_mlp_back_kernel,
        part_shapes + [wide_rows, all_rows, hidden_shape, vec_shape],
        [*lat, proj_weight, enc_slope, enc_up_weight, enc_down_weight],
        name="enc_mlp_back",
    )
    bundle = shape((blocks // 2, enc_rows, 2 * enc_units), LOW)
    mlp_keep, mlp_send = call(
        enc_mlp_weights_kernel,
        [bundle, bundle],
        [enc_n2, enc_hid, enc_gol, enc_act],
        scalars=[place],
        name="enc_mlp_weights",
    )
    mlp_chain = Chain(line, "enc_mlp", [mlp_keep], mlp_send)
    own = add_cores(parts_here, "enc_add_back")
    out = shape(up_keep.shape[1:], LOW)
    up_near, up_far = call(
        split_whole_kernel, [out, out], [up_keep, *map(core, up_sends)], name="dec_up_split"
    )
    up_far = swap(up_far, "tensor", 2)

    dec_bundle = shape((2, blocks, dec_piece, dec_units + 4 * dec_inner + 128), LOW)
    down_keep, *down_sends = call(
        dec_down_kernel,
        [dec_bundle] + [shape((blocks // 2,) + dec_bundle.shape[2:], LOW)] * 4,
        [own_cotangent, dec_act, dec_n1, dec_gqkv, dec_gml, dec_mixed, dec_vec, dec_upvec],
        scalars=[place],
        name="dec_down",
    )
    backs = cross(own, "enc_cross_back")

    *parts_here, enc_mid, enc_gml, enc_gqkv, vec_attn = call(
        functools.partial(enc_attn_back_kernel, length=length),
        part_shapes + [wide_rows, all_rows, shape((rows, 3 * enc_inner), LOW), vec_shape],
        [
            *tok, *sums, *backs, enc_out_bias, enc_mlp_gain, enc_out_grad_in, enc_qkv, qkv_w,
            enc_out_weight,
        ],
        name="enc_attn_back",
    )
    bundle = shape((blocks // 2, enc_rows + VEC_ROWS, 4 * enc_inner), LOW)
    attn_keep, attn_send = call(
        enc_attn_weights_kernel,
        [bundle, bundle],
        [enc_n1, enc_gqkv, enc_gml, enc_mixed, vec_mlp, vec_attn],
        scalars=[place],
        name="enc_attn_weights",
    )
    attn_chain = Chain(line, "enc_attn", [attn_keep], attn_send)
    own = add_cores(parts_here, "enc_add_grad")

    out = shape((blocks // 2,) + down_keep.shape[2:], LOW)
    *down_near, far_0, far_1 = call(
        split_kernel, [out] * 4, [down_keep, *map(core, down_sends)], name="dec_down_split"
    )
    far_1 = swap(far_1, "tensor", 2)
    far_0 = swap(far_0, "tensor", 2)
    out = shape((blocks // 2,) + up_near.shape[1:], LOW)
    up_keep, up_send = call(fold_kernel, [out, out], [up_near, up_far], name="dec_up_first")
    up_chain = Chain(line, "dec_up", [up_keep], up_send)
    mlp_chain.fold()
    grads = cross(own, "enc_cross_grad")
    attn_chain.fold()
    mlp_chain.fold()
    down_send = call(
        sum_kernel, [shape(far_1.shape, LOW)], [down_near[1], far_1], name="dec_down_first"
    )[0]
    down_chain = Chain(line, "dec_down", [down_near[0], far_0], down_send)
    up_chain.fold()
    attn_chain.fold()
    band_grad = call(
        functools.partial(band_grad_kernel, own_chips=own_chips),
        [InHbm(shape(band_patches.shape, F32))],
        [*tok, *grads, enc_mid, enc_attn_gain, visible_index],
        scalars=[place, band_counts],
        name="band_grad",
        scratch=[
            pltpu.VMEM((chips + 1, own_patches, enc_width), F32),
            pltpu.SemaphoreType.DMA((chips, band_total)),
        ],
    )[0]
    up_chain.fold()
    enc_vector = shape((enc_piece,), F32)
    dec_vector = shape((dec_piece,), F32)
    enc_up_grad, enc_down_grad = call(
        enc_mlp_share_kernel,
        [shape((enc_piece, enc_units), F32)] * 2,
        mlp_chain.addends(),
        name="enc_mlp_share",
    )
    down_chain.fold()
    enc_qkv_grad, enc_out_grad, *enc_vecs = call(
        enc_attn_share_kernel,
        [shape((3 * enc_inner, enc_piece), F32), shape((enc_inner, enc_piece), F32)]
        + [enc_vector] * 5
        + [shape((8, enc_piece), F32)],
        attn_chain.addends(),
        name="enc_attn_share",
    )
    norm_core = core(enc_vecs[5])
    dec_up_grad, proj_part = call(
        dec_up_share_kernel,
        [shape((dec_piece, dec_units), F32), shape((enc_piece, proj_own), LOW)],
        up_chain.addends(),
        name="dec_up_share",
    )
    proj_core = core(proj_part)
    decoded_far = swap(jnp.stack([decoded_keep[1], decoded_got[1]]), "tensor", 2)
    decoded = call(
        decoded_kernel,
        [shape((chips, patches, dec_width // parts), F32)],
        [decoded_keep, decoded_got, decoded_far],
        scalars=[place],
        name="decoded_share",
    )[0]
    norm_pair = call(
        norm_add_kernel, [shape((8, enc_piece), F32)], [enc_vecs[5], norm_core], name="enc_norm_add"
    )[0]
    norm_far = swap(norm_pair, "tensor", 2)
    proj_far = swap(jnp.stack([proj_part, proj_core]), "tensor", 2)
    down_chain.fold()
    norm_grads = call(norm_share_kernel, [enc_vector] * 2, [norm_pair, norm_far], name="enc_norm_share")
    proj_grad = call(
        proj_kernel,
        [shape((enc_piece, dec_width), F32)],
        [proj_part, proj_core, proj_far],
        scalars=[place],
        name="dec_proj_share",
    )[0]
    dec_down_grad, dec_qkv_grad, dec_out_grad, *dec_vecs = call(
        dec_down_share_kernel,
        [
            shape((dec_piece, dec_units), F32),
            shape((dec_kinds, dec_piece), F32),
            shape((dec_inner, dec_piece), F32),
        ]
        + [dec_vector] * 9,
        down_chain.addends(),
        name="dec_down_share",
    )
    return (
        decoded,
        band_grad,
        *norm_grads,
        enc_qkv_grad.reshape(3, enc_inner, enc_piece),
        enc_out_grad,
        enc_vecs[0],
        enc_vecs[1],
        enc_vecs[2],
        enc_up_grad,
        enc_vecs[3],
        enc_down_grad.T,
        enc_vecs[4],
        proj_grad,
        dec_vecs[6],
        dec_vecs[7],
        dec_vecs[0],
        dec_vecs[1],
        dec_qkv_grad.reshape(3, dec_inner, dec_piece),
        dec_out_grad,
        dec_vecs[2],
        dec_vecs[3],
        dec_vecs[4],
        dec_up_grad,
        dec_vecs[8],
        dec_down_grad.T,
        dec_vecs[5],
    )


def solution(mesh):
    in_specs = (
        P("dp", None, "tensor", None),
        P("dp"),
        P("dp", None),
        P(),
        P(),
        P(None, "tensor", None),
        P("tensor", None),
        P(),
        P(),
        P(),
        P(None, "tensor"),
        P("tensor"),
        P("tensor", None),
        P(),
        P(),
        P(),
        P(),
        P(),
        P(),
        P(None, "tensor", None),
        P("tensor", None),
        P(),
        P(),
        P(),
        P(None, "tensor"),
        P(),
        P("tensor", None),
        P(),
        P("dp", None, None),
    )
    out_specs = (
        P("dp", None, "tensor"),
        P("dp", None, "tensor", None),
        P("dp"),
        P("dp"),
        P(None, "tensor", "dp"),
        P("tensor", "dp"),
        P("dp"),
        P("dp"),
        P("dp"),
        P("dp", "tensor"),
        P(("tensor", "dp")),
        P("tensor", "dp"),
        P("dp"),
        P("dp", None),
        P("dp"),
        P("dp"),
        P("dp"),
        P("dp"),
        P(None, "tensor", "dp"),
        P("tensor", "dp"),
        P("dp"),
        P("dp"),
        P("dp"),
        P("dp", "tensor"),
        P(("tensor", "dp")),
        P("tensor", "dp"),
        P("dp"),
    )
    return jax.shard_map(body, mesh=mesh, in_specs=in_specs, out_specs=out_specs, check_vma=False)
```

```python
import functools
import math

import jax
import jax.numpy as jnp
from jax import lax
from jax.experimental import pallas as pl
from jax.experimental.pallas import tpu as pltpu
from jax.sharding import PartitionSpec as P

HEAD = 64
EPSILON = 1e-05
SCALE = HEAD ** (-0.5)
VMEM_BYTES = 24 * 1024 * 1024
DEC_VMEM_BYTES = 30 * 1024 * 1024
F32 = jnp.float32
LOW = jnp.bfloat16
NN = (((1,), (0,)), ((), ()))
NT = (((1,), (1,)), ((), ()))
TN = (((0,), (0,)), ((), ()))
VEC_ROWS = 16
UP_HALVES, DOWN_HALVES = False, True
ORDER = (
    "dec_up", "pair", "mlp_back", "add_back", "mlp_early", "lat_core", "up_split", "mlp_weights", "dec_down",
    "cross_back", "attn_back", "down_split", "attn_weights", "add_grad", "mlp", "up", "down", "attn", "mlp",
    "up", "up", "cross_grad", "down", "up", "attn", "down", "band_grads", "down", "attn", "finish", "norm_add",
    "proj_far", "decoded_share", "proj_share", "norm_share",
)
KINDS = ("y", "z", "paired")
ATTN, UP, DOWN = "y", "z", "y"


def dot(left, right, dims=NN):
    return lax.dot_general(left, right, dims, preferred_element_type=F32)


def col_sum(values):
    return jnp.sum(values, 0, keepdims=True)


def vec(ref):
    return ref[...][None, :]


def norm_parts(stream):
    center = stream - jnp.mean(stream, -1, keepdims=True)
    inverse = lax.rsqrt(jnp.mean(center * center, -1, keepdims=True) + EPSILON)
    return center * inverse, inverse


def norm_back(grad, xhat, inverse, gain):
    scaled = grad * gain
    mean_q = jnp.mean(scaled, -1, keepdims=True)
    mean_qx = jnp.mean(scaled * xhat, -1, keepdims=True)
    return inverse * (scaled - mean_q - xhat * mean_qx)


def gelu_parts(hidden):
    phi = 0.5 + 0.5 * lax.erf(hidden * (0.5**0.5))
    density = jnp.exp(hidden * hidden * -0.5) * (1.0 / math.sqrt(2.0 * math.pi))
    return hidden * phi, phi + hidden * density


def softmax_rows(scores):
    weights = jnp.exp(scores - jnp.max(scores, -1, keepdims=True))
    return weights * (1.0 / jnp.sum(weights, -1, keepdims=True))


def same_chip(rows, length):
    first = lax.broadcasted_iota(jnp.int32, (rows, rows), 0) // length
    second = lax.broadcasted_iota(jnp.int32, (rows, rows), 1) // length
    return first == second


def attend(queries, keyset, mask):
    scores = dot(queries, keyset, NT) * SCALE
    if mask is not None:
        scores = jnp.where(mask, scores, -1e30)
    return softmax_rows(scores)


def attend_back(probs, queries, keyset, valset, grad_mixed):
    grad_probs = dot(grad_mixed, valset, NT)
    grad_values = dot(probs.astype(LOW), grad_mixed, TN)
    grad_scores = probs * (grad_probs - jnp.sum(grad_probs * probs, -1, keepdims=True))
    score_low = grad_scores.astype(LOW)
    grad_queries = dot(score_low, keyset) * SCALE
    grad_keys = dot(score_low, queries, TN) * SCALE
    return grad_queries.astype(LOW), grad_keys.astype(LOW), grad_values.astype(LOW)


class Line:
    def __init__(self):
        self.token = None

    def call(self, body, out_shape, args, scalars=(), after=(), name=None, scratch=(), vmem=VMEM_BYTES):
        after = list(after) + ([] if self.token is None else [self.token])
        specs = [pl.BlockSpec(memory_space=pltpu.SMEM) for _ in scalars]
        specs += [pl.BlockSpec(memory_space=pltpu.VMEM) for _ in args]
        specs += [pl.BlockSpec(memory_space=pl.ANY) for _ in after]
        inputs = len(scalars) + len(args)
        outputs = len(out_shape)
        out_specs = []
        for out in out_shape:
            in_hbm = isinstance(out, InHbm)
            out_specs.append(pl.BlockSpec(memory_space=pltpu.HBM if in_hbm else pltpu.VMEM))
        out_shape = [out.array if isinstance(out, InHbm) else out for out in out_shape]
        out_shape = [jax.ShapeDtypeStruct(out.shape, out.dtype) for out in out_shape]

        def wrapped(*refs):
            outs = refs[inputs + len(after) :]
            outs[outputs][...] = jnp.zeros_like(outs[outputs])
            body(*refs[:inputs], *outs[:outputs], *outs[outputs + 1 :])

        *found, self.token = pl.pallas_call(
            wrapped,
            out_shape=out_shape + [jax.ShapeDtypeStruct((8, 128), F32)],
            in_specs=specs,
            out_specs=out_specs + [pl.BlockSpec(memory_space=pltpu.VMEM)],
            scratch_shapes=list(scratch),
            compiler_params=pltpu.CompilerParams(vmem_limit_bytes=vmem),
            cost_estimate=pl.CostEstimate(flops=1, bytes_accessed=1, transcendentals=0),
            name=name,
        )(*scalars, *args, *after)
        return found


class InHbm:
    def __init__(self, array):
        self.array = array


def steps_of(blocks, kind):
    steps = list(range(blocks.bit_length() - 1))
    if kind == "z":
        steps[:2] = [1, 0]
    if kind == "paired":
        steps.remove(1)
    return steps


def place_of(value, blocks, kind):
    steps = steps_of(blocks, kind)
    result = 0
    for place, bit in enumerate(steps):
        result = result | (((value >> bit) & 1) << (len(steps) - 1 - place))
    return result


def spot_of(place_ref, block, blocks, kind):
    return place_ref[1 + KINDS.index(kind)] ^ place_of(block, blocks, kind)


def put_block(keep, send, lead, place, half, rows, columns, values):
    @pl.when(place < half)
    def _():
        keep[lead + (place, rows, columns)] = values

    @pl.when(place >= half)
    def _():
        send[lead + (place - half, rows, columns)] = values


def chip_of(step, rank, own_chips):
    part, index = step // own_chips, step % own_chips
    apart = 2 * (part % 2) + part // 2
    return (rank ^ apart) * own_chips + index


def put_rows(parts, first, values):
    for part in parts:
        if first < part.shape[0]:
            part[first : first + values.shape[0]] = values
            return
        first -= part.shape[0]


def get_rows(parts, first, count):
    found = []
    for part in parts:
        size = part.shape[0]
        if first < size and count > 0:
            taken = min(count, size - first)
            found.append(part[first : first + taken])
            count -= taken
            first = size
        first -= size
    return found[0] if len(found) == 1 else jnp.concatenate(found, 0)


def band_mean_kernel(place_ref, count_ref, bands_ref, visible_ref, *parts, own_chips):
    rank = place_ref[0]
    chips, bands, own, width = bands_ref.shape
    length = visible_ref.shape[1]
    patch = lax.broadcasted_iota(jnp.int32, (own, length), 0) + rank * own
    for step in range(chips):
        spot = chip_of(step, rank, own_chips)
        count = count_ref[spot]
        means = []
        for first in range(0, own, 16):
            span = slice(first, first + 16)
            total = bands_ref[spot, 0, span].astype(F32)
            for band in range(1, bands):
                used = jnp.where(band < count, 1.0, 0.0).astype(F32)
                total = total + bands_ref[spot, band, span].astype(F32) * used
            means.append((total / count.astype(F32)).astype(LOW))
        chosen = visible_ref[pl.ds(spot, 1)] == patch
        chosen = jnp.where(chosen, 1.0, 0.0).astype(LOW)
        values = dot(chosen, jnp.concatenate(means, 0), TN).astype(LOW)
        put_rows(parts, step * length, values)


def enc_attn_kernel(*refs, length):
    tok, (gain, shift, qkv_w, out_w) = refs[:4], refs[4:8]
    parts, (normed_ref, qkv_ref, mixed_ref, prob_ref) = refs[8:11], refs[11:]
    rows = normed_ref.shape[0] // 2
    inner = out_w.shape[0]
    block = 2 * length
    mask = same_chip(block, length)
    for group in range(2):
        span = slice(group * rows, (group + 1) * rows)
        xhat, _ = norm_parts(get_rows(tok, group * rows, rows).astype(F32))
        normed = (xhat * vec(gain) + vec(shift)).astype(LOW)
        normed_ref[span] = normed
        qkv = dot(normed, qkv_w[...], NT).astype(LOW)
        qkv_ref[span] = qkv
        blocks = []
        for first in range(0, rows, block):
            heads = []
            for head in range(inner // HEAD):
                at = [
                    qkv[first : first + block, k * inner + head * HEAD : k * inner + (head + 1) * HEAD]
                    for k in range(3)
                ]
                probs = attend(at[0], at[1], mask)
                prob_ref[head, group * rows + first : group * rows + first + block] = probs
                heads.append(dot(probs.astype(LOW), at[2]).astype(LOW))
            blocks.append(jnp.concatenate(heads, 1))
        mixed = jnp.concatenate(blocks, 0)
        mixed_ref[span] = mixed
        part = dot(mixed, out_w[...]).astype(LOW)
        for first in range(0, rows, block):
            put_rows(parts, group * rows + first, part[first : first + block])


def own_columns(values, which, blocks):
    piece = values.shape[1] // blocks
    kinds = []
    for bit in range(2):
        starts = [(4 * run + 2 * bit) * piece for run in range(blocks // 4)]
        kinds.append(jnp.concatenate([values[:, start : start + 2 * piece] for start in starts], 1))
    return jnp.where(which == 0, kinds[0], kinds[1])


def enc_mlp_kernel(*refs):
    tok, sums = refs[:4], refs[4:8]
    out_bias, gain, shift, up_w, up_bias, down_w = refs[8:14]
    parts, (normed_ref, act_ref, slope_ref) = refs[14:18], refs[18:]
    rows = normed_ref.shape[0] // 2
    block = rows // 2
    for group in range(2):
        span = slice(group * rows, (group + 1) * rows)
        middle = get_rows(tok, group * rows, rows).astype(F32) + vec(out_bias)
        middle = middle + get_rows(sums, group * rows, rows).astype(F32)
        xhat, _ = norm_parts(middle)
        normed = (xhat * vec(gain) + vec(shift)).astype(LOW)
        normed_ref[span] = normed
        activation, slope = gelu_parts(dot(normed, up_w[...]) + vec(up_bias))
        act_low, slope_low = activation.astype(LOW), slope.astype(LOW)
        act_ref[span] = act_low
        slope_ref[span] = slope_low
        part = dot(act_low, down_w[...]).astype(LOW)
        for first in range(0, rows, block):
            put_rows(parts, group * rows + first, part[first : first + block])


def enc_out_kernel(tok, total, out_bias, own, other, down_bias, low_ref):
    low_ref[...] = (
        tok[...].astype(F32)
        + total[...].astype(F32)
        + vec(out_bias)
        + own[...].astype(F32)
        + other[...].astype(F32)
        + vec(down_bias)
    ).astype(LOW)


def enc_mlp_back_kernel(lat_pair, lat_core, proj_w, slope_ref, up_w, down_w, *refs):
    lat = (lat_pair.at[0], lat_pair.at[1], lat_core.at[0], lat_core.at[1])
    parts, (out_ref, low_ref, hidden_ref, vec_ref) = refs[:3], refs[3:]
    rows = out_ref.shape[0] // 2
    block = rows // 2
    down_sum, up_sum = 0.0, 0.0
    for group in range(2):
        span = slice(group * rows, (group + 1) * rows)
        grad_out = dot(get_rows(lat, group * rows, rows), proj_w[...], NT)
        out_ref[span] = grad_out
        grad_low = grad_out.astype(LOW)
        low_ref[span] = grad_low
        grad_hidden = dot(grad_low, down_w[...], NT) * slope_ref[span].astype(F32)
        hidden_low = grad_hidden.astype(LOW)
        hidden_ref[span] = hidden_low
        down_sum = down_sum + col_sum(grad_out)
        up_sum = up_sum + col_sum(grad_hidden)
        part = dot(hidden_low, up_w[...], NT).astype(LOW)
        for first in range(0, rows, block):
            put_rows(parts, group * rows + first, part[first : first + block])
    vec_ref[...] = jnp.concatenate(
        [down_sum, up_sum, jnp.zeros((vec_ref.shape[0] - 2, down_sum.shape[1]), F32)], 0
    )


def enc_mlp_early_kernel(early_ref, up_w, up_bias, act_ref, slope_ref):
    activation, slope = gelu_parts(dot(early_ref[...], up_w[...]) + vec(up_bias))
    act_ref[...] = activation.astype(LOW)
    slope_ref[...] = slope.astype(LOW)


def enc_mlp_weights_kernel(
    place_ref, normed_ref, hidden_ref, low_ref, act_ref, early_ref, early_act, early_slope, lat_pair, lat_core,
    proj_w, down_w, keep, send
):
    half = keep.shape[0]
    blocks = 4 * half
    width, units = normed_ref.shape[1], hidden_ref.shape[1]
    piece = width // blocks
    which = place_ref[4] // 2
    lat = jnp.concatenate([lat_pair[0], lat_pair[1], lat_core[0], lat_core[1]], 0)
    low = dot(lat, proj_w[...], NT).astype(LOW)
    hidden = (dot(low, down_w[...], NT) * early_slope[...].astype(F32)).astype(LOW)
    for kind in range(2):
        if kind == 0:
            found = dot(own_columns(normed_ref[...], which, blocks), hidden_ref[...], TN)
            found = found + dot(own_columns(early_ref[...], which, blocks), hidden, TN)
        else:
            found = dot(own_columns(low_ref[...], which, blocks), act_ref[...], TN)
            found = found + dot(own_columns(low, which, blocks), early_act[...], TN)
        columns = slice(kind * units, (kind + 1) * units)
        for block in range(blocks // 2):
            values = found[block * piece : (block + 1) * piece].astype(LOW)
            place = spot_of(place_ref, 4 * (block // 2) + block % 2, blocks, "paired")
            put_block(keep, send, (), place, half, slice(0, piece), columns, values)


def enc_attn_back_kernel(*refs, length):
    tok, sums, backs = refs[:4], refs[4:8], refs[8:12]
    out_bias, mlp_gain, out_ref, qkv_ref, qkv_w, out_w, prob_ref = refs[12:19]
    parts, (mid_ref, low_ref, grad_qkv_ref, vec_ref) = refs[19:22], refs[22:]
    rows = out_ref.shape[0] // 2
    inner = out_w.shape[0]
    block = 2 * length
    found = [0.0] * 5
    for group in range(2):
        span = slice(group * rows, (group + 1) * rows)
        stream = get_rows(tok, group * rows, rows).astype(F32)
        total = get_rows(sums, group * rows, rows).astype(F32)
        xhat, inverse = norm_parts(stream + total + vec(out_bias))
        grad = get_rows(backs, group * rows, rows).astype(F32)
        found[0] = found[0] + col_sum(grad * xhat)
        found[1] = found[1] + col_sum(grad)
        grad_middle = out_ref[span] + norm_back(grad, xhat, inverse, vec(mlp_gain))
        mid_ref[span] = grad_middle
        found[2] = found[2] + col_sum(grad_middle)
        middle_low = grad_middle.astype(LOW)
        low_ref[span] = middle_low
        grad_mixed = dot(middle_low, out_w[...], NT).astype(LOW)
        blocks = []
        for first in range(0, rows, block):
            near = slice(group * rows + first, group * rows + first + block)
            grads = ([], [], [])
            for head in range(inner // HEAD):
                at = [
                    qkv_ref[near, k * inner + head * HEAD : k * inner + (head + 1) * HEAD]
                    for k in range(3)
                ]
                own = grad_mixed[first : first + block, head * HEAD : (head + 1) * HEAD]
                for kind, values in enumerate(attend_back(prob_ref[head, near], *at, own)):
                    grads[kind].append(values)
            blocks.append(jnp.concatenate(grads[0] + grads[1] + grads[2], 1))
        grad_qkv = jnp.concatenate(blocks, 0)
        grad_qkv_ref[span] = grad_qkv
        partial = dot(grad_qkv, qkv_w[...])
        part = partial.astype(LOW)
        for first in range(0, rows, block):
            put_rows(parts, group * rows + first, part[first : first + block])
        xhat, _ = norm_parts(stream)
        found[3] = found[3] + col_sum(partial * xhat)
        found[4] = found[4] + col_sum(partial)
    vec_ref[...] = jnp.concatenate(
        found + [jnp.zeros((vec_ref.shape[0] - 5, found[0].shape[1]), F32)], 0
    )


def enc_attn_weights_kernel(
    place_ref, normed_ref, grad_qkv_ref, low_ref, mixed_ref, vec_mlp, vec_attn, keep, send
):
    half = keep.shape[0]
    blocks = 2 * half
    width = normed_ref.shape[1]
    qkv = dot(normed_ref[...], grad_qkv_ref[...], TN)
    out = dot(low_ref[...], mixed_ref[...], TN)
    vectors = jnp.concatenate([vec_mlp[...], vec_attn[...]], 0)
    piece = width // blocks
    first = keep.shape[1] - VEC_ROWS
    for block in range(blocks):
        at = slice(block * piece, (block + 1) * piece)
        place = spot_of(place_ref, block, blocks, ATTN)
        values = jnp.concatenate([qkv[at], out[at]], 1).astype(LOW)
        put_block(keep, send, (), place, half, slice(0, piece), slice(None), values)
        put_block(
            keep, send, (), place, half, slice(first, first + VEC_ROWS), slice(0, piece),
            vectors[:, at].astype(LOW),
        )


def band_grad_kernel(place_ref, count_ref, *refs, own_chips):
    tok, backs, (mid_ref, gain, visible_ref) = refs[:4], refs[4:8], refs[8:11]
    out_ref, stage, left = refs[11:]
    rank = place_ref[0]
    chips, bands, own, width = out_ref.shape
    length = visible_ref.shape[1]
    spots = [chip_of(step, rank, own_chips) for step in range(chips)]
    counts = [count_ref[spot] for spot in spots]

    def copy_of(source, step, band):
        return pltpu.make_async_copy(
            stage.at[source], out_ref.at[spots[step], band], left.at[step, band]
        )

    stage[chips] = jnp.zeros((own, width), F32)
    for step in range(chips):

        def blank(band, carry, step=step):
            copy_of(chips, step, band).start()
            return carry

        lax.fori_loop(counts[step], bands, blank, 0)
    patch = lax.broadcasted_iota(jnp.int32, (own, length), 0) + rank * own
    for step in range(chips):
        first = step * length
        xhat, inverse = norm_parts(get_rows(tok, first, length).astype(F32))
        back = get_rows(backs, first, length).astype(F32)
        grad = mid_ref[first : first + length] + norm_back(back, xhat, inverse, vec(gain))
        grad = grad / counts[step].astype(F32)
        chosen = visible_ref[pl.ds(spots[step], 1)] == patch
        chosen = jnp.where(chosen, 1.0, 0.0).astype(LOW)
        high = grad.astype(LOW)
        rest = (grad - high.astype(F32)).astype(LOW)
        stage[step] = dot(chosen, high) + dot(chosen, rest)

        def fill(band, carry, step=step):
            copy_of(step, step, band).start()
            return carry

        lax.fori_loop(0, counts[step], fill, 0)
    for step in range(chips):

        def finish(band, carry, step=step):
            copy_of(step, step, band).wait()
            return carry

        lax.fori_loop(0, bands, finish, 0)


def dec_kernel(
    place_ref, enc_low, proj_w, proj_bias, mask_token, position, visible_ref,
    attn_gain, attn_shift, out_bias, mlp_gain, mlp_shift, down_bias, up_bias,
    w0, w1, w2, w3, cotangent,
    decoded_keep, decoded_send, grad_latent_ref, n1_ref, n2_ref, gml_ref, act_ref, hid_ref,
    gqkv_ref, mixed_ref, vec_ref, upvec_ref,
    slope_scr, prob_scr, qkv_scr,
):
    weights = (w0, w1, w2, w3)
    parts = len(weights)
    chips, length = visible_ref.shape
    patches, width = position.shape
    kinds = 3 * HEAD
    inner = kinds + HEAD
    units = up_bias.shape[0] // parts
    up_at, down_at = slice(inner, inner + width), slice(inner + width, inner + width + units)
    spans = [slice(chip * patches, (chip + 1) * patches) for chip in range(chips)]
    latent = dot(enc_low[...], proj_w[...]) + vec(proj_bias)
    high = latent.astype(LOW)
    rest = (latent - high.astype(F32)).astype(LOW)
    streams, chosen, seen = [], [], []
    for chip in range(chips):
        near = slice(chip * length, (chip + 1) * length)
        hit = lax.broadcasted_iota(jnp.int32, (patches, length), 0) == visible_ref[chip : chip + 1]
        hit = jnp.where(hit, 1.0, 0.0)
        is_visible = jnp.sum(hit, 1, keepdims=True)
        hit = hit.astype(LOW)
        filled = dot(hit, high[near]) + dot(hit, rest[near])
        streams.append(filled + (1.0 - is_visible) * vec(mask_token) + position[...])
        chosen.append(hit)
        seen.append(is_visible)
    stream = jnp.concatenate(streams, 0)
    xhat1, inverse1 = norm_parts(stream)
    n1 = (xhat1 * vec(attn_gain) + vec(attn_shift)).astype(LOW)
    n1_ref[...] = n1
    for part, weight in enumerate(weights):
        qkv_scr[part] = dot(n1, weight[0:kinds], NT).astype(LOW)

    def qkv_of(part, span):
        return [qkv_scr[part, span, k * HEAD : (k + 1) * HEAD] for k in range(3)]

    for part in range(parts):
        for span in spans:
            queries, keyset, valset = qkv_of(part, span)
            probs = attend(queries, keyset, None)
            prob_scr[part, span] = probs
            mixed_ref[part, span] = dot(probs.astype(LOW), valset).astype(LOW)
    out_all = jnp.concatenate([weight[kinds:inner] for weight in weights], 0)
    mixed = jnp.concatenate([mixed_ref[part] for part in range(parts)], 1)
    middle = stream + dot(mixed, out_all) + vec(out_bias)
    xhat2, inverse2 = norm_parts(middle)
    n2 = (xhat2 * vec(mlp_gain) + vec(mlp_shift)).astype(LOW)
    n2_ref[...] = n2
    total = middle + vec(down_bias)
    for part, weight in enumerate(weights):
        spot = pl.multiple_of((place_ref[0] ^ part) * units, units)
        bias = up_bias[pl.ds(spot, units)][None, :]
        activation, slope = gelu_parts(dot(n2, weight[up_at]) + bias)
        act_low = activation.astype(LOW)
        act_ref[part] = act_low
        slope_scr[part] = slope.astype(LOW)
        total = total + dot(act_low, weight[down_at])
    column = width // parts
    half = parts // 2
    for part in range(parts):
        apart = place_ref[0] ^ part
        for chip, span in enumerate(spans):
            values = total[span, part * column : (part + 1) * column].astype(LOW)

            @pl.when(apart % 2 == 0)
            def _(values=values, apart=apart, chip=chip):
                decoded_keep[apart // 2, chip] = values

            @pl.when(apart % 2 == 1)
            def _(values=values, apart=apart, chip=chip):
                decoded_send[apart // 2, chip] = values

    grad_low = cotangent[...]
    grad_out = grad_low.astype(F32)
    grad_n2 = 0.0
    up_sums = []
    for part, weight in enumerate(weights):
        grad_hidden = dot(grad_low, weight[down_at], NT) * slope_scr[part].astype(F32)
        hidden_low = grad_hidden.astype(LOW)
        hid_ref[part] = hidden_low
        up_sums.append(col_sum(grad_hidden))
        grad_n2 = grad_n2 + dot(hidden_low, weight[up_at], NT)
    grad_middle = grad_out + norm_back(grad_n2, xhat2, inverse2, vec(mlp_gain))
    mlp_gain_sum, mlp_shift_sum = col_sum(grad_n2 * xhat2), col_sum(grad_n2)
    middle_low = grad_middle.astype(LOW)
    gml_ref[...] = middle_low
    grad_mixed = dot(middle_low, out_all, NT).astype(LOW)
    grad_n1 = 0.0
    for part, weight in enumerate(weights):
        for span in spans:
            own = grad_mixed[span, part * HEAD : (part + 1) * HEAD]
            found = attend_back(prob_scr[part, span], *qkv_of(part, span), own)
            gqkv_ref[part, span] = jnp.concatenate(found, 1)
        grad_n1 = grad_n1 + dot(gqkv_ref[part], weight[0:kinds])
    grad_stream = grad_middle + norm_back(grad_n1, xhat1, inverse1, vec(attn_gain))
    stream_low = grad_stream.astype(LOW)
    for chip, span in enumerate(spans):
        near = slice(chip * length, (chip + 1) * length)
        grad_latent_ref[near] = dot(chosen[chip], stream_low[span], TN).astype(LOW)
    seen_sum = col_sum(grad_stream * jnp.concatenate(seen, 0))
    vec_ref[...] = jnp.concatenate(
        [
            col_sum(grad_n1 * xhat1),
            col_sum(grad_n1),
            col_sum(grad_middle),
            mlp_gain_sum,
            mlp_shift_sum,
            col_sum(grad_out),
            seen_sum,
            col_sum(grad_stream) - seen_sum,
        ],
        0,
    )
    upvec_ref[...] = jnp.concatenate(up_sums + [jnp.zeros((8 - parts, units), F32)], 0)


def put_quarter(keep, sends, part, place, values):
    if part % 2 == 0:
        keep[part // 2, place] = values
        return
    half = sends[0].shape[0]
    put_block(sends[part - 1], sends[part], (), place, half, slice(None), slice(None), values)


def dec_up_kernel(
    place_ref, n2_ref, hid_ref, enc_low, latent, vec_ref, upvec_ref, keep, *sends
):
    parts, _, units = hid_ref.shape
    blocks = keep.shape[1]
    width, enc_width = n2_ref.shape[1], enc_low.shape[1]
    piece, enc_piece = width // blocks, enc_width // blocks
    column = latent.shape[1] // parts
    left = n2_ref[...].T
    left_proj = enc_low[...].T
    half_column = latent.shape[1] // parts // 2
    blank = jnp.zeros((half_column - 9, width), F32)
    for part in (1, 3, 0, 2):
        vectors = jnp.concatenate([vec_ref[...], upvec_ref[part : part + 1], blank], 0).T
        up = dot(left, hid_ref[part])
        spot = pl.multiple_of((place_ref[0] ^ part) * column, column)
        proj = dot(left_proj, latent[:, pl.ds(spot, column)])
        for block in range(blocks):
            first = block * enc_piece
            rest = proj[first + piece : first + enc_piece]
            rest = jnp.concatenate([rest[:, :half_column], rest[:, half_column:]], 0)
            values = jnp.concatenate(
                [
                    up[block * piece : (block + 1) * piece],
                    proj[first : first + piece],
                    rest,
                    vectors[block * piece : (block + 1) * piece],
                ],
                1,
            )
            place = spot_of(place_ref, block, blocks, UP)
            put_quarter(keep, sends, part, place, values.astype(LOW))


def dec_down_kernel(
    place_ref, cot_ref, act_ref, n1_ref, gqkv_ref, gml_ref, mixed_ref, keep, *sends
):
    parts = act_ref.shape[0]
    blocks = keep.shape[1]
    piece = n1_ref.shape[1] // blocks
    left_down, left_qkv, left_out = cot_ref[...].T, n1_ref[...].T, gml_ref[...].T
    for part in (1, 3, 0, 2):
        values = jnp.concatenate(
            [
                dot(left_down, act_ref[part]),
                dot(left_qkv, gqkv_ref[part]),
                dot(left_out, mixed_ref[part]),
            ],
            1,
        ).astype(LOW)
        for block in range(blocks):
            place = spot_of(place_ref, block, blocks, DOWN)
            put_quarter(keep, sends, part, place, values[block * piece : (block + 1) * piece])


def add_kernel(keep, got_0, got_1, out):
    half = got_0.shape[0]
    out[0:half] = (keep[0:half].astype(F32) + got_0[...].astype(F32)).astype(LOW)
    out[half:] = (keep[half:].astype(F32) + got_1[...].astype(F32)).astype(LOW)


def add_two_kernel(far_keep, far_got, near_keep, near_got, normed, far, near, early):
    early[...] = normed[...]
    far[...] = (far_keep[...].astype(F32) + far_got[...].astype(F32)).astype(LOW)
    near[...] = (near_keep[...].astype(F32) + near_got[...].astype(F32)).astype(LOW)


def add_with_kernel(keep, got_0, got_1, rest, out):
    rows = keep.shape[0]
    add_kernel(keep, got_0, got_1, out.at[0:rows])
    out[rows:] = rest[...]


def add_crossed_kernel(own, other, first, second):
    half = first.shape[0]
    first[...] = (own[0:half].astype(F32) + other[half : 2 * half].astype(F32)).astype(LOW)
    second[...] = (own[half : 2 * half].astype(F32) + other[0:half].astype(F32)).astype(LOW)


def assemble_kernel(place_ref, *refs):
    for sources, target in ((refs[0:4], refs[8]), (refs[4:8], refs[9])):
        for apart, source in enumerate(sources):
            rows = source.shape[0]
            spot = pl.multiple_of((place_ref[4] ^ apart) * rows, rows)
            target[pl.ds(spot, rows)] = source[...]


def copy_kernel(source, out):
    out[...] = source[...]


def pair_kernel(first, second, out):
    out[0] = first[...]
    out[1] = second[...]


def pick_kernel(place_ref, source, out):
    rows = out.shape[0]
    out[...] = source[pl.ds(pl.multiple_of(place_ref[4] * rows, rows), rows)]


class Behind:
    def __init__(self, array, places, rows):
        self.array, self.places, self.rows = array, places, rows

    def __getitem__(self, place):
        if len(self.array.shape) == 3:
            return self.array[place]
        first = self.array.shape[0] - (self.places - place) * self.rows
        return self.array[first : first + self.rows]


def total_of(arrays, place):
    total = arrays[0][place].astype(F32)
    for array in arrays[1:]:
        total = total + array[place].astype(F32)
    return total


def fold_kernel(*refs):
    arrays, (next_keep, next_send) = refs[:-2], refs[-2:]
    half = next_keep.shape[0]
    arrays = [Behind(array, 2 * half, arrays[0].shape[1]) for array in arrays]
    for place in range(half):
        next_send[place] = total_of(arrays, half + place).astype(LOW)
        next_keep[place] = total_of(arrays, place).astype(LOW)


def sum_kernel(*refs):
    for place in range(refs[-1].shape[0]):
        refs[-1][place] = total_of(refs[:-1], place).astype(LOW)


def split_kernel(keep, got_0, got_1, got_2, got_3, near_0, near_1, far_0, far_1):
    half = got_0.shape[0]
    pieces = ((0, got_0, near_0), (0, got_1, near_1), (1, got_2, far_0), (1, got_3, far_1))
    for number, (part, got, target) in enumerate(pieces):
        for place in range(half):
            first = keep[part, number % 2 * half + place].astype(F32)
            target[place] = (first + got[place].astype(F32)).astype(LOW)


def split_whole_kernel(keep, got_0, got_1, got_2, got_3, near, far):
    half = got_0.shape[0]
    split_kernel(
        keep, got_0, got_1, got_2, got_3,
        near.at[0:half], near.at[half:], far.at[0:half], far.at[half:],
    )


def enc_mlp_share_kernel(keep, got, up_ref, down_ref):
    piece, units = up_ref.shape
    total = total_of((keep, got), 0)
    up_ref[...] = total[:piece, :units]
    down_ref[...] = total[:piece, units:]


def enc_attn_share_kernel(keep, got, qkv_ref, out_ref, *vectors):
    total = total_of((keep, got), 0)
    inner, piece = out_ref.shape
    qkv_ref[...] = total[:piece, : 3 * inner].T
    out_ref[...] = total[:piece, 3 * inner :].T
    for row, vector in zip((10, 8, 9, 1, 0), vectors[:5], strict=True):
        vector[...] = total[total.shape[0] - VEC_ROWS + row, :piece]
    norms = total[total.shape[0] - VEC_ROWS :, :piece]
    vectors[5][...] = jnp.concatenate([norms[11:13], jnp.zeros((6, piece), F32)], 0)


def dec_up_share_kernel(keep, got, up_ref, proj_ref, *vectors):
    total = total_of((keep, got), 0)
    piece, units = up_ref.shape
    enc_piece, column = proj_ref.shape
    up_ref[...] = total[:, :units]
    rest = enc_piece - piece
    ends = total[:, units + column :]
    tail = jnp.concatenate([ends[:rest, : column // 2], ends[rest:, : column // 2]], 1)
    proj_ref[...] = jnp.concatenate([total[:, units : units + column], tail], 0).astype(LOW)
    rows = ends.T
    for row, vector in enumerate(vectors):
        vector[...] = rows[column // 2 + row, :piece]


def dec_down_share_kernel(keep, got, down_ref, qkv_ref, out_ref):
    total = total_of((keep, got), 0)
    units = down_ref.shape[1]
    inner = out_ref.shape[0]
    down_ref[...] = total[:, :units]
    qkv_ref[...] = total[:, units : units + 3 * inner].T
    out_ref[...] = total[:, units + 3 * inner :].T


def norm_add_kernel(first, second, out):
    out[...] = first[...] + second[...]


def norm_share_kernel(first, second, gain_ref, shift_ref):
    total = first[...] + second[...]
    gain_ref[...] = total[0]
    shift_ref[...] = total[1]


def proj_kernel(place_ref, own, core, far, out):
    column = own.shape[1]
    for apart, part in enumerate((own[...], core[...], far[0], far[1])):
        spot = pl.multiple_of((place_ref[0] ^ apart) * column, column)
        out[:, pl.ds(spot, column)] = part.astype(F32)


def decoded_kernel(place_ref, keep, got, far, out):
    chips = keep.shape[1]
    for index in range(chips):
        pieces = (keep[0, index], got[0, index], far[0, index], far[1, index])
        for apart, piece in enumerate(pieces):
            out[(place_ref[0] ^ apart) * chips + index] = piece.astype(F32)


def swap(values, axis, apart):
    size = lax.axis_size(axis)
    return lax.ppermute(values, axis, [(i, i ^ apart) for i in range(size)])


class Chain:
    def __init__(self, line, name, keep, send, steps):
        self.line, self.name, self.keep, self.step = line, name, list(keep), 0
        self.steps = steps
        self.got = self.exchange(send)

    def exchange(self, send):
        return swap(send, "dp", 1 << self.steps[self.step])

    def fold(self):
        half = self.places() // 2
        out = jax.ShapeDtypeStruct((half,) + self.got.shape[1:], LOW)
        self.step += 1
        keep, send = self.line.call(
            fold_kernel, [out, out], [*self.keep, self.got], name="%s_fold_%d" % (self.name, self.step)
        )
        self.keep = [keep]
        self.got = self.exchange(send)

    def places(self):
        return self.got.shape[0]

    def advance(self):
        if self.places() == 1:
            return True
        self.fold()
        return False

    def addends(self):
        return [*self.keep, self.got]


class DecChain(Chain):
    def __init__(self, line, name, near, far, steps):
        self.line, self.name, self.near, self.far, self.step = line, name, near, far, 0
        self.steps, self.got = steps, None

    def advance(self):
        if self.got is not None:
            return super().advance()
        name = self.name + "_first"
        if len(self.near) == 1:
            out = jax.ShapeDtypeStruct((self.near[0].shape[0] // 2,) + self.near[0].shape[1:], LOW)
            keep, send = self.line.call(fold_kernel, [out, out], [self.near[0], self.far[0]], name=name)
            self.keep = [keep]
        else:
            out = jax.ShapeDtypeStruct(self.near[1].shape, LOW)
            send = self.line.call(sum_kernel, [out], [self.near[1], self.far[1]], name=name)[0]
            self.keep = [self.near[0], self.far[0]]
        self.got = self.exchange(send)
        return False


def body(
    band_patches,
    band_counts,
    visible_index,
    enc_attn_gain,
    enc_attn_shift,
    enc_qkv_weight,
    enc_out_weight,
    enc_out_bias,
    enc_mlp_gain,
    enc_mlp_shift,
    enc_up_weight,
    enc_up_bias,
    enc_down_weight,
    enc_down_bias,
    proj_weight,
    proj_bias,
    mask_token,
    dec_attn_gain,
    dec_attn_shift,
    dec_qkv_weight,
    dec_out_weight,
    dec_out_bias,
    dec_mlp_gain,
    dec_mlp_shift,
    dec_up_weight,
    dec_up_bias,
    dec_down_weight,
    dec_down_bias,
    cotangent,
):
    parts = lax.axis_size("tensor")
    blocks = lax.axis_size("dp")
    rank = lax.axis_index("tensor")
    number = lax.axis_index("dp")
    place = jnp.stack(
        [rank, *(place_of(number, blocks, kind) for kind in KINDS), number % 4]
    ).astype(jnp.int32)
    chips, length = visible_index.shape
    band_total, own_patches = band_patches.shape[1:3]
    own_chips = chips // parts
    enc_width = band_patches.shape[3]
    patches, dec_width = cotangent.shape[1:]
    enc_inner = enc_out_weight.shape[0]
    enc_units = enc_up_weight.shape[1]
    dec_units = dec_up_weight.shape[1]
    dec_inner = dec_out_weight.shape[0]
    dec_kinds = 3 * dec_inner
    rows = chips * length
    shape = jax.ShapeDtypeStruct
    half_rows = shape((rows // 2, enc_width), LOW)
    quarter_rows = shape((rows // 4, enc_width), LOW)
    all_rows = shape((rows, enc_width), LOW)
    wide_rows = shape((rows, enc_width), F32)
    hidden_shape = shape((rows, enc_units), LOW)
    vec_shape = shape((8, enc_width), F32)
    part_shapes = [half_rows, quarter_rows, quarter_rows]

    line = Line()
    call = line.call

    def core(values):
        return swap(values, "tensor", 1)

    def add_cores(parts, name, after=()):
        keep, *sends = parts
        return call(add_kernel, [half_rows], [keep, *map(core, sends)], after=after, name=name)[0]

    def cross(own, name, after=()):
        pair = call(
            add_crossed_kernel, [quarter_rows] * 2, [own, swap(own, "tensor", 2)], after=after, name=name
        )
        return [*pair, *map(core, pair)]

    w_own = jnp.concatenate(
        [
            dec_qkv_weight.reshape(dec_kinds, dec_width),
            dec_out_weight,
            dec_up_weight,
            dec_down_weight,
        ],
        0,
    )
    angles = lax.broadcasted_iota(F32, (patches, dec_width // 2), 0) * jnp.exp(
        lax.broadcasted_iota(F32, (patches, dec_width // 2), 1)
        * (-math.log(10000.0) / (dec_width // 2))
    )
    position = jnp.concatenate([jnp.sin(angles), jnp.cos(angles)], 1)
    own_visible = lax.dynamic_slice_in_dim(visible_index, rank * own_chips, own_chips, 0)
    own_cotangent = lax.dynamic_slice_in_dim(cotangent, rank * own_chips, own_chips, 0)
    own_cotangent = own_cotangent.reshape(-1, dec_width)
    parts_here = call(
        functools.partial(band_mean_kernel, own_chips=own_chips),
        part_shapes,
        [band_patches, visible_index],
        scalars=[place, band_counts],
        after=[],
        name="band_mean",
    )
    own = add_cores(parts_here, "enc_add_tokens")
    tok = cross(own, "enc_cross_tokens")

    w_core = core(w_own)
    w_rows = w_own.shape[0] // 4
    w_pick = call(
        pick_kernel, [shape((w_rows, dec_width), LOW)], [w_own], scalars=[place], name="enc_pick"
    )[0]
    w_fourths = [swap(w_pick, "tensor", 2)]
    w_fourths.append(swap(w_fourths[0], "dp", 1))
    w_fourths.append(swap(w_fourths[0], "dp", 2))
    w_fourths.append(swap(w_fourths[2], "dp", 1))

    qkv_w = enc_qkv_weight.reshape(3 * enc_inner, enc_width)
    *parts_here, enc_n1, enc_qkv, enc_mixed, enc_probs = call(
        functools.partial(enc_attn_kernel, length=length),
        part_shapes
        + [
            all_rows, shape((rows, 3 * enc_inner), LOW), shape((rows, enc_inner), LOW),
            shape((enc_inner // HEAD, rows, 2 * length), F32),
        ],
        [*tok, enc_attn_gain, enc_attn_shift, qkv_w, enc_out_weight],
        after=[position, own_cotangent, own_visible],
        name="enc_attn",
    )
    own = add_cores(parts_here, "enc_add_attn", [w_fourths[0]])
    sums = cross(own, "enc_cross_attn", [w_fourths[1], w_fourths[2]])
    *parts_here, enc_n2, enc_act, enc_slope = call(
        enc_mlp_kernel,
        [quarter_rows] * 4 + [all_rows, hidden_shape, hidden_shape],
        [
            *tok, *sums, enc_out_bias, enc_mlp_gain, enc_mlp_shift,
            enc_up_weight, enc_up_bias, enc_down_weight,
        ],
        name="enc_mlp",
    )
    far, near, early = call(
        add_two_kernel,
        [quarter_rows] * 2 + [all_rows],
        [parts_here[1], core(parts_here[3]), parts_here[0], core(parts_here[2]), enc_n2],
        name="enc_add_mlp",
    )
    early = swap(early, "dp", 2)
    w_x, w_diag = call(
        assemble_kernel,
        [shape(w_own.shape, LOW)] * 2,
        [*w_fourths, *map(core, w_fourths)],
        scalars=[place],
        name="enc_assemble",
    )
    enc_low = call(
        enc_out_kernel,
        [quarter_rows],
        [tok[0], sums[0], enc_out_bias, near, swap(far, "tensor", 2), enc_down_bias],
        name="enc_out",
    )[0]

    dec_rows = own_chips * patches
    dec_all = shape((dec_rows, dec_width), LOW)
    dec_hidden = shape((parts, dec_rows, dec_units), LOW)
    dec_column = shape((parts // 2, own_chips, patches, dec_width // parts), LOW)
    (
        decoded_keep, decoded_send, grad_latent, dec_n1, dec_n2, dec_gml, dec_act, dec_hid,
        dec_gqkv, dec_mixed, dec_vec, dec_upvec,
    ) = call(
        dec_kernel,
        [
            dec_column, dec_column, shape((own_chips * length, dec_width), LOW), dec_all, dec_all,
            dec_all, dec_hidden, dec_hidden, shape((parts, dec_rows, 3 * HEAD), LOW),
            shape((parts, dec_rows, HEAD), LOW), shape((8, dec_width), F32), shape((8, dec_units), F32),
        ],
        [
            enc_low, proj_weight, proj_bias, mask_token, position, own_visible, dec_attn_gain,
            dec_attn_shift, dec_out_bias, dec_mlp_gain, dec_mlp_shift, dec_down_bias, dec_up_bias,
            w_own, w_core, w_x, w_diag, own_cotangent,
        ],
        scalars=[place],
        name="decoder",
        vmem=DEC_VMEM_BYTES,
        scratch=[
            pltpu.VMEM((parts, dec_rows, dec_units), LOW),
            pltpu.VMEM((parts, dec_rows, patches), F32),
            pltpu.VMEM((parts, dec_rows, 3 * HEAD), LOW),
        ],
    )
    lat_far = swap(grad_latent, "tensor", 2)
    decoded_got = core(decoded_send)
    decoded_far = swap(jnp.stack([decoded_keep[1], decoded_got[1]]), "tensor", 2)
    dec_piece = dec_width // blocks
    enc_piece = enc_width // blocks
    enc_rows = -(-enc_piece // 16) * 16
    proj_own = dec_width // parts
    enc_vector = shape((enc_piece,), F32)
    dec_vector = shape((dec_piece,), F32)
    have = {}

    def dec_bundle(kernel, name, columns, args):
        sends = [shape((blocks // 2, dec_piece, columns), LOW)] * 4
        keep, *sends = call(
            kernel, [shape((2, blocks, dec_piece, columns), LOW)] + sends, args, scalars=[place], name=name
        )
        have[name] = [keep, *map(core, sends)]

    def dec_up():
        args = [dec_n2, dec_hid, enc_low, grad_latent, dec_vec, dec_upvec]
        dec_bundle(dec_up_kernel, "dec_up", dec_units + 2 * proj_own, args)

    def dec_down():
        args = [own_cotangent, dec_act, dec_n1, dec_gqkv, dec_gml, dec_mixed]
        dec_bundle(dec_down_kernel, "dec_down", dec_units + 4 * dec_inner, args)

    def split(name, steps):
        out = shape((blocks // 2,) + have[name][0].shape[2:], LOW)
        *near, far_0, far_1 = call(split_kernel, [out] * 4, have[name], name=name + "_split")
        far_1 = swap(far_1, "tensor", 2)
        have[name] = DecChain(line, name, near, [far_0, far_1], steps)

    def split_whole(name, steps):
        out = shape(have[name][0].shape[1:], LOW)
        near, far = call(split_whole_kernel, [out] * 2, have[name], name=name + "_split")
        have[name] = DecChain(line, name, [near], [swap(far, "tensor", 2)], steps)

    def pair():
        have["lat"] = call(
            pair_kernel, [shape((2,) + grad_latent.shape, LOW)], [grad_latent, lat_far], name="enc_pair"
        )[0]
        have["lat_core"] = core(have["lat"])
        have["lat_z"] = swap(have["lat"], "dp", 2)

    def lat_core():
        have["lat_z"] = call(copy_kernel, [have["lat"]], [have["lat_z"]], name="enc_lat")[0]
        have["lat_z_core"] = core(have["lat_z"])

    def mlp_back():
        *have["parts"], have["out_grad"], have["gol"], have["hid"], have["vec_mlp"] = call(
            enc_mlp_back_kernel,
            part_shapes + [wide_rows, all_rows, hidden_shape, vec_shape],
            [have["lat"], have["lat_core"], proj_weight, enc_slope, enc_up_weight, enc_down_weight],
            name="enc_mlp_back",
        )

    def add_back():
        have["own"] = add_cores(have["parts"], "enc_add_back")

    def cross_back():
        have["backs"] = cross(have["own"], "enc_cross_back")

    def mlp_early():
        have["early"] = call(
            enc_mlp_early_kernel,
            [hidden_shape] * 2,
            [early, enc_up_weight, enc_up_bias],
            name="enc_mlp_early",
        )

    def mlp_weights():
        bundle = shape((blocks // 4, enc_rows, 2 * enc_units), LOW)
        keep, send = call(
            enc_mlp_weights_kernel,
            [bundle] * 2,
            [
                enc_n2, have["hid"], have["gol"], enc_act, early, *have["early"],
                have["lat_z"], have["lat_z_core"],
                proj_weight, enc_down_weight,
            ],
            scalars=[place],
            name="enc_mlp_weights",
        )
        have["mlp"] = Chain(line, "enc_mlp", [keep], send, steps_of(blocks, "paired"))

    def attn_back():
        *have["parts"], have["mid"], have["gml"], have["gqkv"], have["vec_attn"] = call(
            functools.partial(enc_attn_back_kernel, length=length),
            part_shapes + [wide_rows, all_rows, shape((rows, 3 * enc_inner), LOW), vec_shape],
            [
                *tok, *sums, *have["backs"], enc_out_bias, enc_mlp_gain, have["out_grad"], enc_qkv, qkv_w,
                enc_out_weight, enc_probs,
            ],
            name="enc_attn_back",
        )

    def attn_weights():
        bundle = shape((blocks // 2, enc_rows + VEC_ROWS, 4 * enc_inner), LOW)
        keep, send = call(
            enc_attn_weights_kernel,
            [bundle, bundle],
            [enc_n1, have["gqkv"], have["gml"], enc_mixed, have["vec_mlp"], have["vec_attn"]],
            scalars=[place],
            name="enc_attn_weights",
        )
        have["attn"] = Chain(line, "enc_attn", [keep], send, steps_of(blocks, ATTN))

    def add_grad():
        keep, *sends = have["parts"]
        chain = have["dec_down"]
        if DOWN_HALVES:
            rest = chain.far[0].reshape(-1, enc_width)
            own = call(
                add_with_kernel, [shape((rows // 2 + rest.shape[0], enc_width), LOW)],
                [keep, *map(core, sends), rest], name="enc_add_grad",
            )[0]
            have["own"], far = own, swap(own, "tensor", 2)
            chain.far[0] = far
            have["far"] = far
        else:
            own = call(add_kernel, [half_rows], [keep, *map(core, sends)], name="enc_add_grad")[0]
            have["own"], have["far"] = own, swap(own, "tensor", 2)

    def cross_grad():
        halves = call(
            add_crossed_kernel, [quarter_rows] * 2, [have["own"], have["far"]], name="enc_cross_grad"
        )
        have["grads"] = [*halves, *map(core, halves)]

    def band_grads():
        have["band_grad"] = call(
            functools.partial(band_grad_kernel, own_chips=own_chips),
            [InHbm(shape(band_patches.shape, F32))],
            [*tok, *have["grads"], have["mid"], enc_attn_gain, visible_index],
            scalars=[place, band_counts],
            name="band_grad",
            scratch=[
                pltpu.VMEM((chips + 1, own_patches, enc_width), F32),
                pltpu.SemaphoreType.DMA((chips, band_total)),
            ],
        )[0]

    def mlp():
        if have["mlp"].advance():
            have["mlp"] = call(
                enc_mlp_share_kernel,
                [shape((enc_piece, enc_units), F32)] * 2,
                have["mlp"].addends(),
                name="enc_mlp_share",
            )

    def attn():
        if have["attn"].advance():
            have["attn"] = call(
                enc_attn_share_kernel,
                [shape((3 * enc_inner, enc_piece), F32), shape((enc_inner, enc_piece), F32)]
                + [enc_vector] * 5
                + [shape((8, enc_piece), F32)],
                have["attn"].addends(),
                name="enc_attn_share",
            )
            have["norm_core"] = core(have["attn"][-1])

    def up():
        if have["dec_up"].advance():
            have["dec_up"] = call(
                dec_up_share_kernel,
                [shape((dec_piece, dec_units), F32), shape((enc_piece, proj_own), LOW)] + [dec_vector] * 9,
                have["dec_up"].addends(),
                name="dec_up_share",
            )
            have["proj_core"] = core(have["dec_up"][1])

    def down():
        if have["dec_down"].advance():
            have["dec_down"] = call(
                dec_down_share_kernel,
                [
                    shape((dec_piece, dec_units), F32),
                    shape((dec_kinds, dec_piece), F32),
                    shape((dec_inner, dec_piece), F32),
                ],
                have["dec_down"].addends(),
                name="dec_down_share",
            )

    def finish():
        for name, step in (("mlp", mlp), ("attn", attn), ("dec_up", up), ("dec_down", down)):
            while isinstance(have[name], Chain):
                step()

    def norm_add():
        own_norm = have["attn"][-1]
        have["norm"] = call(
            norm_add_kernel, [shape((8, enc_piece), F32)], [own_norm, have["norm_core"]], name="enc_norm_add"
        )[0]
        have["norm_far"] = swap(have["norm"], "tensor", 2)

    def norm_share():
        have["norm_grads"] = call(
            norm_share_kernel, [enc_vector] * 2, [have["norm"], have["norm_far"]], name="enc_norm_share"
        )

    def proj_far():
        have["proj_far"] = swap(jnp.stack([have["dec_up"][1], have["proj_core"]]), "tensor", 2)

    def proj_share():
        have["proj_grad"] = call(
            proj_kernel,
            [shape((enc_piece, dec_width), F32)],
            [have["dec_up"][1], have["proj_core"], have["proj_far"]],
            scalars=[place],
            name="dec_proj_share",
        )[0]

    def decoded_share():
        have["decoded"] = call(
            decoded_kernel,
            [shape((chips, patches, dec_width // parts), F32)],
            [decoded_keep, decoded_got, decoded_far],
            scalars=[place],
            name="decoded_share",
        )[0]

    steps = {
        "dec_up": dec_up,
        "dec_down": dec_down,
        "up_split": lambda: (split if UP_HALVES else split_whole)("dec_up", steps_of(blocks, UP)),
        "down_split": lambda: (split if DOWN_HALVES else split_whole)("dec_down", steps_of(blocks, DOWN)),
    }
    for step in (
        pair, lat_core, mlp_back, add_back, cross_back, mlp_early, mlp_weights, attn_back, attn_weights, add_grad, cross_grad,
        band_grads, mlp, attn, up, down, finish, norm_add, norm_share, proj_far, proj_share, decoded_share,
    ):
        steps[step.__name__] = step
    for name in ORDER:
        steps[name]()
    decoded, band_grad, norm_grads = have["decoded"], have["band_grad"], have["norm_grads"]
    enc_up_grad, enc_down_grad = have["mlp"]
    enc_qkv_grad, enc_out_grad, *enc_vecs = have["attn"]
    dec_up_grad, _, *dec_vecs = have["dec_up"]
    dec_down_grad, dec_qkv_grad, dec_out_grad = have["dec_down"]
    proj_grad = have["proj_grad"]
    return (
        decoded,
        band_grad,
        *norm_grads,
        enc_qkv_grad.reshape(3, enc_inner, enc_piece),
        enc_out_grad,
        enc_vecs[0],
        enc_vecs[1],
        enc_vecs[2],
        enc_up_grad,
        enc_vecs[3],
        enc_down_grad.T,
        enc_vecs[4],
        proj_grad,
        dec_vecs[6],
        dec_vecs[7],
        dec_vecs[0],
        dec_vecs[1],
        dec_qkv_grad.reshape(3, dec_inner, dec_piece),
        dec_out_grad,
        dec_vecs[2],
        dec_vecs[3],
        dec_vecs[4],
        dec_up_grad,
        dec_vecs[8],
        dec_down_grad.T,
        dec_vecs[5],
    )


def solution(mesh):
    in_specs = (
        P("dp", None, "tensor", None),
        P("dp"),
        P("dp", None),
        P(),
        P(),
        P(None, "tensor", None),
        P("tensor", None),
        P(),
        P(),
        P(),
        P(None, "tensor"),
        P("tensor"),
        P("tensor", None),
        P(),
        P(),
        P(),
        P(),
        P(),
        P(),
        P(None, "tensor", None),
        P("tensor", None),
        P(),
        P(),
        P(),
        P(None, "tensor"),
        P(),
        P("tensor", None),
        P(),
        P("dp", None, None),
    )
    out_specs = (
        P("dp", None, "tensor"),
        P("dp", None, "tensor", None),
        P("dp"),
        P("dp"),
        P(None, "tensor", "dp"),
        P("tensor", "dp"),
        P("dp"),
        P("dp"),
        P("dp"),
        P("dp", "tensor"),
        P(("tensor", "dp")),
        P("tensor", "dp"),
        P("dp"),
        P("dp", None),
        P("dp"),
        P("dp"),
        P("dp"),
        P("dp"),
        P(None, "tensor", "dp"),
        P("tensor", "dp"),
        P("dp"),
        P("dp"),
        P("dp"),
        P("dp", "tensor"),
        P(("tensor", "dp")),
        P("tensor", "dp"),
        P("dp"),
    )
    return jax.shard_map(body, mesh=mesh, in_specs=in_specs, out_specs=out_specs, check_vma=False)
```

```python
import functools
import math
import types

import jax
import jax.numpy as jnp
from jax import lax
from jax.experimental import pallas as pl
from jax.experimental.pallas import tpu as pltpu
from jax.sharding import PartitionSpec as P

HEAD = 64
EPSILON = 1e-05
SCALE = HEAD ** (-0.5)
VMEM_BYTES = 30 * 1024 * 1024
F32 = jnp.float32
LOW = jnp.bfloat16
NN = (((1,), (0,)), ((), ()))
NT = (((1,), (1,)), ((), ()))
TN = (((0,), (0,)), ((), ()))
VEC_ROWS = 16
DP, TENSOR = "dp", "tensor"
Y, Z, PAIRED = range(3)
ATTN, UP, DOWN = Y, Z, Y


def dot(left, right, dims=NN):
    return lax.dot_general(left, right, dims, preferred_element_type=F32)


def col_sum(values):
    return jnp.sum(values, 0, keepdims=True)


def vec(ref):
    return ref[...][None, :]


def norm_parts(stream):
    center = stream - jnp.mean(stream, -1, keepdims=True)
    inverse = lax.rsqrt(jnp.mean(center * center, -1, keepdims=True) + EPSILON)
    return center * inverse, inverse


def norm_back(grad, xhat, inverse, gain):
    scaled = grad * gain
    mean_q = jnp.mean(scaled, -1, keepdims=True)
    mean_qx = jnp.mean(scaled * xhat, -1, keepdims=True)
    return inverse * (scaled - mean_q - xhat * mean_qx)


def gelu_parts(hidden):
    phi = 0.5 + 0.5 * lax.erf(hidden * (0.5**0.5))
    density = jnp.exp(hidden * hidden * -0.5) * (1.0 / math.sqrt(2.0 * math.pi))
    return hidden * phi, phi + hidden * density


def softmax_rows(scores):
    weights = jnp.exp(scores - jnp.max(scores, -1, keepdims=True))
    return weights * (1.0 / jnp.sum(weights, -1, keepdims=True))


def same_chip(rows, length):
    first = lax.broadcasted_iota(jnp.int32, (rows, rows), 0) // length
    second = lax.broadcasted_iota(jnp.int32, (rows, rows), 1) // length
    return first == second


def attend(queries, keyset, mask):
    scores = dot(queries, keyset, NT) * SCALE
    if mask is not None:
        scores = jnp.where(mask, scores, -1e30)
    return softmax_rows(scores)


def attend_back(probs, queries, keyset, valset, grad_mixed):
    grad_probs = dot(grad_mixed, valset, NT)
    grad_values = dot(probs.astype(LOW), grad_mixed, TN)
    grad_scores = probs * (grad_probs - jnp.sum(grad_probs * probs, -1, keepdims=True))
    score_low = grad_scores.astype(LOW)
    grad_queries = dot(score_low, keyset) * SCALE
    grad_keys = dot(score_low, queries, TN) * SCALE
    return grad_queries.astype(LOW), grad_keys.astype(LOW), grad_values.astype(LOW)


class Line:
    def __init__(self):
        self.token = None

    def call(self, body, out_shape, args, scalars=(), after=(), scratch=(), in_place=False, vmem=VMEM_BYTES):
        after = list(after) + ([] if self.token is None else [self.token])
        specs = [pl.BlockSpec(memory_space=pltpu.SMEM) for _ in scalars]
        for arg in args:
            specs.append(pl.BlockSpec(memory_space=pltpu.HBM if isinstance(arg, InHbm) else pltpu.VMEM))
        args = [arg.array if isinstance(arg, InHbm) else arg for arg in args]
        specs += [pl.BlockSpec(memory_space=pl.ANY) for _ in after]
        inputs = len(scalars) + len(args)
        outputs = len(out_shape)
        out_specs = []
        for out in out_shape:
            in_hbm = isinstance(out, InHbm)
            out_specs.append(pl.BlockSpec(memory_space=pltpu.HBM if in_hbm else pltpu.VMEM))
        out_shape = [out.array if isinstance(out, InHbm) else out for out in out_shape]
        out_shape = [jax.ShapeDtypeStruct(out.shape, out.dtype) for out in out_shape]

        def wrapped(*refs):
            outs = refs[inputs + len(after) :]
            outs[outputs][...] = jnp.zeros_like(outs[outputs])
            body(*refs[:inputs], *outs[:outputs], *outs[outputs + 1 :])

        *found, self.token = pl.pallas_call(
            wrapped,
            out_shape=out_shape + [jax.ShapeDtypeStruct((8, 128), F32)],
            in_specs=specs,
            out_specs=out_specs + [pl.BlockSpec(memory_space=pltpu.VMEM)],
            scratch_shapes=list(scratch),
            input_output_aliases={inputs - 1: 0} if in_place else {},
            compiler_params=pltpu.CompilerParams(vmem_limit_bytes=vmem),
            cost_estimate=pl.CostEstimate(flops=1, bytes_accessed=1, transcendentals=0),
            name=(body.func if isinstance(body, functools.partial) else body).__name__,
        )(*scalars, *args, *after)
        return found


class InHbm:
    def __init__(self, array):
        self.array = array


def steps_of(blocks, kind):
    steps = list(range(blocks.bit_length() - 1))
    if kind == Z:
        steps[:2] = [1, 0]
    if kind == PAIRED:
        steps.remove(1)
    return steps


def place_of(value, blocks, kind):
    steps = steps_of(blocks, kind)
    result = 0
    for place, bit in enumerate(steps):
        result = result | (((value >> bit) & 1) << (len(steps) - 1 - place))
    return result


def spot_of(place_ref, block, blocks, kind):
    return place_ref[1 + kind] ^ place_of(block, blocks, kind)


def put_block(keep, send, lead, place, half, rows, columns, values):
    @pl.when(place < half)
    def _():
        keep[lead + (place, rows, columns)] = values

    @pl.when(place >= half)
    def _():
        send[lead + (place - half, rows, columns)] = values


def chip_of(step, rank, own_chips):
    part, index = step // own_chips, step % own_chips
    apart = 2 * (part % 2) + part // 2
    return (rank ^ apart) * own_chips + index


def put_rows(parts, first, values):
    for part in parts:
        if first < part.shape[0]:
            part[first : first + values.shape[0]] = values
            return
        first -= part.shape[0]


def get_rows(parts, first, count):
    found = []
    for part in parts:
        size = part.shape[0]
        if first < size and count > 0:
            taken = min(count, size - first)
            found.append(part[first : first + taken])
            count -= taken
            first = size
        first -= size
    return found[0] if len(found) == 1 else jnp.concatenate(found, 0)


def band_mean_kernel(place_ref, count_ref, all_ref, visible_ref, *parts, own_chips):
    *parts, bands_ref, arrived = parts
    rank = place_ref[0]
    chips, bands, own, width = bands_ref.shape
    copies = []
    for step in range(chips):
        spot = chip_of(step, rank, own_chips)
        copies.append(pltpu.make_async_copy(all_ref.at[spot], bands_ref.at[step], arrived.at[step]))
        copies[-1].start()
    length = visible_ref.shape[1]
    patch = lax.broadcasted_iota(jnp.int32, (own, length), 0) + rank * own
    for step in range(chips):
        spot = chip_of(step, rank, own_chips)
        count = count_ref[spot]
        copies[step].wait()
        means = []
        for first in range(0, own, 16):
            span = slice(first, first + 16)
            total = bands_ref[step, 0, span].astype(F32)
            for band in range(1, bands):
                used = jnp.where(band < count, 1.0, 0.0).astype(F32)
                total = total + bands_ref[step, band, span].astype(F32) * used
            means.append((total / count.astype(F32)).astype(LOW))
        chosen = visible_ref[pl.ds(spot, 1)] == patch
        chosen = jnp.where(chosen, 1.0, 0.0).astype(LOW)
        values = dot(chosen, jnp.concatenate(means, 0), TN).astype(LOW)
        put_rows(parts, step * length, values)


def enc_attn_kernel(*refs, length):
    tok, (gain, shift, qkv_w, out_w) = refs[:4], refs[4:8]
    parts, (normed_ref, qkv_ref, mixed_ref, prob_ref) = refs[8:11], refs[11:]
    rows = normed_ref.shape[0] // 2
    inner = out_w.shape[0]
    block = 2 * length
    mask = same_chip(block, length)
    for group in range(2):
        span = slice(group * rows, (group + 1) * rows)
        xhat, _ = norm_parts(get_rows(tok, group * rows, rows).astype(F32))
        normed = (xhat * vec(gain) + vec(shift)).astype(LOW)
        normed_ref[span] = normed
        qkv = dot(normed, qkv_w[...], NT).astype(LOW)
        qkv_ref[span] = qkv
        blocks = []
        for first in range(0, rows, block):
            heads = []
            for head in range(inner // HEAD):
                at = [
                    qkv[first : first + block, k * inner + head * HEAD : k * inner + (head + 1) * HEAD]
                    for k in range(3)
                ]
                probs = attend(at[0], at[1], mask)
                prob_ref[head, group * rows + first : group * rows + first + block] = probs
                heads.append(dot(probs.astype(LOW), at[2]).astype(LOW))
            blocks.append(jnp.concatenate(heads, 1))
        mixed = jnp.concatenate(blocks, 0)
        mixed_ref[span] = mixed
        part = dot(mixed, out_w[...]).astype(LOW)
        for first in range(0, rows, block):
            put_rows(parts, group * rows + first, part[first : first + block])


def own_columns(values, which, blocks):
    piece = values.shape[1] // blocks
    kinds = []
    for bit in range(2):
        starts = [(4 * run + 2 * bit) * piece for run in range(blocks // 4)]
        kinds.append(jnp.concatenate([values[:, start : start + 2 * piece] for start in starts], 1))
    return jnp.where(which == 0, kinds[0], kinds[1])


def enc_mlp_kernel(*refs):
    tok, sums = refs[:4], refs[4:8]
    out_bias, gain, shift, up_w, up_bias, down_w = refs[8:14]
    parts, (normed_ref, act_ref, slope_ref) = refs[14:18], refs[18:]
    rows = normed_ref.shape[0] // 2
    block = rows // 2
    for group in range(2):
        span = slice(group * rows, (group + 1) * rows)
        middle = get_rows(tok, group * rows, rows).astype(F32) + vec(out_bias)
        middle = middle + get_rows(sums, group * rows, rows).astype(F32)
        xhat, _ = norm_parts(middle)
        normed = (xhat * vec(gain) + vec(shift)).astype(LOW)
        normed_ref[span] = normed
        activation, slope = gelu_parts(dot(normed, up_w[...]) + vec(up_bias))
        act_low, slope_low = activation.astype(LOW), slope.astype(LOW)
        act_ref[span] = act_low
        slope_ref[span] = slope_low
        part = dot(act_low, down_w[...]).astype(LOW)
        for first in range(0, rows, block):
            put_rows(parts, group * rows + first, part[first : first + block])


def enc_out_kernel(tok, total, out_bias, own, other, down_bias, low_ref):
    low_ref[...] = (
        tok[...].astype(F32)
        + total[...].astype(F32)
        + vec(out_bias)
        + own[...].astype(F32)
        + other[...].astype(F32)
        + vec(down_bias)
    ).astype(LOW)


def enc_mlp_back_kernel(lat_pair, lat_core, proj_w, slope_ref, up_w, down_w, *refs):
    lat = (lat_pair.at[0], lat_pair.at[1], lat_core.at[0], lat_core.at[1])
    parts, (out_ref, low_ref, hidden_ref, vec_ref) = refs[:3], refs[3:]
    rows = out_ref.shape[0] // 2
    block = rows // 2
    down_sum, up_sum = 0.0, 0.0
    for group in range(2):
        span = slice(group * rows, (group + 1) * rows)
        grad_out = dot(get_rows(lat, group * rows, rows), proj_w[...], NT)
        out_ref[span] = grad_out
        grad_low = grad_out.astype(LOW)
        low_ref[span] = grad_low
        grad_hidden = dot(grad_low, down_w[...], NT) * slope_ref[span].astype(F32)
        hidden_low = grad_hidden.astype(LOW)
        hidden_ref[span] = hidden_low
        down_sum = down_sum + col_sum(grad_out)
        up_sum = up_sum + col_sum(grad_hidden)
        part = dot(hidden_low, up_w[...], NT).astype(LOW)
        for first in range(0, rows, block):
            put_rows(parts, group * rows + first, part[first : first + block])
    vec_ref[...] = jnp.concatenate(
        [down_sum, up_sum, jnp.zeros((vec_ref.shape[0] - 2, down_sum.shape[1]), F32)], 0
    )


def enc_mlp_early_kernel(early_ref, up_w, up_bias, act_ref, slope_ref):
    activation, slope = gelu_parts(dot(early_ref[...], up_w[...]) + vec(up_bias))
    act_ref[...] = activation.astype(LOW)
    slope_ref[...] = slope.astype(LOW)


def enc_mlp_weights_kernel(
    place_ref, normed_ref, hidden_ref, low_ref, act_ref, early_ref, early_act, early_slope, lat_pair, lat_core,
    proj_w, down_w, keep, send
):
    half = keep.shape[0]
    blocks = 4 * half
    width, units = normed_ref.shape[1], hidden_ref.shape[1]
    piece = width // blocks
    which = place_ref[4] // 2
    lat = jnp.concatenate([lat_pair[0], lat_pair[1], lat_core[0], lat_core[1]], 0)
    low = dot(lat, proj_w[...], NT).astype(LOW)
    hidden = (dot(low, down_w[...], NT) * early_slope[...].astype(F32)).astype(LOW)
    for kind in range(2):
        if kind == 0:
            found = dot(own_columns(normed_ref[...], which, blocks), hidden_ref[...], TN)
            found = found + dot(own_columns(early_ref[...], which, blocks), hidden, TN)
        else:
            found = dot(own_columns(low_ref[...], which, blocks), act_ref[...], TN)
            found = found + dot(own_columns(low, which, blocks), early_act[...], TN)
        columns = slice(kind * units, (kind + 1) * units)
        for block in range(blocks // 2):
            values = found[block * piece : (block + 1) * piece].astype(LOW)
            place = spot_of(place_ref, 4 * (block // 2) + block % 2, blocks, PAIRED)
            put_block(keep, send, (), place, half, slice(0, piece), columns, values)


def enc_attn_back_kernel(*refs, length):
    tok, sums, backs = refs[:4], refs[4:8], refs[8:12]
    out_bias, mlp_gain, out_ref, qkv_ref, qkv_w, out_w, prob_ref = refs[12:19]
    parts, (mid_ref, low_ref, grad_qkv_ref, vec_ref) = refs[19:22], refs[22:]
    rows = out_ref.shape[0] // 2
    inner = out_w.shape[0]
    block = 2 * length
    found = [0.0] * 5
    for group in range(2):
        span = slice(group * rows, (group + 1) * rows)
        stream = get_rows(tok, group * rows, rows).astype(F32)
        total = get_rows(sums, group * rows, rows).astype(F32)
        xhat, inverse = norm_parts(stream + total + vec(out_bias))
        grad = get_rows(backs, group * rows, rows).astype(F32)
        found[0] = found[0] + col_sum(grad * xhat)
        found[1] = found[1] + col_sum(grad)
        grad_middle = out_ref[span] + norm_back(grad, xhat, inverse, vec(mlp_gain))
        mid_ref[span] = grad_middle
        found[2] = found[2] + col_sum(grad_middle)
        middle_low = grad_middle.astype(LOW)
        low_ref[span] = middle_low
        grad_mixed = dot(middle_low, out_w[...], NT).astype(LOW)
        blocks = []
        for first in range(0, rows, block):
            near = slice(group * rows + first, group * rows + first + block)
            grads = ([], [], [])
            for head in range(inner // HEAD):
                at = [
                    qkv_ref[near, k * inner + head * HEAD : k * inner + (head + 1) * HEAD]
                    for k in range(3)
                ]
                own = grad_mixed[first : first + block, head * HEAD : (head + 1) * HEAD]
                for kind, values in enumerate(attend_back(prob_ref[head, near], *at, own)):
                    grads[kind].append(values)
            blocks.append(jnp.concatenate(grads[0] + grads[1] + grads[2], 1))
        grad_qkv = jnp.concatenate(blocks, 0)
        grad_qkv_ref[span] = grad_qkv
        partial = dot(grad_qkv, qkv_w[...])
        part = partial.astype(LOW)
        for first in range(0, rows, block):
            put_rows(parts, group * rows + first, part[first : first + block])
        xhat, _ = norm_parts(stream)
        found[3] = found[3] + col_sum(partial * xhat)
        found[4] = found[4] + col_sum(partial)
    vec_ref[...] = jnp.concatenate(
        found + [jnp.zeros((vec_ref.shape[0] - 5, found[0].shape[1]), F32)], 0
    )


def enc_attn_weights_kernel(
    place_ref, normed_ref, grad_qkv_ref, low_ref, mixed_ref, vec_mlp, vec_attn, keep, send
):
    half = keep.shape[0]
    blocks = 2 * half
    width = normed_ref.shape[1]
    qkv = dot(normed_ref[...], grad_qkv_ref[...], TN)
    out = dot(low_ref[...], mixed_ref[...], TN)
    vectors = jnp.concatenate([vec_mlp[...], vec_attn[...]], 0)
    piece = width // blocks
    first = keep.shape[1] - VEC_ROWS
    for block in range(blocks):
        at = slice(block * piece, (block + 1) * piece)
        place = spot_of(place_ref, block, blocks, ATTN)
        values = jnp.concatenate([qkv[at], out[at]], 1).astype(LOW)
        put_block(keep, send, (), place, half, slice(0, piece), slice(None), values)
        put_block(
            keep, send, (), place, half, slice(first, first + VEC_ROWS), slice(0, piece),
            vectors[:, at].astype(LOW),
        )


def band_zero_kernel(place_ref, count_ref, out_ref, blank, left, *, own_chips):
    chips, bands = out_ref.shape[:2]
    blank[...] = jnp.zeros_like(blank)
    spots = [chip_of(step, place_ref[0], own_chips) for step in range(chips)]

    def copy_of(step, band):
        return pltpu.make_async_copy(blank, out_ref.at[spots[step], band], left.at[step, band])

    for step in range(chips):

        def begin(band, carry, step=step):
            copy_of(step, band).start()
            return carry

        lax.fori_loop(count_ref[spots[step]], bands, begin, 0)
    for step in range(chips):

        def finish(band, carry, step=step):
            copy_of(step, band).wait()
            return carry

        lax.fori_loop(count_ref[spots[step]], bands, finish, 0)


def band_grad_kernel(place_ref, count_ref, *refs, own_chips):
    tok, backs, (mid_ref, gain, visible_ref, _) = refs[:4], refs[4:8], refs[8:12]
    out_ref, stage, left = refs[12:]
    rank = place_ref[0]
    chips, bands, own, width = out_ref.shape
    length = visible_ref.shape[1]
    spots = [chip_of(step, rank, own_chips) for step in range(chips)]
    counts = [count_ref[spot] for spot in spots]

    def copy_of(source, step, band):
        return pltpu.make_async_copy(
            stage.at[source], out_ref.at[spots[step], band], left.at[step, band]
        )

    patch = lax.broadcasted_iota(jnp.int32, (own, length), 0) + rank * own
    for step in range(chips):
        first = step * length
        xhat, inverse = norm_parts(get_rows(tok, first, length).astype(F32))
        back = get_rows(backs, first, length).astype(F32)
        grad = mid_ref[first : first + length] + norm_back(back, xhat, inverse, vec(gain))
        grad = grad / counts[step].astype(F32)
        chosen = visible_ref[pl.ds(spots[step], 1)] == patch
        chosen = jnp.where(chosen, 1.0, 0.0).astype(LOW)
        high = grad.astype(LOW)
        rest = (grad - high.astype(F32)).astype(LOW)
        stage[step] = dot(chosen, high) + dot(chosen, rest)

        def fill(band, carry, step=step):
            copy_of(step, step, band).start()
            return carry

        lax.fori_loop(0, counts[step], fill, 0)
    for step in range(chips):

        def finish(band, carry, step=step):
            copy_of(step, step, band).wait()
            return carry

        lax.fori_loop(0, counts[step], finish, 0)


def dec_kernel(
    place_ref, enc_low, proj_w, proj_bias, mask_token, position, visible_ref,
    attn_gain, attn_shift, out_bias, mlp_gain, mlp_shift, down_bias, up_bias,
    w0, w1, w2, w3, cotangent,
    decoded_keep, decoded_send, grad_latent_ref, n1_ref, n2_ref, gml_ref, act_ref, hid_ref,
    gqkv_ref, mixed_ref, vec_ref, upvec_ref,
    slope_scr, prob_scr, qkv_scr,
):
    weights = (w0, w1, w2, w3)
    parts = len(weights)
    chips, length = visible_ref.shape
    patches, width = position.shape
    kinds = 3 * HEAD
    inner = kinds + HEAD
    units = up_bias.shape[0] // parts
    up_at, down_at = slice(inner, inner + width), slice(inner + width, inner + width + units)
    spans = [slice(chip * patches, (chip + 1) * patches) for chip in range(chips)]
    latent = dot(enc_low[...], proj_w[...]) + vec(proj_bias)
    high = latent.astype(LOW)
    rest = (latent - high.astype(F32)).astype(LOW)
    streams, chosen, seen = [], [], []
    for chip in range(chips):
        near = slice(chip * length, (chip + 1) * length)
        hit = lax.broadcasted_iota(jnp.int32, (patches, length), 0) == visible_ref[chip : chip + 1]
        hit = jnp.where(hit, 1.0, 0.0)
        is_visible = jnp.sum(hit, 1, keepdims=True)
        hit = hit.astype(LOW)
        filled = dot(hit, high[near]) + dot(hit, rest[near])
        streams.append(filled + (1.0 - is_visible) * vec(mask_token) + position[...])
        chosen.append(hit)
        seen.append(is_visible)
    stream = jnp.concatenate(streams, 0)
    xhat1, inverse1 = norm_parts(stream)
    n1 = (xhat1 * vec(attn_gain) + vec(attn_shift)).astype(LOW)
    n1_ref[...] = n1
    for part, weight in enumerate(weights):
        qkv_scr[part] = dot(n1, weight[0:kinds], NT).astype(LOW)

    def qkv_of(part, span):
        return [qkv_scr[part, span, k * HEAD : (k + 1) * HEAD] for k in range(3)]

    for part in range(parts):
        for span in spans:
            queries, keyset, valset = qkv_of(part, span)
            probs = attend(queries, keyset, None)
            prob_scr[part, span] = probs
            mixed_ref[part, span] = dot(probs.astype(LOW), valset).astype(LOW)
    out_all = jnp.concatenate([weight[kinds:inner] for weight in weights], 0)
    mixed = jnp.concatenate([mixed_ref[part] for part in range(parts)], 1)
    middle = stream + dot(mixed, out_all) + vec(out_bias)
    xhat2, inverse2 = norm_parts(middle)
    n2 = (xhat2 * vec(mlp_gain) + vec(mlp_shift)).astype(LOW)
    n2_ref[...] = n2
    total = middle + vec(down_bias)
    for part, weight in enumerate(weights):
        spot = pl.multiple_of((place_ref[0] ^ part) * units, units)
        bias = up_bias[pl.ds(spot, units)][None, :]
        activation, slope = gelu_parts(dot(n2, weight[up_at]) + bias)
        act_low = activation.astype(LOW)
        act_ref[part] = act_low
        slope_scr[part] = slope.astype(LOW)
        total = total + dot(act_low, weight[down_at])
    column = width // parts
    half = parts // 2
    for part in range(parts):
        apart = place_ref[0] ^ part
        for chip, span in enumerate(spans):
            values = total[span, part * column : (part + 1) * column].astype(LOW)

            @pl.when(apart % 2 == 0)
            def _(values=values, apart=apart, chip=chip):
                decoded_keep[apart // 2, chip] = values

            @pl.when(apart % 2 == 1)
            def _(values=values, apart=apart, chip=chip):
                decoded_send[apart // 2, chip] = values

    grad_low = cotangent[...]
    grad_out = grad_low.astype(F32)
    grad_n2 = 0.0
    up_sums = []
    for part, weight in enumerate(weights):
        grad_hidden = dot(grad_low, weight[down_at], NT) * slope_scr[part].astype(F32)
        hidden_low = grad_hidden.astype(LOW)
        hid_ref[part] = hidden_low
        up_sums.append(col_sum(grad_hidden))
        grad_n2 = grad_n2 + dot(hidden_low, weight[up_at], NT)
    grad_middle = grad_out + norm_back(grad_n2, xhat2, inverse2, vec(mlp_gain))
    mlp_gain_sum, mlp_shift_sum = col_sum(grad_n2 * xhat2), col_sum(grad_n2)
    middle_low = grad_middle.astype(LOW)
    gml_ref[...] = middle_low
    grad_mixed = dot(middle_low, out_all, NT).astype(LOW)
    grad_n1 = 0.0
    for part, weight in enumerate(weights):
        for span in spans:
            own = grad_mixed[span, part * HEAD : (part + 1) * HEAD]
            found = attend_back(prob_scr[part, span], *qkv_of(part, span), own)
            gqkv_ref[part, span] = jnp.concatenate(found, 1)
        grad_n1 = grad_n1 + dot(gqkv_ref[part], weight[0:kinds])
    grad_stream = grad_middle + norm_back(grad_n1, xhat1, inverse1, vec(attn_gain))
    stream_low = grad_stream.astype(LOW)
    for chip, span in enumerate(spans):
        near = slice(chip * length, (chip + 1) * length)
        grad_latent_ref[near] = dot(chosen[chip], stream_low[span], TN).astype(LOW)
    seen_sum = col_sum(grad_stream * jnp.concatenate(seen, 0))
    vec_ref[...] = jnp.concatenate(
        [
            col_sum(grad_n1 * xhat1),
            col_sum(grad_n1),
            col_sum(grad_middle),
            mlp_gain_sum,
            mlp_shift_sum,
            col_sum(grad_out),
            seen_sum,
            col_sum(grad_stream) - seen_sum,
        ],
        0,
    )
    upvec_ref[...] = jnp.concatenate(up_sums + [jnp.zeros((8 - parts, units), F32)], 0)


def put_quarter(keep, sends, part, place, values):
    if part % 2 == 0:
        keep[part // 2, place] = values
        return
    half = sends[0].shape[0]
    put_block(sends[part - 1], sends[part], (), place, half, slice(None), slice(None), values)


def dec_up_kernel(
    place_ref, n2_ref, hid_ref, enc_low, latent, vec_ref, upvec_ref, keep, *sends
):
    parts, _, units = hid_ref.shape
    blocks = keep.shape[1]
    width, enc_width = n2_ref.shape[1], enc_low.shape[1]
    piece, enc_piece = width // blocks, enc_width // blocks
    column = latent.shape[1] // parts
    left = n2_ref[...].T
    left_proj = enc_low[...].T
    half_column = latent.shape[1] // parts // 2
    blank = jnp.zeros((half_column - 9, width), F32)
    for part in (1, 3, 0, 2):
        vectors = jnp.concatenate([vec_ref[...], upvec_ref[part : part + 1], blank], 0).T
        up = dot(left, hid_ref[part])
        spot = pl.multiple_of((place_ref[0] ^ part) * column, column)
        proj = dot(left_proj, latent[:, pl.ds(spot, column)])
        for block in range(blocks):
            first = block * enc_piece
            rest = proj[first + piece : first + enc_piece]
            rest = jnp.concatenate([rest[:, :half_column], rest[:, half_column:]], 0)
            values = jnp.concatenate(
                [
                    up[block * piece : (block + 1) * piece],
                    proj[first : first + piece],
                    rest,
                    vectors[block * piece : (block + 1) * piece],
                ],
                1,
            )
            place = spot_of(place_ref, block, blocks, UP)
            put_quarter(keep, sends, part, place, values.astype(LOW))


def dec_down_kernel(
    place_ref, cot_ref, act_ref, n1_ref, gqkv_ref, gml_ref, mixed_ref, keep, *sends
):
    parts = act_ref.shape[0]
    blocks = keep.shape[1]
    piece = n1_ref.shape[1] // blocks
    left_down, left_qkv, left_out = cot_ref[...].T, n1_ref[...].T, gml_ref[...].T
    for part in (1, 3, 0, 2):
        values = jnp.concatenate(
            [
                dot(left_down, act_ref[part]),
                dot(left_qkv, gqkv_ref[part]),
                dot(left_out, mixed_ref[part]),
            ],
            1,
        ).astype(LOW)
        for block in range(blocks):
            place = spot_of(place_ref, block, blocks, DOWN)
            put_quarter(keep, sends, part, place, values[block * piece : (block + 1) * piece])


def add_kernel(keep, got_0, got_1, out):
    half = got_0.shape[0]
    out[0:half] = (keep[0:half].astype(F32) + got_0[...].astype(F32)).astype(LOW)
    out[half:] = (keep[half:].astype(F32) + got_1[...].astype(F32)).astype(LOW)


def add_two_kernel(far_keep, far_got, near_keep, near_got, normed, far, near, early):
    early[...] = normed[...]
    far[...] = (far_keep[...].astype(F32) + far_got[...].astype(F32)).astype(LOW)
    near[...] = (near_keep[...].astype(F32) + near_got[...].astype(F32)).astype(LOW)


def add_with_kernel(keep, got_0, got_1, rest, out):
    rows = keep.shape[0]
    add_kernel(keep, got_0, got_1, out.at[0:rows])
    out[rows:] = rest[...]


def add_crossed_kernel(own, other, first, second):
    half = first.shape[0]
    first[...] = (own[0:half].astype(F32) + other[half : 2 * half].astype(F32)).astype(LOW)
    second[...] = (own[half : 2 * half].astype(F32) + other[0:half].astype(F32)).astype(LOW)


def assemble_kernel(place_ref, *refs):
    for sources, target in ((refs[0:4], refs[8]), (refs[4:8], refs[9])):
        for apart, source in enumerate(sources):
            rows = source.shape[0]
            spot = pl.multiple_of((place_ref[4] ^ apart) * rows, rows)
            target[pl.ds(spot, rows)] = source[...]


def copy_kernel(source, out):
    out[...] = source[...]


def pair_kernel(first, second, out):
    out[0] = first[...]
    out[1] = second[...]


def pick_kernel(place_ref, source, out):
    rows = out.shape[0]
    out[...] = source[pl.ds(pl.multiple_of(place_ref[4] * rows, rows), rows)]


class Behind:
    def __init__(self, array, places, rows):
        self.array, self.places, self.rows = array, places, rows

    def __getitem__(self, place):
        if len(self.array.shape) == 3:
            return self.array[place]
        first = self.array.shape[0] - (self.places - place) * self.rows
        return self.array[first : first + self.rows]


def total_of(arrays, place):
    total = arrays[0][place].astype(F32)
    for array in arrays[1:]:
        total = total + array[place].astype(F32)
    return total


def fold_kernel(*refs):
    arrays, (next_keep, next_send) = refs[:-2], refs[-2:]
    half = next_keep.shape[0]
    arrays = [Behind(array, 2 * half, arrays[0].shape[1]) for array in arrays]
    for place in range(half):
        next_send[place] = total_of(arrays, half + place).astype(LOW)
        next_keep[place] = total_of(arrays, place).astype(LOW)


def sum_kernel(*refs):
    for place in range(refs[-1].shape[0]):
        refs[-1][place] = total_of(refs[:-1], place).astype(LOW)


def split_kernel(keep, got_0, got_1, got_2, got_3, near_0, near_1, far_0, far_1):
    half = got_0.shape[0]
    pieces = ((0, got_0, near_0), (0, got_1, near_1), (1, got_2, far_0), (1, got_3, far_1))
    for number, (part, got, target) in enumerate(pieces):
        for place in range(half):
            first = keep[part, number % 2 * half + place].astype(F32)
            target[place] = (first + got[place].astype(F32)).astype(LOW)


def split_whole_kernel(keep, got_0, got_1, got_2, got_3, near, far):
    half = got_0.shape[0]
    split_kernel(
        keep, got_0, got_1, got_2, got_3,
        near.at[0:half], near.at[half:], far.at[0:half], far.at[half:],
    )


def enc_mlp_share_kernel(keep, got, up_ref, down_ref):
    piece, units = up_ref.shape
    total = total_of((keep, got), 0)
    up_ref[...] = total[:piece, :units]
    down_ref[...] = total[:piece, units:]


def enc_attn_share_kernel(keep, got, qkv_ref, out_ref, *vectors):
    total = total_of((keep, got), 0)
    inner, piece = out_ref.shape
    qkv_ref[...] = total[:piece, : 3 * inner].T
    out_ref[...] = total[:piece, 3 * inner :].T
    for row, vector in zip((10, 8, 9, 1, 0), vectors[:5], strict=True):
        vector[...] = total[total.shape[0] - VEC_ROWS + row, :piece]
    norms = total[total.shape[0] - VEC_ROWS :, :piece]
    vectors[5][...] = jnp.concatenate([norms[11:13], jnp.zeros((6, piece), F32)], 0)


def dec_up_share_kernel(keep, got, up_ref, proj_ref, *vectors):
    total = total_of((keep, got), 0)
    piece, units = up_ref.shape
    enc_piece, column = proj_ref.shape
    up_ref[...] = total[:, :units]
    rest = enc_piece - piece
    ends = total[:, units + column :]
    tail = jnp.concatenate([ends[:rest, : column // 2], ends[rest:, : column // 2]], 1)
    proj_ref[...] = jnp.concatenate([total[:, units : units + column], tail], 0).astype(LOW)
    rows = ends.T
    for row, vector in enumerate(vectors):
        vector[...] = rows[column // 2 + row, :piece]


def dec_down_share_kernel(keep, got, down_ref, qkv_ref, out_ref):
    total = total_of((keep, got), 0)
    units = down_ref.shape[1]
    inner = out_ref.shape[0]
    down_ref[...] = total[:, :units]
    qkv_ref[...] = total[:, units : units + 3 * inner].T
    out_ref[...] = total[:, units + 3 * inner :].T


def norm_add_kernel(first, second, out):
    out[...] = first[...] + second[...]


def norm_share_kernel(first, second, gain_ref, shift_ref):
    total = first[...] + second[...]
    gain_ref[...] = total[0]
    shift_ref[...] = total[1]


def proj_kernel(place_ref, own, core, far, out):
    column = own.shape[1]
    for apart, part in enumerate((own[...], core[...], far[0], far[1])):
        spot = pl.multiple_of((place_ref[0] ^ apart) * column, column)
        out[:, pl.ds(spot, column)] = part.astype(F32)


def decoded_kernel(place_ref, keep, got, far, out):
    chips = keep.shape[1]
    for index in range(chips):
        pieces = (keep[0, index], got[0, index], far[0, index], far[1, index])
        for apart, piece in enumerate(pieces):
            out[(place_ref[0] ^ apart) * chips + index] = piece.astype(F32)


def swap(values, axis, apart):
    size = lax.axis_size(axis)
    return lax.ppermute(values, axis, [(i, i ^ apart) for i in range(size)])


class Chain:
    def __init__(self, line, keep, send, steps):
        self.line, self.keep, self.step = line, list(keep), 0
        self.steps = steps
        self.got = self.exchange(send)

    def exchange(self, send):
        return swap(send, DP, 1 << self.steps[self.step])

    def fold(self):
        half = self.places() // 2
        out = jax.ShapeDtypeStruct((half,) + self.got.shape[1:], LOW)
        self.step += 1
        keep, send = self.line.call(
            fold_kernel, [out, out], [*self.keep, self.got]
        )
        self.keep = [keep]
        self.got = self.exchange(send)

    def places(self):
        return self.got.shape[0]

    def advance(self):
        if self.places() == 1:
            return True
        self.fold()
        return False

    def addends(self):
        return [*self.keep, self.got]


class DecChain(Chain):
    def __init__(self, line, near, far, steps):
        self.line, self.near, self.far, self.step = line, near, far, 0
        self.steps, self.got = steps, None

    def advance(self):
        if self.got is not None:
            return super().advance()
        if len(self.near) == 1:
            out = jax.ShapeDtypeStruct((self.near[0].shape[0] // 2,) + self.near[0].shape[1:], LOW)
            keep, send = self.line.call(fold_kernel, [out, out], [self.near[0], self.far[0]])
            self.keep = [keep]
        else:
            out = jax.ShapeDtypeStruct(self.near[1].shape, LOW)
            send = self.line.call(sum_kernel, [out], [self.near[1], self.far[1]])[0]
            self.keep = [self.near[0], self.far[0]]
        self.got = self.exchange(send)
        return False


def body(
    band_patches,
    band_counts,
    visible_index,
    enc_attn_gain,
    enc_attn_shift,
    enc_qkv_weight,
    enc_out_weight,
    enc_out_bias,
    enc_mlp_gain,
    enc_mlp_shift,
    enc_up_weight,
    enc_up_bias,
    enc_down_weight,
    enc_down_bias,
    proj_weight,
    proj_bias,
    mask_token,
    dec_attn_gain,
    dec_attn_shift,
    dec_qkv_weight,
    dec_out_weight,
    dec_out_bias,
    dec_mlp_gain,
    dec_mlp_shift,
    dec_up_weight,
    dec_up_bias,
    dec_down_weight,
    dec_down_bias,
    cotangent,
):
    parts = lax.axis_size(TENSOR)
    blocks = lax.axis_size(DP)
    rank = lax.axis_index(TENSOR)
    number = lax.axis_index(DP)
    place = jnp.stack(
        [rank, *(place_of(number, blocks, kind) for kind in (Y, Z, PAIRED)), number % 4]
    ).astype(jnp.int32)
    chips, length = visible_index.shape
    band_total, own_patches = band_patches.shape[1:3]
    own_chips = chips // parts
    enc_width = band_patches.shape[3]
    patches, dec_width = cotangent.shape[1:]
    enc_inner = enc_out_weight.shape[0]
    enc_units = enc_up_weight.shape[1]
    dec_units = dec_up_weight.shape[1]
    dec_inner = dec_out_weight.shape[0]
    dec_kinds = 3 * dec_inner
    rows = chips * length
    shape = jax.ShapeDtypeStruct
    half_rows = shape((rows // 2, enc_width), LOW)
    quarter_rows = shape((rows // 4, enc_width), LOW)
    all_rows = shape((rows, enc_width), LOW)
    wide_rows = shape((rows, enc_width), F32)
    hidden_shape = shape((rows, enc_units), LOW)
    vec_shape = shape((8, enc_width), F32)
    part_shapes = [half_rows, quarter_rows, quarter_rows]

    line = Line()
    call = line.call

    def core(values):
        return swap(values, TENSOR, 1)

    def add_cores(parts, after=()):
        keep, *sends = parts
        return call(add_kernel, [half_rows], [keep, *map(core, sends)], after=after)[0]

    def cross(own, after=()):
        pair = call(
            add_crossed_kernel, [quarter_rows] * 2, [own, swap(own, TENSOR, 2)], after=after
        )
        return [*pair, *map(core, pair)]

    w_own = jnp.concatenate(
        [
            dec_qkv_weight.reshape(dec_kinds, dec_width),
            dec_out_weight,
            dec_up_weight,
            dec_down_weight,
        ],
        0,
    )
    angles = lax.broadcasted_iota(F32, (patches, dec_width // 2), 0) * jnp.exp(
        lax.broadcasted_iota(F32, (patches, dec_width // 2), 1)
        * (-math.log(10000.0) / (dec_width // 2))
    )
    position = jnp.concatenate([jnp.sin(angles), jnp.cos(angles)], 1)
    own_visible = lax.dynamic_slice_in_dim(visible_index, rank * own_chips, own_chips, 0)
    own_cotangent = lax.dynamic_slice_in_dim(cotangent, rank * own_chips, own_chips, 0)
    own_cotangent = own_cotangent.reshape(-1, dec_width)
    parts_here = call(
        functools.partial(band_mean_kernel, own_chips=own_chips),
        part_shapes,
        [InHbm(band_patches), visible_index],
        scalars=[place, band_counts],
        scratch=[pltpu.VMEM(band_patches.shape, LOW), pltpu.SemaphoreType.DMA((chips,))],
        vmem=58 * 1024 * 1024,
        after=[],
    )
    own = add_cores(parts_here)
    band_zeros = call(
        functools.partial(band_zero_kernel, own_chips=own_chips),
        [InHbm(shape(band_patches.shape, F32))],
        [],
        scalars=[place, band_counts],
        scratch=[
            pltpu.VMEM((own_patches, enc_width), F32),
            pltpu.SemaphoreType.DMA((chips, band_total)),
        ],
    )[0]
    tok = cross(own)

    w_core = core(w_own)
    w_rows = w_own.shape[0] // 4
    w_pick = call(
        pick_kernel, [shape((w_rows, dec_width), LOW)], [w_own], scalars=[place]
    )[0]
    w_fourths = [swap(w_pick, TENSOR, 2)]
    w_fourths.append(swap(w_fourths[0], DP, 1))
    w_fourths.append(swap(w_fourths[0], DP, 2))
    w_fourths.append(swap(w_fourths[2], DP, 1))

    qkv_w = enc_qkv_weight.reshape(3 * enc_inner, enc_width)
    *parts_here, enc_n1, enc_qkv, enc_mixed, enc_probs = call(
        functools.partial(enc_attn_kernel, length=length),
        part_shapes
        + [
            all_rows, shape((rows, 3 * enc_inner), LOW), shape((rows, enc_inner), LOW),
            shape((enc_inner // HEAD, rows, 2 * length), F32),
        ],
        [*tok, enc_attn_gain, enc_attn_shift, qkv_w, enc_out_weight],
        after=[position, own_cotangent, own_visible],
    )
    own = add_cores(parts_here, [w_fourths[0]])
    sums = cross(own, [w_fourths[1], w_fourths[2]])
    *parts_here, enc_n2, enc_act, enc_slope = call(
        enc_mlp_kernel,
        [quarter_rows] * 4 + [all_rows, hidden_shape, hidden_shape],
        [
            *tok, *sums, enc_out_bias, enc_mlp_gain, enc_mlp_shift,
            enc_up_weight, enc_up_bias, enc_down_weight,
        ],
    )
    far, near, early = call(
        add_two_kernel,
        [quarter_rows] * 2 + [all_rows],
        [parts_here[1], core(parts_here[3]), parts_here[0], core(parts_here[2]), enc_n2],
    )
    early = swap(early, DP, 2)
    w_x, w_diag = call(
        assemble_kernel,
        [shape(w_own.shape, LOW)] * 2,
        [*w_fourths, *map(core, w_fourths)],
        scalars=[place],
    )
    enc_low = call(
        enc_out_kernel,
        [quarter_rows],
        [tok[0], sums[0], enc_out_bias, near, swap(far, TENSOR, 2), enc_down_bias],
    )[0]

    dec_rows = own_chips * patches
    dec_all = shape((dec_rows, dec_width), LOW)
    dec_hidden = shape((parts, dec_rows, dec_units), LOW)
    dec_column = shape((parts // 2, own_chips, patches, dec_width // parts), LOW)
    (
        decoded_keep, decoded_send, grad_latent, dec_n1, dec_n2, dec_gml, dec_act, dec_hid,
        dec_gqkv, dec_mixed, dec_vec, dec_upvec,
    ) = call(
        dec_kernel,
        [
            dec_column, dec_column, shape((own_chips * length, dec_width), LOW), dec_all, dec_all,
            dec_all, dec_hidden, dec_hidden, shape((parts, dec_rows, 3 * HEAD), LOW),
            shape((parts, dec_rows, HEAD), LOW), shape((8, dec_width), F32), shape((8, dec_units), F32),
        ],
        [
            enc_low, proj_weight, proj_bias, mask_token, position, own_visible, dec_attn_gain,
            dec_attn_shift, dec_out_bias, dec_mlp_gain, dec_mlp_shift, dec_down_bias, dec_up_bias,
            w_own, w_core, w_x, w_diag, own_cotangent,
        ],
        scalars=[place],
        scratch=[
            pltpu.VMEM((parts, dec_rows, dec_units), LOW),
            pltpu.VMEM((parts, dec_rows, patches), F32),
            pltpu.VMEM((parts, dec_rows, 3 * HEAD), LOW),
        ],
    )
    lat_far = swap(grad_latent, TENSOR, 2)
    decoded_got = core(decoded_send)
    decoded_far = swap(jnp.stack([decoded_keep[1], decoded_got[1]]), TENSOR, 2)
    dec_piece = dec_width // blocks
    enc_piece = enc_width // blocks
    enc_rows = -(-enc_piece // 16) * 16
    proj_own = dec_width // parts
    enc_vector = shape((enc_piece,), F32)
    dec_vector = shape((dec_piece,), F32)
    have = types.SimpleNamespace()

    def dec_bundle(kernel, columns, args):
        sends = [shape((blocks // 2, dec_piece, columns), LOW)] * 4
        keep, *sends = call(
            kernel, [shape((2, blocks, dec_piece, columns), LOW)] + sends, args, scalars=[place]
        )
        return [keep, *map(core, sends)]

    def dec_up():
        args = [dec_n2, dec_hid, enc_low, grad_latent, dec_vec, dec_upvec]
        have.dec_up = dec_bundle(dec_up_kernel, dec_units + 2 * proj_own, args)

    def dec_down():
        args = [own_cotangent, dec_act, dec_n1, dec_gqkv, dec_gml, dec_mixed]
        have.dec_down = dec_bundle(dec_down_kernel, dec_units + 4 * dec_inner, args)

    def up_split():
        out = shape(have.dec_up[0].shape[1:], LOW)
        near, far = call(split_whole_kernel, [out] * 2, have.dec_up)
        have.dec_up = DecChain(line, [near], [swap(far, TENSOR, 2)], steps_of(blocks, UP))

    def down_split():
        out = shape((blocks // 2,) + have.dec_down[0].shape[2:], LOW)
        *near, far_0, far_1 = call(split_kernel, [out] * 4, have.dec_down)
        have.dec_down = DecChain(line, near, [far_0, swap(far_1, TENSOR, 2)], steps_of(blocks, DOWN))

    def pair():
        have.lat = call(
            pair_kernel, [shape((2,) + grad_latent.shape, LOW)], [grad_latent, lat_far]
        )[0]
        have.lat_core = core(have.lat)
        have.lat_z = swap(have.lat, DP, 2)

    def lat_core():
        have.lat_z = call(copy_kernel, [have.lat], [have.lat_z])[0]
        have.lat_z_core = core(have.lat_z)

    def mlp_back():
        *have.parts, have.out_grad, have.gol, have.hid, have.vec_mlp = call(
            enc_mlp_back_kernel,
            part_shapes + [wide_rows, all_rows, hidden_shape, vec_shape],
            [have.lat, have.lat_core, proj_weight, enc_slope, enc_up_weight, enc_down_weight],
        )

    def add_back():
        have.own = add_cores(have.parts)

    def cross_back():
        have.backs = cross(have.own)

    def mlp_early():
        have.early = call(
            enc_mlp_early_kernel,
            [hidden_shape] * 2,
            [early, enc_up_weight, enc_up_bias],
        )

    def mlp_weights():
        bundle = shape((blocks // 4, enc_rows, 2 * enc_units), LOW)
        keep, send = call(
            enc_mlp_weights_kernel,
            [bundle] * 2,
            [
                enc_n2, have.hid, have.gol, enc_act, early, *have.early,
                have.lat_z, have.lat_z_core,
                proj_weight, enc_down_weight,
            ],
            scalars=[place],
        )
        have.mlp = Chain(line, [keep], send, steps_of(blocks, PAIRED))

    def attn_back():
        *have.parts, have.mid, have.gml, have.gqkv, have.vec_attn = call(
            functools.partial(enc_attn_back_kernel, length=length),
            part_shapes + [wide_rows, all_rows, shape((rows, 3 * enc_inner), LOW), vec_shape],
            [
                *tok, *sums, *have.backs, enc_out_bias, enc_mlp_gain, have.out_grad, enc_qkv, qkv_w,
                enc_out_weight, enc_probs,
            ],
        )

    def attn_weights():
        bundle = shape((blocks // 2, enc_rows + VEC_ROWS, 4 * enc_inner), LOW)
        keep, send = call(
            enc_attn_weights_kernel,
            [bundle, bundle],
            [enc_n1, have.gqkv, have.gml, enc_mixed, have.vec_mlp, have.vec_attn],
            scalars=[place],
        )
        have.attn = Chain(line, [keep], send, steps_of(blocks, ATTN))

    def add_grad():
        keep, *sends = have.parts
        chain = have.dec_down
        rest = chain.far[0].reshape(-1, enc_width)
        have.own = call(
            add_with_kernel,
            [shape((rows // 2 + rest.shape[0], enc_width), LOW)],
            [keep, *map(core, sends), rest],
        )[0]
        have.far = chain.far[0] = swap(have.own, TENSOR, 2)

    def cross_grad():
        halves = call(
            add_crossed_kernel, [quarter_rows] * 2, [have.own, have.far]
        )
        have.grads = [*halves, *map(core, halves)]

    def band_grads():
        have.band_grad = call(
            functools.partial(band_grad_kernel, own_chips=own_chips),
            [InHbm(shape(band_patches.shape, F32))],
            [*tok, *have.grads, have.mid, enc_attn_gain, visible_index, InHbm(band_zeros)],
            scalars=[place, band_counts],
            scratch=[
                pltpu.VMEM((chips, own_patches, enc_width), F32),
                pltpu.SemaphoreType.DMA((chips, band_total)),
            ],
            in_place=True,
        )[0]

    def mlp():
        if have.mlp.advance():
            have.mlp = call(
                enc_mlp_share_kernel,
                [shape((enc_piece, enc_units), F32)] * 2,
                have.mlp.addends(),
            )

    def attn():
        if have.attn.advance():
            have.attn = call(
                enc_attn_share_kernel,
                [shape((3 * enc_inner, enc_piece), F32), shape((enc_inner, enc_piece), F32)]
                + [enc_vector] * 5
                + [shape((8, enc_piece), F32)],
                have.attn.addends(),
            )
            have.norm_core = core(have.attn[-1])

    def up():
        if have.dec_up.advance():
            have.dec_up = call(
                dec_up_share_kernel,
                [shape((dec_piece, dec_units), F32), shape((enc_piece, proj_own), LOW)] + [dec_vector] * 9,
                have.dec_up.addends(),
            )
            have.proj_core = core(have.dec_up[1])

    def down():
        if have.dec_down.advance():
            have.dec_down = call(
                dec_down_share_kernel,
                [
                    shape((dec_piece, dec_units), F32),
                    shape((dec_kinds, dec_piece), F32),
                    shape((dec_inner, dec_piece), F32),
                ],
                have.dec_down.addends(),
            )

    def finish():
        while isinstance(have.mlp, Chain):
            mlp()
        while isinstance(have.attn, Chain):
            attn()
        while isinstance(have.dec_up, Chain):
            up()
        while isinstance(have.dec_down, Chain):
            down()

    def norm_add():
        own_norm = have.attn[-1]
        have.norm = call(
            norm_add_kernel, [shape((8, enc_piece), F32)], [own_norm, have.norm_core]
        )[0]
        have.norm_far = swap(have.norm, TENSOR, 2)

    def norm_share():
        have.norm_grads = call(
            norm_share_kernel, [enc_vector] * 2, [have.norm, have.norm_far]
        )

    def proj_far():
        have.proj_far = swap(jnp.stack([have.dec_up[1], have.proj_core]), TENSOR, 2)

    def proj_share():
        have.proj_grad = call(
            proj_kernel,
            [shape((enc_piece, dec_width), F32)],
            [have.dec_up[1], have.proj_core, have.proj_far],
            scalars=[place],
        )[0]

    def decoded_share():
        have.decoded = call(
            decoded_kernel,
            [shape((chips, patches, dec_width // parts), F32)],
            [decoded_keep, decoded_got, decoded_far],
            scalars=[place],
        )[0]

    order = (
        dec_up, pair, mlp_back, add_back, mlp_early, lat_core, up_split, mlp_weights, dec_down, cross_back,
        attn_back, down_split, attn_weights, add_grad, up, mlp, down, attn, mlp, up, up, cross_grad, down, up,
        attn, down, band_grads, down, attn, finish, norm_add, proj_far, decoded_share, proj_share, norm_share,
    )
    for step in order:
        step()
    decoded, band_grad, norm_grads = have.decoded, have.band_grad, have.norm_grads
    enc_up_grad, enc_down_grad = have.mlp
    enc_qkv_grad, enc_out_grad, *enc_vecs = have.attn
    dec_up_grad, _, *dec_vecs = have.dec_up
    dec_down_grad, dec_qkv_grad, dec_out_grad = have.dec_down
    proj_grad = have.proj_grad
    return (
        decoded,
        band_grad,
        *norm_grads,
        enc_qkv_grad.reshape(3, enc_inner, enc_piece),
        enc_out_grad,
        enc_vecs[0],
        enc_vecs[1],
        enc_vecs[2],
        enc_up_grad,
        enc_vecs[3],
        enc_down_grad.T,
        enc_vecs[4],
        proj_grad,
        dec_vecs[6],
        dec_vecs[7],
        dec_vecs[0],
        dec_vecs[1],
        dec_qkv_grad.reshape(3, dec_inner, dec_piece),
        dec_out_grad,
        dec_vecs[2],
        dec_vecs[3],
        dec_vecs[4],
        dec_up_grad,
        dec_vecs[8],
        dec_down_grad.T,
        dec_vecs[5],
    )


def solution(mesh):
    in_specs = (
        P(DP, None, TENSOR, None),
        P(DP),
        P(DP, None),
        P(),
        P(),
        P(None, TENSOR, None),
        P(TENSOR, None),
        P(),
        P(),
        P(),
        P(None, TENSOR),
        P(TENSOR),
        P(TENSOR, None),
        P(),
        P(),
        P(),
        P(),
        P(),
        P(),
        P(None, TENSOR, None),
        P(TENSOR, None),
        P(),
        P(),
        P(),
        P(None, TENSOR),
        P(),
        P(TENSOR, None),
        P(),
        P(DP, None, None),
    )
    out_specs = (
        P(DP, None, TENSOR),
        P(DP, None, TENSOR, None),
        P(DP),
        P(DP),
        P(None, TENSOR, DP),
        P(TENSOR, DP),
        P(DP),
        P(DP),
        P(DP),
        P(DP, TENSOR),
        P((TENSOR, DP)),
        P(TENSOR, DP),
        P(DP),
        P(DP, None),
        P(DP),
        P(DP),
        P(DP),
        P(DP),
        P(None, TENSOR, DP),
        P(TENSOR, DP),
        P(DP),
        P(DP),
        P(DP),
        P(DP, TENSOR),
        P((TENSOR, DP)),
        P(TENSOR, DP),
        P(DP),
    )
    return jax.shard_map(body, mesh=mesh, in_specs=in_specs, out_specs=out_specs, check_vma=False)
```

```python
import functools
import math
import types

import jax
import jax.numpy as jnp
from jax import lax
from jax.experimental import pallas as pl
from jax.experimental.pallas import tpu as pltpu
from jax.sharding import PartitionSpec as P

HEAD = 64
EPSILON = 1e-05
SCALE = HEAD ** (-0.5)
VMEM_BYTES = 30 * 1024 * 1024
F32 = jnp.float32
LOW = jnp.bfloat16
NN = (((1,), (0,)), ((), ()))
NT = (((1,), (1,)), ((), ()))
TN = (((0,), (0,)), ((), ()))
VEC_ROWS = 16
DP, TENSOR = "dp", "tensor"
Y, Z, PAIRED = range(3)
ATTN, UP, DOWN = Y, Z, Y


def dot(left, right, dims=NN):
    return lax.dot_general(left, right, dims, preferred_element_type=F32)


def col_sum(values):
    return jnp.sum(values, 0, keepdims=True)


def vec(ref):
    return ref[...][None, :]


def norm_parts(stream):
    center = stream - jnp.mean(stream, -1, keepdims=True)
    inverse = lax.rsqrt(jnp.mean(center * center, -1, keepdims=True) + EPSILON)
    return center * inverse, inverse


def norm_back(grad, xhat, inverse, gain):
    scaled = grad * gain
    mean_q = jnp.mean(scaled, -1, keepdims=True)
    mean_qx = jnp.mean(scaled * xhat, -1, keepdims=True)
    return inverse * (scaled - mean_q - xhat * mean_qx)


def gelu_parts(hidden):
    phi = 0.5 + 0.5 * lax.erf(hidden * (0.5**0.5))
    density = jnp.exp(hidden * hidden * -0.5) * (1.0 / math.sqrt(2.0 * math.pi))
    return hidden * phi, phi + hidden * density


def softmax_rows(scores):
    weights = jnp.exp(scores - jnp.max(scores, -1, keepdims=True))
    return weights * (1.0 / jnp.sum(weights, -1, keepdims=True))


def same_chip(rows, length):
    first = lax.broadcasted_iota(jnp.int32, (rows, rows), 0) // length
    second = lax.broadcasted_iota(jnp.int32, (rows, rows), 1) // length
    return first == second


def attend(queries, keyset, mask):
    scores = dot(queries, keyset, NT) * SCALE
    if mask is not None:
        scores = jnp.where(mask, scores, -1e30)
    return softmax_rows(scores)


def attend_back(probs, queries, keyset, valset, grad_mixed):
    grad_probs = dot(grad_mixed, valset, NT)
    grad_values = dot(probs.astype(LOW), grad_mixed, TN)
    grad_scores = probs * (grad_probs - jnp.sum(grad_probs * probs, -1, keepdims=True))
    score_low = grad_scores.astype(LOW)
    grad_queries = dot(score_low, keyset) * SCALE
    grad_keys = dot(score_low, queries, TN) * SCALE
    return grad_queries.astype(LOW), grad_keys.astype(LOW), grad_values.astype(LOW)


class Line:
    def __init__(self):
        self.token = None

    def call(self, body, out_shape, args, scalars=(), after=(), scratch=(), in_place=False, vmem=VMEM_BYTES):
        after = list(after) + ([] if self.token is None else [self.token])
        specs = [pl.BlockSpec(memory_space=pltpu.SMEM) for _ in scalars]
        for arg in args:
            specs.append(pl.BlockSpec(memory_space=pltpu.HBM if isinstance(arg, InHbm) else pltpu.VMEM))
        args = [arg.array if isinstance(arg, InHbm) else arg for arg in args]
        specs += [pl.BlockSpec(memory_space=pl.ANY) for _ in after]
        inputs = len(scalars) + len(args)
        outputs = len(out_shape)
        out_specs = []
        for out in out_shape:
            in_hbm = isinstance(out, InHbm)
            out_specs.append(pl.BlockSpec(memory_space=pltpu.HBM if in_hbm else pltpu.VMEM))
        out_shape = [out.array if isinstance(out, InHbm) else out for out in out_shape]
        out_shape = [jax.ShapeDtypeStruct(out.shape, out.dtype) for out in out_shape]

        def wrapped(*refs):
            outs = refs[inputs + len(after) :]
            outs[outputs][...] = jnp.zeros_like(outs[outputs])
            body(*refs[:inputs], *outs[:outputs], *outs[outputs + 1 :])

        *found, self.token = pl.pallas_call(
            wrapped,
            out_shape=out_shape + [jax.ShapeDtypeStruct((8, 128), F32)],
            in_specs=specs,
            out_specs=out_specs + [pl.BlockSpec(memory_space=pltpu.VMEM)],
            scratch_shapes=list(scratch),
            input_output_aliases={inputs - 1: 0} if in_place else {},
            compiler_params=pltpu.CompilerParams(vmem_limit_bytes=vmem),
            cost_estimate=pl.CostEstimate(flops=1, bytes_accessed=1, transcendentals=0),
            name=(body.func if isinstance(body, functools.partial) else body).__name__,
        )(*scalars, *args, *after)
        return found


class InHbm:
    def __init__(self, array):
        self.array = array


def steps_of(blocks, kind):
    steps = list(range(blocks.bit_length() - 1))
    if kind == Z:
        steps[:2] = [1, 0]
    if kind == PAIRED:
        steps.remove(1)
    return steps


def place_of(value, blocks, kind):
    steps = steps_of(blocks, kind)
    result = 0
    for place, bit in enumerate(steps):
        result = result | (((value >> bit) & 1) << (len(steps) - 1 - place))
    return result


def spot_of(place_ref, block, blocks, kind):
    return place_ref[1 + kind] ^ place_of(block, blocks, kind)


def put_block(keep, send, lead, place, half, rows, columns, values):
    @pl.when(place < half)
    def _():
        keep[lead + (place, rows, columns)] = values

    @pl.when(place >= half)
    def _():
        send[lead + (place - half, rows, columns)] = values


def chip_of(step, rank, own_chips):
    part, index = step // own_chips, step % own_chips
    apart = 2 * (part % 2) + part // 2
    return (rank ^ apart) * own_chips + index


def put_rows(parts, first, values):
    for part in parts:
        if first < part.shape[0]:
            part[first : first + values.shape[0]] = values
            return
        first -= part.shape[0]


def get_rows(parts, first, count):
    found = []
    for part in parts:
        size = part.shape[0]
        if first < size and count > 0:
            taken = min(count, size - first)
            found.append(part[first : first + taken])
            count -= taken
            first = size
        first -= size
    return found[0] if len(found) == 1 else jnp.concatenate(found, 0)


def band_mean_kernel(place_ref, count_ref, all_ref, visible_ref, *parts, own_chips):
    *parts, bands_ref, arrived = parts
    rank = place_ref[0]
    chips, bands, own, width = bands_ref.shape
    copies = []
    for step in range(chips):
        spot = chip_of(step, rank, own_chips)
        copies.append(pltpu.make_async_copy(all_ref.at[spot], bands_ref.at[step], arrived.at[step]))
        copies[-1].start()
    length = visible_ref.shape[1]
    patch = lax.broadcasted_iota(jnp.int32, (own, length), 0) + rank * own
    for step in range(chips):
        spot = chip_of(step, rank, own_chips)
        count = count_ref[spot]
        copies[step].wait()
        means = []
        for first in range(0, own, 16):
            span = slice(first, first + 16)
            total = bands_ref[step, 0, span].astype(F32)
            for band in range(1, bands):
                used = jnp.where(band < count, 1.0, 0.0).astype(F32)
                total = total + bands_ref[step, band, span].astype(F32) * used
            means.append((total / count.astype(F32)).astype(LOW))
        chosen = visible_ref[pl.ds(spot, 1)] == patch
        chosen = jnp.where(chosen, 1.0, 0.0).astype(LOW)
        values = dot(chosen, jnp.concatenate(means, 0), TN).astype(LOW)
        put_rows(parts, step * length, values)


def enc_attn_kernel(*refs, length):
    tok, (gain, shift, qkv_w, out_w) = refs[:4], refs[4:8]
    parts, (normed_ref, qkv_ref, mixed_ref, prob_ref) = refs[8:11], refs[11:]
    rows = normed_ref.shape[0] // 2
    inner = out_w.shape[0]
    block = 2 * length
    mask = same_chip(block, length)
    for group in range(2):
        span = slice(group * rows, (group + 1) * rows)
        xhat, _ = norm_parts(get_rows(tok, group * rows, rows).astype(F32))
        normed = (xhat * vec(gain) + vec(shift)).astype(LOW)
        normed_ref[span] = normed
        qkv = dot(normed, qkv_w[...], NT).astype(LOW)
        qkv_ref[span] = qkv
        blocks = []
        for first in range(0, rows, block):
            heads = []
            for head in range(inner // HEAD):
                at = [
                    qkv[first : first + block, k * inner + head * HEAD : k * inner + (head + 1) * HEAD]
                    for k in range(3)
                ]
                probs = attend(at[0], at[1], mask)
                prob_ref[head, group * rows + first : group * rows + first + block] = probs
                heads.append(dot(probs.astype(LOW), at[2]).astype(LOW))
            blocks.append(jnp.concatenate(heads, 1))
        mixed = jnp.concatenate(blocks, 0)
        mixed_ref[span] = mixed
        part = dot(mixed, out_w[...]).astype(LOW)
        for first in range(0, rows, block):
            put_rows(parts, group * rows + first, part[first : first + block])


def own_columns(values, which, blocks):
    piece = values.shape[1] // blocks
    kinds = []
    for bit in range(2):
        starts = [(4 * run + 2 * bit) * piece for run in range(blocks // 4)]
        kinds.append(jnp.concatenate([values[:, start : start + 2 * piece] for start in starts], 1))
    return jnp.where(which == 0, kinds[0], kinds[1])


def enc_mlp_kernel(*refs):
    tok, sums = refs[:4], refs[4:8]
    out_bias, gain, shift, up_w, up_bias, down_w = refs[8:14]
    parts, (normed_ref, act_ref, slope_ref) = refs[14:18], refs[18:]
    rows = normed_ref.shape[0] // 2
    block = rows // 2
    for group in range(2):
        span = slice(group * rows, (group + 1) * rows)
        middle = get_rows(tok, group * rows, rows).astype(F32) + vec(out_bias)
        middle = middle + get_rows(sums, group * rows, rows).astype(F32)
        xhat, _ = norm_parts(middle)
        normed = (xhat * vec(gain) + vec(shift)).astype(LOW)
        normed_ref[span] = normed
        activation, slope = gelu_parts(dot(normed, up_w[...]) + vec(up_bias))
        act_low, slope_low = activation.astype(LOW), slope.astype(LOW)
        act_ref[span] = act_low
        slope_ref[span] = slope_low
        part = dot(act_low, down_w[...]).astype(LOW)
        for first in range(0, rows, block):
            put_rows(parts, group * rows + first, part[first : first + block])


def enc_out_kernel(tok, total, out_bias, own, other, down_bias, low_ref):
    low_ref[...] = (
        tok[...].astype(F32)
        + total[...].astype(F32)
        + vec(out_bias)
        + own[...].astype(F32)
        + other[...].astype(F32)
        + vec(down_bias)
    ).astype(LOW)


def enc_mlp_back_kernel(lat_pair, lat_core, proj_w, slope_ref, up_w, down_w, *refs):
    lat = (lat_pair.at[0], lat_pair.at[1], lat_core.at[0], lat_core.at[1])
    parts, (out_ref, low_ref, hidden_ref, vec_ref) = refs[:3], refs[3:]
    rows = out_ref.shape[0] // 2
    block = rows // 2
    down_sum, up_sum = 0.0, 0.0
    for group in range(2):
        span = slice(group * rows, (group + 1) * rows)
        grad_out = dot(get_rows(lat, group * rows, rows), proj_w[...], NT)
        out_ref[span] = grad_out
        grad_low = grad_out.astype(LOW)
        low_ref[span] = grad_low
        grad_hidden = dot(grad_low, down_w[...], NT) * slope_ref[span].astype(F32)
        hidden_low = grad_hidden.astype(LOW)
        hidden_ref[span] = hidden_low
        down_sum = down_sum + col_sum(grad_out)
        up_sum = up_sum + col_sum(grad_hidden)
        part = dot(hidden_low, up_w[...], NT).astype(LOW)
        for first in range(0, rows, block):
            put_rows(parts, group * rows + first, part[first : first + block])
    vec_ref[...] = jnp.concatenate(
        [down_sum, up_sum, jnp.zeros((vec_ref.shape[0] - 2, down_sum.shape[1]), F32)], 0
    )


def enc_mlp_early_kernel(early_ref, up_w, up_bias, act_ref, slope_ref):
    activation, slope = gelu_parts(dot(early_ref[...], up_w[...]) + vec(up_bias))
    act_ref[...] = activation.astype(LOW)
    slope_ref[...] = slope.astype(LOW)


def enc_mlp_weights_kernel(
    place_ref, normed_ref, hidden_ref, low_ref, act_ref, early_ref, early_act, early_slope, lat_pair, lat_core,
    proj_w, down_w, keep, send
):
    half = keep.shape[0]
    blocks = 4 * half
    width, units = normed_ref.shape[1], hidden_ref.shape[1]
    piece = width // blocks
    which = place_ref[4] // 2
    lat = jnp.concatenate([lat_pair[0], lat_pair[1], lat_core[0], lat_core[1]], 0)
    low = dot(lat, proj_w[...], NT).astype(LOW)
    hidden = (dot(low, down_w[...], NT) * early_slope[...].astype(F32)).astype(LOW)
    for kind in range(2):
        if kind == 0:
            found = dot(own_columns(normed_ref[...], which, blocks), hidden_ref[...], TN)
            found = found + dot(own_columns(early_ref[...], which, blocks), hidden, TN)
        else:
            found = dot(own_columns(low_ref[...], which, blocks), act_ref[...], TN)
            found = found + dot(own_columns(low, which, blocks), early_act[...], TN)
        columns = slice(kind * units, (kind + 1) * units)
        for block in range(blocks // 2):
            values = found[block * piece : (block + 1) * piece].astype(LOW)
            place = spot_of(place_ref, 4 * (block // 2) + block % 2, blocks, PAIRED)
            put_block(keep, send, (), place, half, slice(0, piece), columns, values)


def enc_attn_back_kernel(*refs, length):
    tok, sums, backs = refs[:4], refs[4:8], refs[8:12]
    out_bias, mlp_gain, out_ref, qkv_ref, qkv_w, out_w, prob_ref = refs[12:19]
    parts, (mid_ref, low_ref, grad_qkv_ref, vec_ref) = refs[19:22], refs[22:]
    rows = out_ref.shape[0] // 2
    inner = out_w.shape[0]
    block = 2 * length
    found = [0.0] * 5
    for group in range(2):
        span = slice(group * rows, (group + 1) * rows)
        stream = get_rows(tok, group * rows, rows).astype(F32)
        total = get_rows(sums, group * rows, rows).astype(F32)
        xhat, inverse = norm_parts(stream + total + vec(out_bias))
        grad = get_rows(backs, group * rows, rows).astype(F32)
        found[0] = found[0] + col_sum(grad * xhat)
        found[1] = found[1] + col_sum(grad)
        grad_middle = out_ref[span] + norm_back(grad, xhat, inverse, vec(mlp_gain))
        mid_ref[span] = grad_middle
        found[2] = found[2] + col_sum(grad_middle)
        middle_low = grad_middle.astype(LOW)
        low_ref[span] = middle_low
        grad_mixed = dot(middle_low, out_w[...], NT).astype(LOW)
        blocks = []
        for first in range(0, rows, block):
            near = slice(group * rows + first, group * rows + first + block)
            grads = ([], [], [])
            for head in range(inner // HEAD):
                at = [
                    qkv_ref[near, k * inner + head * HEAD : k * inner + (head + 1) * HEAD]
                    for k in range(3)
                ]
                own = grad_mixed[first : first + block, head * HEAD : (head + 1) * HEAD]
                for kind, values in enumerate(attend_back(prob_ref[head, near], *at, own)):
                    grads[kind].append(values)
            blocks.append(jnp.concatenate(grads[0] + grads[1] + grads[2], 1))
        grad_qkv = jnp.concatenate(blocks, 0)
        grad_qkv_ref[span] = grad_qkv
        partial = dot(grad_qkv, qkv_w[...])
        part = partial.astype(LOW)
        for first in range(0, rows, block):
            put_rows(parts, group * rows + first, part[first : first + block])
        xhat, _ = norm_parts(stream)
        found[3] = found[3] + col_sum(partial * xhat)
        found[4] = found[4] + col_sum(partial)
    vec_ref[...] = jnp.concatenate(
        found + [jnp.zeros((vec_ref.shape[0] - 5, found[0].shape[1]), F32)], 0
    )


def enc_attn_weights_kernel(
    place_ref, normed_ref, grad_qkv_ref, low_ref, mixed_ref, vec_mlp, vec_attn, keep, send
):
    half = keep.shape[0]
    blocks = 2 * half
    width = normed_ref.shape[1]
    qkv = dot(normed_ref[...], grad_qkv_ref[...], TN)
    out = dot(low_ref[...], mixed_ref[...], TN)
    vectors = jnp.concatenate([vec_mlp[...], vec_attn[...]], 0)
    piece = width // blocks
    first = keep.shape[1] - VEC_ROWS
    for block in range(blocks):
        at = slice(block * piece, (block + 1) * piece)
        place = spot_of(place_ref, block, blocks, ATTN)
        values = jnp.concatenate([qkv[at], out[at]], 1).astype(LOW)
        put_block(keep, send, (), place, half, slice(0, piece), slice(None), values)
        put_block(
            keep, send, (), place, half, slice(first, first + VEC_ROWS), slice(0, piece),
            vectors[:, at].astype(LOW),
        )


def band_zero_kernel(place_ref, count_ref, out_ref, blank, left, *, own_chips):
    chips, bands = out_ref.shape[:2]
    blank[...] = jnp.zeros_like(blank)
    spots = [chip_of(step, place_ref[0], own_chips) for step in range(chips)]

    def copy_of(step, band):
        return pltpu.make_async_copy(blank, out_ref.at[spots[step], band], left.at[step, band])

    for step in range(chips):

        def begin(band, carry, step=step):
            copy_of(step, band).start()
            return carry

        lax.fori_loop(count_ref[spots[step]], bands, begin, 0)
    for step in range(chips):

        def finish(band, carry, step=step):
            copy_of(step, band).wait()
            return carry

        lax.fori_loop(count_ref[spots[step]], bands, finish, 0)


def band_grad_kernel(place_ref, count_ref, *refs, own_chips):
    tok, backs, (mid_ref, gain, visible_ref, _) = refs[:4], refs[4:8], refs[8:12]
    out_ref, stage, left = refs[12:]
    rank = place_ref[0]
    chips, bands, own, width = out_ref.shape
    length = visible_ref.shape[1]
    spots = [chip_of(step, rank, own_chips) for step in range(chips)]
    counts = [count_ref[spot] for spot in spots]

    def copy_of(source, step, band):
        return pltpu.make_async_copy(
            stage.at[source], out_ref.at[spots[step], band], left.at[step, band]
        )

    patch = lax.broadcasted_iota(jnp.int32, (own, length), 0) + rank * own
    for step in range(chips):
        first = step * length
        xhat, inverse = norm_parts(get_rows(tok, first, length).astype(F32))
        back = get_rows(backs, first, length).astype(F32)
        grad = mid_ref[first : first + length] + norm_back(back, xhat, inverse, vec(gain))
        grad = grad / counts[step].astype(F32)
        chosen = visible_ref[pl.ds(spots[step], 1)] == patch
        chosen = jnp.where(chosen, 1.0, 0.0).astype(LOW)
        high = grad.astype(LOW)
        rest = (grad - high.astype(F32)).astype(LOW)
        stage[step] = dot(chosen, high) + dot(chosen, rest)

        def fill(band, carry, step=step):
            copy_of(step, step, band).start()
            return carry

        lax.fori_loop(0, counts[step], fill, 0)
    for step in range(chips):

        def finish(band, carry, step=step):
            copy_of(step, step, band).wait()
            return carry

        lax.fori_loop(0, counts[step], finish, 0)


def dec_kernel(
    place_ref, enc_low, proj_w, proj_bias, mask_token, position, visible_ref,
    attn_gain, attn_shift, out_bias, mlp_gain, mlp_shift, down_bias, up_bias,
    w0, w1, w2, w3, cotangent,
    decoded_keep, decoded_send, grad_latent_ref, n1_ref, n2_ref, gml_ref, act_ref, hid_ref,
    gqkv_ref, mixed_ref, vec_ref, upvec_ref,
    slope_scr, prob_scr, qkv_scr,
):
    weights = (w0, w1, w2, w3)
    parts = len(weights)
    chips, length = visible_ref.shape
    patches, width = position.shape
    kinds = 3 * HEAD
    inner = kinds + HEAD
    units = up_bias.shape[0] // parts
    up_at, down_at = slice(inner, inner + width), slice(inner + width, inner + width + units)
    spans = [slice(chip * patches, (chip + 1) * patches) for chip in range(chips)]
    latent = dot(enc_low[...], proj_w[...]) + vec(proj_bias)
    high = latent.astype(LOW)
    rest = (latent - high.astype(F32)).astype(LOW)
    streams, chosen, seen = [], [], []
    for chip in range(chips):
        near = slice(chip * length, (chip + 1) * length)
        hit = lax.broadcasted_iota(jnp.int32, (patches, length), 0) == visible_ref[chip : chip + 1]
        hit = jnp.where(hit, 1.0, 0.0)
        is_visible = jnp.sum(hit, 1, keepdims=True)
        hit = hit.astype(LOW)
        filled = dot(hit, high[near]) + dot(hit, rest[near])
        streams.append(filled + (1.0 - is_visible) * vec(mask_token) + position[...])
        chosen.append(hit)
        seen.append(is_visible)
    stream = jnp.concatenate(streams, 0)
    xhat1, inverse1 = norm_parts(stream)
    n1 = (xhat1 * vec(attn_gain) + vec(attn_shift)).astype(LOW)
    n1_ref[...] = n1
    for part, weight in enumerate(weights):
        qkv_scr[part] = dot(n1, weight[0:kinds], NT).astype(LOW)

    def qkv_of(part, span):
        return [qkv_scr[part, span, k * HEAD : (k + 1) * HEAD] for k in range(3)]

    for part in range(parts):
        for span in spans:
            queries, keyset, valset = qkv_of(part, span)
            probs = attend(queries, keyset, None)
            prob_scr[part, span] = probs
            mixed_ref[part, span] = dot(probs.astype(LOW), valset).astype(LOW)
    out_all = jnp.concatenate([weight[kinds:inner] for weight in weights], 0)
    mixed = jnp.concatenate([mixed_ref[part] for part in range(parts)], 1)
    middle = stream + dot(mixed, out_all) + vec(out_bias)
    xhat2, inverse2 = norm_parts(middle)
    n2 = (xhat2 * vec(mlp_gain) + vec(mlp_shift)).astype(LOW)
    n2_ref[...] = n2
    total = middle + vec(down_bias)
    for part, weight in enumerate(weights):
        spot = pl.multiple_of((place_ref[0] ^ part) * units, units)
        bias = up_bias[pl.ds(spot, units)][None, :]
        activation, slope = gelu_parts(dot(n2, weight[up_at]) + bias)
        act_low = activation.astype(LOW)
        act_ref[part] = act_low
        slope_scr[part] = slope.astype(LOW)
        total = total + dot(act_low, weight[down_at])
    column = width // parts
    half = parts // 2
    for part in range(parts):
        apart = place_ref[0] ^ part
        for chip, span in enumerate(spans):
            values = total[span, part * column : (part + 1) * column].astype(LOW)

            @pl.when(apart % 2 == 0)
            def _(values=values, apart=apart, chip=chip):
                decoded_keep[apart // 2, chip] = values

            @pl.when(apart % 2 == 1)
            def _(values=values, apart=apart, chip=chip):
                decoded_send[apart // 2, chip] = values

    grad_low = cotangent[...]
    grad_out = grad_low.astype(F32)
    grad_n2 = 0.0
    up_sums = []
    for part, weight in enumerate(weights):
        grad_hidden = dot(grad_low, weight[down_at], NT) * slope_scr[part].astype(F32)
        hidden_low = grad_hidden.astype(LOW)
        hid_ref[part] = hidden_low
        up_sums.append(col_sum(grad_hidden))
        grad_n2 = grad_n2 + dot(hidden_low, weight[up_at], NT)
    grad_middle = grad_out + norm_back(grad_n2, xhat2, inverse2, vec(mlp_gain))
    mlp_gain_sum, mlp_shift_sum = col_sum(grad_n2 * xhat2), col_sum(grad_n2)
    middle_low = grad_middle.astype(LOW)
    gml_ref[...] = middle_low
    grad_mixed = dot(middle_low, out_all, NT).astype(LOW)
    grad_n1 = 0.0
    for part, weight in enumerate(weights):
        for span in spans:
            own = grad_mixed[span, part * HEAD : (part + 1) * HEAD]
            found = attend_back(prob_scr[part, span], *qkv_of(part, span), own)
            gqkv_ref[part, span] = jnp.concatenate(found, 1)
        grad_n1 = grad_n1 + dot(gqkv_ref[part], weight[0:kinds])
    grad_stream = grad_middle + norm_back(grad_n1, xhat1, inverse1, vec(attn_gain))
    stream_low = grad_stream.astype(LOW)
    for chip, span in enumerate(spans):
        near = slice(chip * length, (chip + 1) * length)
        grad_latent_ref[near] = dot(chosen[chip], stream_low[span], TN).astype(LOW)
    seen_sum = col_sum(grad_stream * jnp.concatenate(seen, 0))
    vec_ref[...] = jnp.concatenate(
        [
            col_sum(grad_n1 * xhat1),
            col_sum(grad_n1),
            col_sum(grad_middle),
            mlp_gain_sum,
            mlp_shift_sum,
            col_sum(grad_out),
            seen_sum,
            col_sum(grad_stream) - seen_sum,
        ],
        0,
    )
    upvec_ref[...] = jnp.concatenate(up_sums + [jnp.zeros((8 - parts, units), F32)], 0)


def put_quarter(keep, sends, part, place, values):
    if part % 2 == 0:
        keep[part // 2, place] = values
        return
    half = sends[0].shape[0]
    put_block(sends[part - 1], sends[part], (), place, half, slice(None), slice(None), values)


def dec_up_kernel(
    place_ref, n2_ref, hid_ref, enc_low, latent, vec_ref, upvec_ref, keep, *sends
):
    parts, _, units = hid_ref.shape
    blocks = keep.shape[1]
    width, enc_width = n2_ref.shape[1], enc_low.shape[1]
    piece, enc_piece = width // blocks, enc_width // blocks
    column = latent.shape[1] // parts
    left = n2_ref[...].T
    left_proj = enc_low[...].T
    half_column = latent.shape[1] // parts // 2
    blank = jnp.zeros((half_column - 9, width), F32)
    for part in (1, 3, 0, 2):
        vectors = jnp.concatenate([vec_ref[...], upvec_ref[part : part + 1], blank], 0).T
        up = dot(left, hid_ref[part])
        spot = pl.multiple_of((place_ref[0] ^ part) * column, column)
        proj = dot(left_proj, latent[:, pl.ds(spot, column)])
        for block in range(blocks):
            first = block * enc_piece
            rest = proj[first + piece : first + enc_piece]
            rest = jnp.concatenate([rest[:, :half_column], rest[:, half_column:]], 0)
            values = jnp.concatenate(
                [
                    up[block * piece : (block + 1) * piece],
                    proj[first : first + piece],
                    rest,
                    vectors[block * piece : (block + 1) * piece],
                ],
                1,
            )
            place = spot_of(place_ref, block, blocks, UP)
            put_quarter(keep, sends, part, place, values.astype(LOW))


def dec_down_kernel(
    place_ref, cot_ref, act_ref, n1_ref, gqkv_ref, gml_ref, mixed_ref, keep, *sends
):
    parts = act_ref.shape[0]
    blocks = keep.shape[1]
    piece = n1_ref.shape[1] // blocks
    left_down, left_qkv, left_out = cot_ref[...].T, n1_ref[...].T, gml_ref[...].T
    for part in (1, 3, 0, 2):
        values = jnp.concatenate(
            [
                dot(left_down, act_ref[part]),
                dot(left_qkv, gqkv_ref[part]),
                dot(left_out, mixed_ref[part]),
            ],
            1,
        ).astype(LOW)
        for block in range(blocks):
            place = spot_of(place_ref, block, blocks, DOWN)
            put_quarter(keep, sends, part, place, values[block * piece : (block + 1) * piece])


def add_kernel(keep, got_0, got_1, out):
    half = got_0.shape[0]
    out[0:half] = (keep[0:half].astype(F32) + got_0[...].astype(F32)).astype(LOW)
    out[half:] = (keep[half:].astype(F32) + got_1[...].astype(F32)).astype(LOW)


def add_two_kernel(far_keep, far_got, near_keep, near_got, normed, far, near, early):
    early[...] = normed[...]
    far[...] = (far_keep[...].astype(F32) + far_got[...].astype(F32)).astype(LOW)
    near[...] = (near_keep[...].astype(F32) + near_got[...].astype(F32)).astype(LOW)


def add_with_kernel(keep, got_0, got_1, rest, out):
    rows = keep.shape[0]
    add_kernel(keep, got_0, got_1, out.at[0:rows])
    out[rows:] = rest[...]


def add_crossed_kernel(own, other, first, second):
    half = first.shape[0]
    first[...] = (own[0:half].astype(F32) + other[half : 2 * half].astype(F32)).astype(LOW)
    second[...] = (own[half : 2 * half].astype(F32) + other[0:half].astype(F32)).astype(LOW)


def assemble_kernel(place_ref, *refs):
    for sources, target in ((refs[0:4], refs[8]), (refs[4:8], refs[9])):
        for apart, source in enumerate(sources):
            rows = source.shape[0]
            spot = pl.multiple_of((place_ref[4] ^ apart) * rows, rows)
            target[pl.ds(spot, rows)] = source[...]


def copy_kernel(source, out):
    out[...] = source[...]


def pair_kernel(first, second, out):
    out[0] = first[...]
    out[1] = second[...]


def pick_kernel(place_ref, source, out):
    rows = out.shape[0]
    out[...] = source[pl.ds(pl.multiple_of(place_ref[4] * rows, rows), rows)]


class Behind:
    def __init__(self, array, places, rows):
        self.array, self.places, self.rows = array, places, rows

    def __getitem__(self, place):
        if len(self.array.shape) == 3:
            return self.array[place]
        first = self.array.shape[0] - (self.places - place) * self.rows
        return self.array[first : first + self.rows]


def total_of(arrays, place):
    total = arrays[0][place].astype(F32)
    for array in arrays[1:]:
        total = total + array[place].astype(F32)
    return total


def fold_kernel(*refs):
    arrays, (next_keep, next_send) = refs[:-2], refs[-2:]
    half = next_keep.shape[0]
    arrays = [Behind(array, 2 * half, arrays[0].shape[1]) for array in arrays]
    for place in range(half):
        next_send[place] = total_of(arrays, half + place).astype(LOW)
        next_keep[place] = total_of(arrays, place).astype(LOW)


def sum_kernel(*refs):
    for place in range(refs[-1].shape[0]):
        refs[-1][place] = total_of(refs[:-1], place).astype(LOW)


def split_kernel(keep, got_0, got_1, got_2, got_3, near_0, near_1, far_0, far_1):
    half = got_0.shape[0]
    pieces = ((0, got_0, near_0), (0, got_1, near_1), (1, got_2, far_0), (1, got_3, far_1))
    for number, (part, got, target) in enumerate(pieces):
        for place in range(half):
            first = keep[part, number % 2 * half + place].astype(F32)
            target[place] = (first + got[place].astype(F32)).astype(LOW)


def split_whole_kernel(keep, got_0, got_1, got_2, got_3, near, far):
    half = got_0.shape[0]
    split_kernel(
        keep, got_0, got_1, got_2, got_3,
        near.at[0:half], near.at[half:], far.at[0:half], far.at[half:],
    )


def enc_mlp_share_kernel(keep, got, up_ref, down_ref):
    piece, units = up_ref.shape
    total = total_of((keep, got), 0)
    up_ref[...] = total[:piece, :units]
    down_ref[...] = total[:piece, units:]


def enc_attn_share_kernel(keep, got, qkv_ref, out_ref, *vectors):
    total = total_of((keep, got), 0)
    inner, piece = out_ref.shape
    qkv_ref[...] = total[:piece, : 3 * inner].T
    out_ref[...] = total[:piece, 3 * inner :].T
    for row, vector in zip((10, 8, 9, 1, 0), vectors[:5], strict=True):
        vector[...] = total[total.shape[0] - VEC_ROWS + row, :piece]
    norms = total[total.shape[0] - VEC_ROWS :, :piece]
    vectors[5][...] = jnp.concatenate([norms[11:13], jnp.zeros((6, piece), F32)], 0)


def dec_up_share_kernel(keep, got, up_ref, proj_ref, *vectors):
    total = total_of((keep, got), 0)
    piece, units = up_ref.shape
    enc_piece, column = proj_ref.shape
    up_ref[...] = total[:, :units]
    rest = enc_piece - piece
    ends = total[:, units + column :]
    tail = jnp.concatenate([ends[:rest, : column // 2], ends[rest:, : column // 2]], 1)
    proj_ref[...] = jnp.concatenate([total[:, units : units + column], tail], 0).astype(LOW)
    rows = ends.T
    for row, vector in enumerate(vectors):
        vector[...] = rows[column // 2 + row, :piece]


def dec_down_share_kernel(keep, got, down_ref, qkv_ref, out_ref):
    total = total_of((keep, got), 0)
    units = down_ref.shape[1]
    inner = out_ref.shape[0]
    down_ref[...] = total[:, :units]
    qkv_ref[...] = total[:, units : units + 3 * inner].T
    out_ref[...] = total[:, units + 3 * inner :].T


def norm_add_kernel(first, second, out):
    out[...] = first[...] + second[...]


def norm_share_kernel(first, second, gain_ref, shift_ref):
    total = first[...] + second[...]
    gain_ref[...] = total[0]
    shift_ref[...] = total[1]


def proj_kernel(place_ref, own, core, far, out):
    column = own.shape[1]
    for apart, part in enumerate((own[...], core[...], far[0], far[1])):
        spot = pl.multiple_of((place_ref[0] ^ apart) * column, column)
        out[:, pl.ds(spot, column)] = part.astype(F32)


def decoded_kernel(place_ref, keep, got, far, out):
    chips = keep.shape[1]
    for index in range(chips):
        pieces = (keep[0, index], got[0, index], far[0, index], far[1, index])
        for apart, piece in enumerate(pieces):
            out[(place_ref[0] ^ apart) * chips + index] = piece.astype(F32)


def swap(values, axis, apart):
    size = lax.axis_size(axis)
    return lax.ppermute(values, axis, [(i, i ^ apart) for i in range(size)])


class Chain:
    def __init__(self, line, keep, send, steps):
        self.line, self.keep, self.step = line, list(keep), 0
        self.steps = steps
        self.got = self.exchange(send)

    def exchange(self, send):
        return swap(send, DP, 1 << self.steps[self.step])

    def fold(self):
        half = self.places() // 2
        out = jax.ShapeDtypeStruct((half,) + self.got.shape[1:], LOW)
        self.step += 1
        keep, send = self.line.call(
            fold_kernel, [out, out], [*self.keep, self.got]
        )
        self.keep = [keep]
        self.got = self.exchange(send)

    def places(self):
        return self.got.shape[0]

    def advance(self):
        if self.places() == 1:
            return True
        self.fold()
        return False

    def addends(self):
        return [*self.keep, self.got]


class DecChain(Chain):
    def __init__(self, line, near, far, steps):
        self.line, self.near, self.far, self.step = line, near, far, 0
        self.steps, self.got = steps, None

    def advance(self):
        if self.got is not None:
            return super().advance()
        if len(self.near) == 1:
            out = jax.ShapeDtypeStruct((self.near[0].shape[0] // 2,) + self.near[0].shape[1:], LOW)
            keep, send = self.line.call(fold_kernel, [out, out], [self.near[0], self.far[0]])
            self.keep = [keep]
        else:
            out = jax.ShapeDtypeStruct(self.near[1].shape, LOW)
            send = self.line.call(sum_kernel, [out], [self.near[1], self.far[1]])[0]
            self.keep = [self.near[0], self.far[0]]
        self.got = self.exchange(send)
        return False


def body(
    band_patches,
    band_counts,
    visible_index,
    enc_attn_gain,
    enc_attn_shift,
    enc_qkv_weight,
    enc_out_weight,
    enc_out_bias,
    enc_mlp_gain,
    enc_mlp_shift,
    enc_up_weight,
    enc_up_bias,
    enc_down_weight,
    enc_down_bias,
    proj_weight,
    proj_bias,
    mask_token,
    dec_attn_gain,
    dec_attn_shift,
    dec_qkv_weight,
    dec_out_weight,
    dec_out_bias,
    dec_mlp_gain,
    dec_mlp_shift,
    dec_up_weight,
    dec_up_bias,
    dec_down_weight,
    dec_down_bias,
    cotangent,
):
    parts = lax.axis_size(TENSOR)
    blocks = lax.axis_size(DP)
    rank = lax.axis_index(TENSOR)
    number = lax.axis_index(DP)
    place = jnp.stack(
        [rank, *(place_of(number, blocks, kind) for kind in (Y, Z, PAIRED)), number % 4]
    ).astype(jnp.int32)
    chips, length = visible_index.shape
    band_total, own_patches = band_patches.shape[1:3]
    own_chips = chips // parts
    enc_width = band_patches.shape[3]
    patches, dec_width = cotangent.shape[1:]
    enc_inner = enc_out_weight.shape[0]
    enc_units = enc_up_weight.shape[1]
    dec_units = dec_up_weight.shape[1]
    dec_inner = dec_out_weight.shape[0]
    dec_kinds = 3 * dec_inner
    rows = chips * length
    shape = jax.ShapeDtypeStruct
    half_rows = shape((rows // 2, enc_width), LOW)
    quarter_rows = shape((rows // 4, enc_width), LOW)
    all_rows = shape((rows, enc_width), LOW)
    wide_rows = shape((rows, enc_width), F32)
    hidden_shape = shape((rows, enc_units), LOW)
    vec_shape = shape((8, enc_width), F32)
    part_shapes = [half_rows, quarter_rows, quarter_rows]

    line = Line()
    call = line.call

    def core(values):
        return swap(values, TENSOR, 1)

    def add_cores(parts, after=()):
        keep, *sends = parts
        return call(add_kernel, [half_rows], [keep, *map(core, sends)], after=after)[0]

    def cross(own, after=()):
        pair = call(
            add_crossed_kernel, [quarter_rows] * 2, [own, swap(own, TENSOR, 2)], after=after
        )
        return [*pair, *map(core, pair)]

    w_own = jnp.concatenate(
        [
            dec_qkv_weight.reshape(dec_kinds, dec_width),
            dec_out_weight,
            dec_up_weight,
            dec_down_weight,
        ],
        0,
    )
    angles = lax.broadcasted_iota(F32, (patches, dec_width // 2), 0) * jnp.exp(
        lax.broadcasted_iota(F32, (patches, dec_width // 2), 1)
        * (-math.log(10000.0) / (dec_width // 2))
    )
    position = jnp.concatenate([jnp.sin(angles), jnp.cos(angles)], 1)
    own_visible = lax.dynamic_slice_in_dim(visible_index, rank * own_chips, own_chips, 0)
    own_cotangent = lax.dynamic_slice_in_dim(cotangent, rank * own_chips, own_chips, 0)
    own_cotangent = own_cotangent.reshape(-1, dec_width)
    parts_here = call(
        functools.partial(band_mean_kernel, own_chips=own_chips),
        part_shapes,
        [InHbm(band_patches), visible_index],
        scalars=[place, band_counts],
        scratch=[pltpu.VMEM(band_patches.shape, LOW), pltpu.SemaphoreType.DMA((chips,))],
        vmem=50 * 1024 * 1024,
        after=[],
    )
    own = add_cores(parts_here)
    band_zeros = call(
        functools.partial(band_zero_kernel, own_chips=own_chips),
        [InHbm(shape(band_patches.shape, F32))],
        [],
        scalars=[place, band_counts],
        scratch=[
            pltpu.VMEM((own_patches, enc_width), F32),
            pltpu.SemaphoreType.DMA((chips, band_total)),
        ],
    )[0]
    tok = cross(own)

    w_core = core(w_own)
    w_rows = w_own.shape[0] // 4
    w_pick = call(
        pick_kernel, [shape((w_rows, dec_width), LOW)], [w_own], scalars=[place]
    )[0]
    w_fourths = [swap(w_pick, TENSOR, 2)]
    w_fourths.append(swap(w_fourths[0], DP, 1))
    w_fourths.append(swap(w_fourths[0], DP, 2))
    w_fourths.append(swap(w_fourths[2], DP, 1))

    qkv_w = enc_qkv_weight.reshape(3 * enc_inner, enc_width)
    *parts_here, enc_n1, enc_qkv, enc_mixed, enc_probs = call(
        functools.partial(enc_attn_kernel, length=length),
        part_shapes
        + [
            all_rows, shape((rows, 3 * enc_inner), LOW), shape((rows, enc_inner), LOW),
            shape((enc_inner // HEAD, rows, 2 * length), F32),
        ],
        [*tok, enc_attn_gain, enc_attn_shift, qkv_w, enc_out_weight],
        after=[position, own_cotangent, own_visible],
    )
    own = add_cores(parts_here, [w_fourths[0]])
    sums = cross(own, [w_fourths[1], w_fourths[2]])
    *parts_here, enc_n2, enc_act, enc_slope = call(
        enc_mlp_kernel,
        [quarter_rows] * 4 + [all_rows, hidden_shape, hidden_shape],
        [
            *tok, *sums, enc_out_bias, enc_mlp_gain, enc_mlp_shift,
            enc_up_weight, enc_up_bias, enc_down_weight,
        ],
    )
    far, near, early = call(
        add_two_kernel,
        [quarter_rows] * 2 + [all_rows],
        [parts_here[1], core(parts_here[3]), parts_here[0], core(parts_here[2]), enc_n2],
    )
    early = swap(early, DP, 2)
    w_x, w_diag = call(
        assemble_kernel,
        [shape(w_own.shape, LOW)] * 2,
        [*w_fourths, *map(core, w_fourths)],
        scalars=[place],
    )
    enc_low = call(
        enc_out_kernel,
        [quarter_rows],
        [tok[0], sums[0], enc_out_bias, near, swap(far, TENSOR, 2), enc_down_bias],
    )[0]

    dec_rows = own_chips * patches
    dec_all = shape((dec_rows, dec_width), LOW)
    dec_hidden = shape((parts, dec_rows, dec_units), LOW)
    dec_column = shape((parts // 2, own_chips, patches, dec_width // parts), LOW)
    (
        decoded_keep, decoded_send, grad_latent, dec_n1, dec_n2, dec_gml, dec_act, dec_hid,
        dec_gqkv, dec_mixed, dec_vec, dec_upvec,
    ) = call(
        dec_kernel,
        [
            dec_column, dec_column, shape((own_chips * length, dec_width), LOW), dec_all, dec_all,
            dec_all, dec_hidden, dec_hidden, shape((parts, dec_rows, 3 * HEAD), LOW),
            shape((parts, dec_rows, HEAD), LOW), shape((8, dec_width), F32), shape((8, dec_units), F32),
        ],
        [
            enc_low, proj_weight, proj_bias, mask_token, position, own_visible, dec_attn_gain,
            dec_attn_shift, dec_out_bias, dec_mlp_gain, dec_mlp_shift, dec_down_bias, dec_up_bias,
            w_own, w_core, w_x, w_diag, own_cotangent,
        ],
        scalars=[place],
        scratch=[
            pltpu.VMEM((parts, dec_rows, dec_units), LOW),
            pltpu.VMEM((parts, dec_rows, patches), F32),
            pltpu.VMEM((parts, dec_rows, 3 * HEAD), LOW),
        ],
    )
    lat_far = swap(grad_latent, TENSOR, 2)
    decoded_got = core(decoded_send)
    decoded_far = swap(jnp.stack([decoded_keep[1], decoded_got[1]]), TENSOR, 2)
    dec_piece = dec_width // blocks
    enc_piece = enc_width // blocks
    enc_rows = -(-enc_piece // 16) * 16
    proj_own = dec_width // parts
    enc_vector = shape((enc_piece,), F32)
    dec_vector = shape((dec_piece,), F32)
    have = types.SimpleNamespace()

    def dec_bundle(kernel, columns, args):
        sends = [shape((blocks // 2, dec_piece, columns), LOW)] * 4
        keep, *sends = call(
            kernel, [shape((2, blocks, dec_piece, columns), LOW)] + sends, args, scalars=[place]
        )
        return [keep, *map(core, sends)]

    def dec_up():
        args = [dec_n2, dec_hid, enc_low, grad_latent, dec_vec, dec_upvec]
        have.dec_up = dec_bundle(dec_up_kernel, dec_units + 2 * proj_own, args)

    def dec_down():
        args = [own_cotangent, dec_act, dec_n1, dec_gqkv, dec_gml, dec_mixed]
        have.dec_down = dec_bundle(dec_down_kernel, dec_units + 4 * dec_inner, args)

    def up_split():
        out = shape(have.dec_up[0].shape[1:], LOW)
        near, far = call(split_whole_kernel, [out] * 2, have.dec_up)
        have.dec_up = DecChain(line, [near], [swap(far, TENSOR, 2)], steps_of(blocks, UP))

    def down_split():
        out = shape((blocks // 2,) + have.dec_down[0].shape[2:], LOW)
        *near, far_0, far_1 = call(split_kernel, [out] * 4, have.dec_down)
        have.dec_down = DecChain(line, near, [far_0, swap(far_1, TENSOR, 2)], steps_of(blocks, DOWN))

    def pair():
        have.lat = call(
            pair_kernel, [shape((2,) + grad_latent.shape, LOW)], [grad_latent, lat_far]
        )[0]
        have.lat_core = core(have.lat)
        have.lat_z = swap(have.lat, DP, 2)

    def lat_core():
        have.lat_z = call(copy_kernel, [have.lat], [have.lat_z])[0]
        have.lat_z_core = core(have.lat_z)

    def mlp_back():
        *have.parts, have.out_grad, have.gol, have.hid, have.vec_mlp = call(
            enc_mlp_back_kernel,
            part_shapes + [wide_rows, all_rows, hidden_shape, vec_shape],
            [have.lat, have.lat_core, proj_weight, enc_slope, enc_up_weight, enc_down_weight],
        )

    def add_back():
        have.own = add_cores(have.parts)

    def cross_back():
        have.backs = cross(have.own)

    def mlp_early():
        have.early = call(
            enc_mlp_early_kernel,
            [hidden_shape] * 2,
            [early, enc_up_weight, enc_up_bias],
        )

    def mlp_weights():
        bundle = shape((blocks // 4, enc_rows, 2 * enc_units), LOW)
        keep, send = call(
            enc_mlp_weights_kernel,
            [bundle] * 2,
            [
                enc_n2, have.hid, have.gol, enc_act, early, *have.early,
                have.lat_z, have.lat_z_core,
                proj_weight, enc_down_weight,
            ],
            scalars=[place],
        )
        have.mlp = Chain(line, [keep], send, steps_of(blocks, PAIRED))

    def attn_back():
        *have.parts, have.mid, have.gml, have.gqkv, have.vec_attn = call(
            functools.partial(enc_attn_back_kernel, length=length),
            part_shapes + [wide_rows, all_rows, shape((rows, 3 * enc_inner), LOW), vec_shape],
            [
                *tok, *sums, *have.backs, enc_out_bias, enc_mlp_gain, have.out_grad, enc_qkv, qkv_w,
                enc_out_weight, enc_probs,
            ],
        )

    def attn_weights():
        bundle = shape((blocks // 2, enc_rows + VEC_ROWS, 4 * enc_inner), LOW)
        keep, send = call(
            enc_attn_weights_kernel,
            [bundle, bundle],
            [enc_n1, have.gqkv, have.gml, enc_mixed, have.vec_mlp, have.vec_attn],
            scalars=[place],
        )
        have.attn = Chain(line, [keep], send, steps_of(blocks, ATTN))

    def add_grad():
        keep, *sends = have.parts
        chain = have.dec_down
        rest = chain.far[0].reshape(-1, enc_width)
        have.own = call(
            add_with_kernel,
            [shape((rows // 2 + rest.shape[0], enc_width), LOW)],
            [keep, *map(core, sends), rest],
        )[0]
        have.far = chain.far[0] = swap(have.own, TENSOR, 2)

    def cross_grad():
        halves = call(
            add_crossed_kernel, [quarter_rows] * 2, [have.own, have.far]
        )
        have.grads = [*halves, *map(core, halves)]

    def band_grads():
        have.band_grad = call(
            functools.partial(band_grad_kernel, own_chips=own_chips),
            [InHbm(shape(band_patches.shape, F32))],
            [*tok, *have.grads, have.mid, enc_attn_gain, visible_index, InHbm(band_zeros)],
            scalars=[place, band_counts],
            scratch=[
                pltpu.VMEM((chips, own_patches, enc_width), F32),
                pltpu.SemaphoreType.DMA((chips, band_total)),
            ],
            in_place=True,
        )[0]

    def mlp():
        if have.mlp.advance():
            have.mlp = call(
                enc_mlp_share_kernel,
                [shape((enc_piece, enc_units), F32)] * 2,
                have.mlp.addends(),
            )

    def attn():
        if have.attn.advance():
            have.attn = call(
                enc_attn_share_kernel,
                [shape((3 * enc_inner, enc_piece), F32), shape((enc_inner, enc_piece), F32)]
                + [enc_vector] * 5
                + [shape((8, enc_piece), F32)],
                have.attn.addends(),
            )
            have.norm_core = core(have.attn[-1])

    def up():
        if have.dec_up.advance():
            have.dec_up = call(
                dec_up_share_kernel,
                [shape((dec_piece, dec_units), F32), shape((enc_piece, proj_own), LOW)] + [dec_vector] * 9,
                have.dec_up.addends(),
            )
            have.proj_core = core(have.dec_up[1])

    def down():
        if have.dec_down.advance():
            have.dec_down = call(
                dec_down_share_kernel,
                [
                    shape((dec_piece, dec_units), F32),
                    shape((dec_kinds, dec_piece), F32),
                    shape((dec_inner, dec_piece), F32),
                ],
                have.dec_down.addends(),
            )

    def finish():
        while isinstance(have.mlp, Chain):
            mlp()
        while isinstance(have.attn, Chain):
            attn()
        while isinstance(have.dec_up, Chain):
            up()
        while isinstance(have.dec_down, Chain):
            down()

    def norm_add():
        own_norm = have.attn[-1]
        have.norm = call(
            norm_add_kernel, [shape((8, enc_piece), F32)], [own_norm, have.norm_core]
        )[0]
        have.norm_far = swap(have.norm, TENSOR, 2)

    def norm_share():
        have.norm_grads = call(
            norm_share_kernel, [enc_vector] * 2, [have.norm, have.norm_far]
        )

    def proj_far():
        have.proj_far = swap(jnp.stack([have.dec_up[1], have.proj_core]), TENSOR, 2)

    def proj_share():
        have.proj_grad = call(
            proj_kernel,
            [shape((enc_piece, dec_width), F32)],
            [have.dec_up[1], have.proj_core, have.proj_far],
            scalars=[place],
        )[0]

    def decoded_share():
        have.decoded = call(
            decoded_kernel,
            [shape((chips, patches, dec_width // parts), F32)],
            [decoded_keep, decoded_got, decoded_far],
            scalars=[place],
        )[0]

    order = (
        dec_up, pair, mlp_back, add_back, mlp_early, lat_core, up_split, mlp_weights, dec_down, cross_back,
        attn_back, down_split, attn_weights, add_grad, up, mlp, down, attn, mlp, up, up, cross_grad, down, up,
        attn, down, band_grads, down, attn, finish, norm_add, proj_far, decoded_share, proj_share, norm_share,
    )
    for step in order:
        step()
    decoded, band_grad, norm_grads = have.decoded, have.band_grad, have.norm_grads
    enc_up_grad, enc_down_grad = have.mlp
    enc_qkv_grad, enc_out_grad, *enc_vecs = have.attn
    dec_up_grad, _, *dec_vecs = have.dec_up
    dec_down_grad, dec_qkv_grad, dec_out_grad = have.dec_down
    proj_grad = have.proj_grad
    return (
        decoded,
        band_grad,
        *norm_grads,
        enc_qkv_grad.reshape(3, enc_inner, enc_piece),
        enc_out_grad,
        enc_vecs[0],
        enc_vecs[1],
        enc_vecs[2],
        enc_up_grad,
        enc_vecs[3],
        enc_down_grad.T,
        enc_vecs[4],
        proj_grad,
        dec_vecs[6],
        dec_vecs[7],
        dec_vecs[0],
        dec_vecs[1],
        dec_qkv_grad.reshape(3, dec_inner, dec_piece),
        dec_out_grad,
        dec_vecs[2],
        dec_vecs[3],
        dec_vecs[4],
        dec_up_grad,
        dec_vecs[8],
        dec_down_grad.T,
        dec_vecs[5],
    )


def solution(mesh):
    in_specs = (
        P(DP, None, TENSOR, None),
        P(DP),
        P(DP, None),
        P(),
        P(),
        P(None, TENSOR, None),
        P(TENSOR, None),
        P(),
        P(),
        P(),
        P(None, TENSOR),
        P(TENSOR),
        P(TENSOR, None),
        P(),
        P(),
        P(),
        P(),
        P(),
        P(),
        P(None, TENSOR, None),
        P(TENSOR, None),
        P(),
        P(),
        P(),
        P(None, TENSOR),
        P(),
        P(TENSOR, None),
        P(),
        P(DP, None, None),
    )
    out_specs = (
        P(DP, None, TENSOR),
        P(DP, None, TENSOR, None),
        P(DP),
        P(DP),
        P(None, TENSOR, DP),
        P(TENSOR, DP),
        P(DP),
        P(DP),
        P(DP),
        P(DP, TENSOR),
        P((TENSOR, DP)),
        P(TENSOR, DP),
        P(DP),
        P(DP, None),
        P(DP),
        P(DP),
        P(DP),
        P(DP),
        P(None, TENSOR, DP),
        P(TENSOR, DP),
        P(DP),
        P(DP),
        P(DP),
        P(DP, TENSOR),
        P((TENSOR, DP)),
        P(TENSOR, DP),
        P(DP),
    )
    return jax.shard_map(body, mesh=mesh, in_specs=in_specs, out_specs=out_specs, check_vma=False)
```

```python
import functools
import math
import types

import jax
import jax.numpy as jnp
from jax import lax
from jax.experimental import pallas as pl
from jax.experimental.pallas import tpu as pltpu
from jax.sharding import PartitionSpec as P

HEAD = 64
EPSILON = 1e-05
SCALE = HEAD ** (-0.5)
VMEM_BYTES = 30 * 1024 * 1024
F32 = jnp.float32
LOW = jnp.bfloat16
NN = (((1,), (0,)), ((), ()))
NT = (((1,), (1,)), ((), ()))
TN = (((0,), (0,)), ((), ()))
VEC_ROWS = 16
DP, TENSOR = "dp", "tensor"
Y, Z, PAIRED = range(3)
ATTN, UP, DOWN = Y, Z, Y


def dot(left, right, dims=NN):
    return lax.dot_general(left, right, dims, preferred_element_type=F32)


def col_sum(values):
    return jnp.sum(values, 0, keepdims=True)


def vec(ref):
    return ref[...][None, :]


def norm_parts(stream):
    center = stream - jnp.mean(stream, -1, keepdims=True)
    inverse = lax.rsqrt(jnp.mean(center * center, -1, keepdims=True) + EPSILON)
    return center * inverse, inverse


def norm_back(grad, xhat, inverse, gain):
    scaled = grad * gain
    mean_q = jnp.mean(scaled, -1, keepdims=True)
    mean_qx = jnp.mean(scaled * xhat, -1, keepdims=True)
    return inverse * (scaled - mean_q - xhat * mean_qx)


def gelu_parts(hidden):
    phi = 0.5 + 0.5 * lax.erf(hidden * (0.5**0.5))
    density = jnp.exp(hidden * hidden * -0.5) * (1.0 / math.sqrt(2.0 * math.pi))
    return hidden * phi, phi + hidden * density


def softmax_rows(scores):
    weights = jnp.exp(scores - jnp.max(scores, -1, keepdims=True))
    return weights * (1.0 / jnp.sum(weights, -1, keepdims=True))


def same_chip(rows, length):
    first = lax.broadcasted_iota(jnp.int32, (rows, rows), 0) // length
    second = lax.broadcasted_iota(jnp.int32, (rows, rows), 1) // length
    return first == second


def attend(queries, keyset, mask):
    scores = dot(queries, keyset, NT) * SCALE
    if mask is not None:
        scores = jnp.where(mask, scores, -1e30)
    return softmax_rows(scores)


def attend_back(probs, queries, keyset, valset, grad_mixed):
    grad_probs = dot(grad_mixed, valset, NT)
    grad_values = dot(probs.astype(LOW), grad_mixed, TN)
    grad_scores = probs * (grad_probs - jnp.sum(grad_probs * probs, -1, keepdims=True))
    score_low = grad_scores.astype(LOW)
    grad_queries = dot(score_low, keyset) * SCALE
    grad_keys = dot(score_low, queries, TN) * SCALE
    return grad_queries.astype(LOW), grad_keys.astype(LOW), grad_values.astype(LOW)


class Line:
    def __init__(self):
        self.token = None

    def call(self, body, out_shape, args, scalars=(), after=(), scratch=(), in_place=False, vmem=VMEM_BYTES):
        after = list(after) + ([] if self.token is None else [self.token])
        specs = [pl.BlockSpec(memory_space=pltpu.SMEM) for _ in scalars]
        for arg in args:
            specs.append(pl.BlockSpec(memory_space=pltpu.HBM if isinstance(arg, InHbm) else pltpu.VMEM))
        args = [arg.array if isinstance(arg, InHbm) else arg for arg in args]
        specs += [pl.BlockSpec(memory_space=pl.ANY) for _ in after]
        inputs = len(scalars) + len(args)
        outputs = len(out_shape)
        out_specs = []
        for out in out_shape:
            in_hbm = isinstance(out, InHbm)
            out_specs.append(pl.BlockSpec(memory_space=pltpu.HBM if in_hbm else pltpu.VMEM))
        out_shape = [out.array if isinstance(out, InHbm) else out for out in out_shape]
        out_shape = [jax.ShapeDtypeStruct(out.shape, out.dtype) for out in out_shape]

        def wrapped(*refs):
            outs = refs[inputs + len(after) :]
            outs[outputs][...] = jnp.zeros_like(outs[outputs])
            body(*refs[:inputs], *outs[:outputs], *outs[outputs + 1 :])

        *found, self.token = pl.pallas_call(
            wrapped,
            out_shape=out_shape + [jax.ShapeDtypeStruct((8, 128), F32)],
            in_specs=specs,
            out_specs=out_specs + [pl.BlockSpec(memory_space=pltpu.VMEM)],
            scratch_shapes=list(scratch),
            input_output_aliases={inputs - 1: 0} if in_place else {},
            compiler_params=pltpu.CompilerParams(vmem_limit_bytes=vmem),
            cost_estimate=pl.CostEstimate(flops=1, bytes_accessed=1, transcendentals=0),
            name=(body.func if isinstance(body, functools.partial) else body).__name__,
        )(*scalars, *args, *after)
        return found


class InHbm:
    def __init__(self, array):
        self.array = array


def steps_of(blocks, kind):
    steps = list(range(blocks.bit_length() - 1))
    if kind == Z:
        steps[:2] = [1, 0]
    if kind == PAIRED:
        steps.remove(1)
    return steps


def place_of(value, blocks, kind):
    steps = steps_of(blocks, kind)
    result = 0
    for place, bit in enumerate(steps):
        result = result | (((value >> bit) & 1) << (len(steps) - 1 - place))
    return result


def spot_of(place_ref, block, blocks, kind):
    return place_ref[1 + kind] ^ place_of(block, blocks, kind)


def put_block(keep, send, lead, place, half, rows, columns, values):
    @pl.when(place < half)
    def _():
        keep[lead + (place, rows, columns)] = values

    @pl.when(place >= half)
    def _():
        send[lead + (place - half, rows, columns)] = values


def chip_of(step, rank, own_chips):
    part, index = step // own_chips, step % own_chips
    apart = 2 * (part % 2) + part // 2
    return (rank ^ apart) * own_chips + index


def put_rows(parts, first, values):
    for part in parts:
        if first < part.shape[0]:
            part[first : first + values.shape[0]] = values
            return
        first -= part.shape[0]


def get_rows(parts, first, count):
    found = []
    for part in parts:
        size = part.shape[0]
        if first < size and count > 0:
            taken = min(count, size - first)
            found.append(part[first : first + taken])
            count -= taken
            first = size
        first -= size
    return found[0] if len(found) == 1 else jnp.concatenate(found, 0)


def band_mean_kernel(place_ref, count_ref, all_ref, visible_ref, *parts, own_chips):
    *parts, bands_ref, arrived = parts
    rank = place_ref[0]
    chips, bands, own, width = bands_ref.shape
    copies = []
    for step in range(chips):
        spot = chip_of(step, rank, own_chips)
        copies.append(pltpu.make_async_copy(all_ref.at[spot], bands_ref.at[step], arrived.at[step]))
        copies[-1].start()
    length = visible_ref.shape[1]
    patch = lax.broadcasted_iota(jnp.int32, (own, length), 0) + rank * own
    for step in range(chips):
        spot = chip_of(step, rank, own_chips)
        count = count_ref[spot]
        copies[step].wait()
        means = []
        for first in range(0, own, 16):
            span = slice(first, first + 16)
            total = bands_ref[step, 0, span].astype(F32)
            for band in range(1, bands):
                used = jnp.where(band < count, 1.0, 0.0).astype(F32)
                total = total + bands_ref[step, band, span].astype(F32) * used
            means.append((total / count.astype(F32)).astype(LOW))
        chosen = visible_ref[pl.ds(spot, 1)] == patch
        chosen = jnp.where(chosen, 1.0, 0.0).astype(LOW)
        values = dot(chosen, jnp.concatenate(means, 0), TN).astype(LOW)
        put_rows(parts, step * length, values)


def enc_attn_kernel(*refs, length):
    tok, (gain, shift, qkv_w, out_w) = refs[:4], refs[4:8]
    parts, (normed_ref, qkv_ref, mixed_ref, prob_ref) = refs[8:11], refs[11:]
    rows = normed_ref.shape[0] // 2
    inner = out_w.shape[0]
    block = 2 * length
    mask = same_chip(block, length)
    for group in range(2):
        span = slice(group * rows, (group + 1) * rows)
        xhat, _ = norm_parts(get_rows(tok, group * rows, rows).astype(F32))
        normed = (xhat * vec(gain) + vec(shift)).astype(LOW)
        normed_ref[span] = normed
        qkv = dot(normed, qkv_w[...], NT).astype(LOW)
        qkv_ref[span] = qkv
        blocks = []
        for first in range(0, rows, block):
            heads = []
            for head in range(inner // HEAD):
                at = [
                    qkv[first : first + block, k * inner + head * HEAD : k * inner + (head + 1) * HEAD]
                    for k in range(3)
                ]
                probs = attend(at[0], at[1], mask)
                prob_ref[head, group * rows + first : group * rows + first + block] = probs
                heads.append(dot(probs.astype(LOW), at[2]).astype(LOW))
            blocks.append(jnp.concatenate(heads, 1))
        mixed = jnp.concatenate(blocks, 0)
        mixed_ref[span] = mixed
        part = dot(mixed, out_w[...]).astype(LOW)
        for first in range(0, rows, block):
            put_rows(parts, group * rows + first, part[first : first + block])


def own_columns(values, which, blocks):
    piece = values.shape[1] // blocks
    kinds = []
    for bit in range(2):
        starts = [(4 * run + 2 * bit) * piece for run in range(blocks // 4)]
        kinds.append(jnp.concatenate([values[:, start : start + 2 * piece] for start in starts], 1))
    return jnp.where(which == 0, kinds[0], kinds[1])


def enc_mlp_kernel(*refs):
    tok, sums = refs[:4], refs[4:8]
    out_bias, gain, shift, up_w, up_bias, down_w = refs[8:14]
    parts, (normed_ref, act_ref, slope_ref) = refs[14:18], refs[18:]
    rows = normed_ref.shape[0] // 2
    block = rows // 2
    for group in range(2):
        span = slice(group * rows, (group + 1) * rows)
        middle = get_rows(tok, group * rows, rows).astype(F32) + vec(out_bias)
        middle = middle + get_rows(sums, group * rows, rows).astype(F32)
        xhat, _ = norm_parts(middle)
        normed = (xhat * vec(gain) + vec(shift)).astype(LOW)
        normed_ref[span] = normed
        activation, slope = gelu_parts(dot(normed, up_w[...]) + vec(up_bias))
        act_low, slope_low = activation.astype(LOW), slope.astype(LOW)
        act_ref[span] = act_low
        slope_ref[span] = slope_low
        part = dot(act_low, down_w[...]).astype(LOW)
        for first in range(0, rows, block):
            put_rows(parts, group * rows + first, part[first : first + block])


def enc_out_kernel(tok, total, out_bias, own, other, down_bias, low_ref):
    low_ref[...] = (
        tok[...].astype(F32)
        + total[...].astype(F32)
        + vec(out_bias)
        + own[...].astype(F32)
        + other[...].astype(F32)
        + vec(down_bias)
    ).astype(LOW)


def enc_mlp_back_kernel(lat_pair, lat_core, proj_w, slope_ref, up_w, down_w, *refs):
    lat = (lat_pair.at[0], lat_pair.at[1], lat_core.at[0], lat_core.at[1])
    parts, (out_ref, low_ref, hidden_ref, vec_ref) = refs[:3], refs[3:]
    rows = out_ref.shape[0] // 2
    block = rows // 2
    down_sum, up_sum = 0.0, 0.0
    for group in range(2):
        span = slice(group * rows, (group + 1) * rows)
        grad_out = dot(get_rows(lat, group * rows, rows), proj_w[...], NT)
        out_ref[span] = grad_out
        grad_low = grad_out.astype(LOW)
        low_ref[span] = grad_low
        grad_hidden = dot(grad_low, down_w[...], NT) * slope_ref[span].astype(F32)
        hidden_low = grad_hidden.astype(LOW)
        hidden_ref[span] = hidden_low
        down_sum = down_sum + col_sum(grad_out)
        up_sum = up_sum + col_sum(grad_hidden)
        part = dot(hidden_low, up_w[...], NT).astype(LOW)
        for first in range(0, rows, block):
            put_rows(parts, group * rows + first, part[first : first + block])
    vec_ref[...] = jnp.concatenate(
        [down_sum, up_sum, jnp.zeros((vec_ref.shape[0] - 2, down_sum.shape[1]), F32)], 0
    )


def enc_mlp_early_kernel(early_ref, up_w, up_bias, act_ref, slope_ref):
    activation, slope = gelu_parts(dot(early_ref[...], up_w[...]) + vec(up_bias))
    act_ref[...] = activation.astype(LOW)
    slope_ref[...] = slope.astype(LOW)


def enc_mlp_weights_kernel(
    place_ref, normed_ref, hidden_ref, low_ref, act_ref, early_ref, early_act, early_slope, lat_pair, lat_core,
    proj_w, down_w, keep, send
):
    half = keep.shape[0]
    blocks = 4 * half
    width, units = normed_ref.shape[1], hidden_ref.shape[1]
    piece = width // blocks
    which = place_ref[4] // 2
    lat = jnp.concatenate([lat_pair[0], lat_pair[1], lat_core[0], lat_core[1]], 0)
    low = dot(lat, proj_w[...], NT).astype(LOW)
    hidden = (dot(low, down_w[...], NT) * early_slope[...].astype(F32)).astype(LOW)
    for kind in range(2):
        if kind == 0:
            found = dot(own_columns(normed_ref[...], which, blocks), hidden_ref[...], TN)
            found = found + dot(own_columns(early_ref[...], which, blocks), hidden, TN)
        else:
            found = dot(own_columns(low_ref[...], which, blocks), act_ref[...], TN)
            found = found + dot(own_columns(low, which, blocks), early_act[...], TN)
        columns = slice(kind * units, (kind + 1) * units)
        for block in range(blocks // 2):
            values = found[block * piece : (block + 1) * piece].astype(LOW)
            place = spot_of(place_ref, 4 * (block // 2) + block % 2, blocks, PAIRED)
            put_block(keep, send, (), place, half, slice(0, piece), columns, values)


def enc_attn_back_kernel(*refs, length):
    tok, sums, backs = refs[:4], refs[4:8], refs[8:12]
    out_bias, mlp_gain, out_ref, qkv_ref, qkv_w, out_w, prob_ref = refs[12:19]
    parts, (mid_ref, low_ref, grad_qkv_ref, vec_ref) = refs[19:22], refs[22:]
    rows = out_ref.shape[0] // 2
    inner = out_w.shape[0]
    block = 2 * length
    found = [0.0] * 5
    for group in range(2):
        span = slice(group * rows, (group + 1) * rows)
        stream = get_rows(tok, group * rows, rows).astype(F32)
        total = get_rows(sums, group * rows, rows).astype(F32)
        xhat, inverse = norm_parts(stream + total + vec(out_bias))
        grad = get_rows(backs, group * rows, rows).astype(F32)
        found[0] = found[0] + col_sum(grad * xhat)
        found[1] = found[1] + col_sum(grad)
        grad_middle = out_ref[span] + norm_back(grad, xhat, inverse, vec(mlp_gain))
        mid_ref[span] = grad_middle
        found[2] = found[2] + col_sum(grad_middle)
        middle_low = grad_middle.astype(LOW)
        low_ref[span] = middle_low
        grad_mixed = dot(middle_low, out_w[...], NT).astype(LOW)
        blocks = []
        for first in range(0, rows, block):
            near = slice(group * rows + first, group * rows + first + block)
            grads = ([], [], [])
            for head in range(inner // HEAD):
                at = [
                    qkv_ref[near, k * inner + head * HEAD : k * inner + (head + 1) * HEAD]
                    for k in range(3)
                ]
                own = grad_mixed[first : first + block, head * HEAD : (head + 1) * HEAD]
                for kind, values in enumerate(attend_back(prob_ref[head, near], *at, own)):
                    grads[kind].append(values)
            blocks.append(jnp.concatenate(grads[0] + grads[1] + grads[2], 1))
        grad_qkv = jnp.concatenate(blocks, 0)
        grad_qkv_ref[span] = grad_qkv
        partial = dot(grad_qkv, qkv_w[...])
        part = partial.astype(LOW)
        for first in range(0, rows, block):
            put_rows(parts, group * rows + first, part[first : first + block])
        xhat, _ = norm_parts(stream)
        found[3] = found[3] + col_sum(partial * xhat)
        found[4] = found[4] + col_sum(partial)
    vec_ref[...] = jnp.concatenate(
        found + [jnp.zeros((vec_ref.shape[0] - 5, found[0].shape[1]), F32)], 0
    )


def enc_attn_weights_kernel(
    place_ref, normed_ref, grad_qkv_ref, low_ref, mixed_ref, vec_mlp, vec_attn, keep, send
):
    half = keep.shape[0]
    blocks = 2 * half
    width = normed_ref.shape[1]
    qkv = dot(normed_ref[...], grad_qkv_ref[...], TN)
    out = dot(low_ref[...], mixed_ref[...], TN)
    vectors = jnp.concatenate([vec_mlp[...], vec_attn[...]], 0)
    piece = width // blocks
    first = keep.shape[1] - VEC_ROWS
    for block in range(blocks):
        at = slice(block * piece, (block + 1) * piece)
        place = spot_of(place_ref, block, blocks, ATTN)
        values = jnp.concatenate([qkv[at], out[at]], 1).astype(LOW)
        put_block(keep, send, (), place, half, slice(0, piece), slice(None), values)
        put_block(
            keep, send, (), place, half, slice(first, first + VEC_ROWS), slice(0, piece),
            vectors[:, at].astype(LOW),
        )


def band_zero_kernel(place_ref, count_ref, out_ref, blank, left, *, own_chips):
    chips, bands = out_ref.shape[:2]
    blank[...] = jnp.zeros_like(blank)
    spots = [chip_of(step, place_ref[0], own_chips) for step in range(chips)]

    def copy_of(step, band):
        return pltpu.make_async_copy(blank, out_ref.at[spots[step], band], left.at[step, band])

    for step in range(chips):

        def begin(band, carry, step=step):
            copy_of(step, band).start()
            return carry

        lax.fori_loop(count_ref[spots[step]], bands, begin, 0)
    for step in range(chips):

        def finish(band, carry, step=step):
            copy_of(step, band).wait()
            return carry

        lax.fori_loop(count_ref[spots[step]], bands, finish, 0)


def band_grad_kernel(place_ref, count_ref, *refs, own_chips):
    tok, backs, (mid_ref, gain, visible_ref, _) = refs[:4], refs[4:8], refs[8:12]
    out_ref, stage, left = refs[12:]
    rank = place_ref[0]
    chips, bands, own, width = out_ref.shape
    length = visible_ref.shape[1]
    spots = [chip_of(step, rank, own_chips) for step in range(chips)]
    counts = [count_ref[spot] for spot in spots]

    def copy_of(source, step, band):
        return pltpu.make_async_copy(
            stage.at[source], out_ref.at[spots[step], band], left.at[step, band]
        )

    patch = lax.broadcasted_iota(jnp.int32, (own, length), 0) + rank * own
    for step in range(chips):
        first = step * length
        xhat, inverse = norm_parts(get_rows(tok, first, length).astype(F32))
        back = get_rows(backs, first, length).astype(F32)
        grad = mid_ref[first : first + length] + norm_back(back, xhat, inverse, vec(gain))
        grad = grad / counts[step].astype(F32)
        chosen = visible_ref[pl.ds(spots[step], 1)] == patch
        chosen = jnp.where(chosen, 1.0, 0.0).astype(LOW)
        high = grad.astype(LOW)
        rest = (grad - high.astype(F32)).astype(LOW)
        stage[step] = dot(chosen, high) + dot(chosen, rest)

        def fill(band, carry, step=step):
            copy_of(step, step, band).start()
            return carry

        lax.fori_loop(0, counts[step], fill, 0)
    for step in range(chips):

        def finish(band, carry, step=step):
            copy_of(step, step, band).wait()
            return carry

        lax.fori_loop(0, counts[step], finish, 0)


def dec_kernel(
    place_ref, enc_low, proj_w, proj_bias, mask_token, position, visible_ref,
    attn_gain, attn_shift, out_bias, mlp_gain, mlp_shift, down_bias, up_bias,
    w0, w1, w2, w3, cotangent,
    decoded_keep, decoded_send, grad_latent_ref, n1_ref, n2_ref, gml_ref, act_ref, hid_ref,
    gqkv_ref, mixed_ref, vec_ref, upvec_ref,
    slope_scr, prob_scr, qkv_scr,
):
    weights = (w0, w1, w2, w3)
    parts = len(weights)
    chips, length = visible_ref.shape
    patches, width = position.shape
    kinds = 3 * HEAD
    inner = kinds + HEAD
    units = up_bias.shape[0] // parts
    up_at, down_at = slice(inner, inner + width), slice(inner + width, inner + width + units)
    spans = [slice(chip * patches, (chip + 1) * patches) for chip in range(chips)]
    latent = dot(enc_low[...], proj_w[...]) + vec(proj_bias)
    high = latent.astype(LOW)
    rest = (latent - high.astype(F32)).astype(LOW)
    streams, chosen, seen = [], [], []
    for chip in range(chips):
        near = slice(chip * length, (chip + 1) * length)
        hit = lax.broadcasted_iota(jnp.int32, (patches, length), 0) == visible_ref[chip : chip + 1]
        hit = jnp.where(hit, 1.0, 0.0)
        is_visible = jnp.sum(hit, 1, keepdims=True)
        hit = hit.astype(LOW)
        filled = dot(hit, high[near]) + dot(hit, rest[near])
        streams.append(filled + (1.0 - is_visible) * vec(mask_token) + position[...])
        chosen.append(hit)
        seen.append(is_visible)
    stream = jnp.concatenate(streams, 0)
    xhat1, inverse1 = norm_parts(stream)
    n1 = (xhat1 * vec(attn_gain) + vec(attn_shift)).astype(LOW)
    n1_ref[...] = n1
    for part, weight in enumerate(weights):
        qkv_scr[part] = dot(n1, weight[0:kinds], NT).astype(LOW)

    def qkv_of(part, span):
        return [qkv_scr[part, span, k * HEAD : (k + 1) * HEAD] for k in range(3)]

    for part in range(parts):
        for span in spans:
            queries, keyset, valset = qkv_of(part, span)
            probs = attend(queries, keyset, None)
            prob_scr[part, span] = probs
            mixed_ref[part, span] = dot(probs.astype(LOW), valset).astype(LOW)
    out_all = jnp.concatenate([weight[kinds:inner] for weight in weights], 0)
    mixed = jnp.concatenate([mixed_ref[part] for part in range(parts)], 1)
    middle = stream + dot(mixed, out_all) + vec(out_bias)
    xhat2, inverse2 = norm_parts(middle)
    n2 = (xhat2 * vec(mlp_gain) + vec(mlp_shift)).astype(LOW)
    n2_ref[...] = n2
    total = middle + vec(down_bias)
    for part, weight in enumerate(weights):
        spot = pl.multiple_of((place_ref[0] ^ part) * units, units)
        bias = up_bias[pl.ds(spot, units)][None, :]
        activation, slope = gelu_parts(dot(n2, weight[up_at]) + bias)
        act_low = activation.astype(LOW)
        act_ref[part] = act_low
        slope_scr[part] = slope.astype(LOW)
        total = total + dot(act_low, weight[down_at])
    column = width // parts
    half = parts // 2
    for part in range(parts):
        apart = place_ref[0] ^ part
        for chip, span in enumerate(spans):
            values = total[span, part * column : (part + 1) * column].astype(LOW)

            @pl.when(apart % 2 == 0)
            def _(values=values, apart=apart, chip=chip):
                decoded_keep[apart // 2, chip] = values

            @pl.when(apart % 2 == 1)
            def _(values=values, apart=apart, chip=chip):
                decoded_send[apart // 2, chip] = values

    grad_low = cotangent[...]
    grad_out = grad_low.astype(F32)
    grad_n2 = 0.0
    up_sums = []
    for part, weight in enumerate(weights):
        grad_hidden = dot(grad_low, weight[down_at], NT) * slope_scr[part].astype(F32)
        hidden_low = grad_hidden.astype(LOW)
        hid_ref[part] = hidden_low
        up_sums.append(col_sum(grad_hidden))
        grad_n2 = grad_n2 + dot(hidden_low, weight[up_at], NT)
    grad_middle = grad_out + norm_back(grad_n2, xhat2, inverse2, vec(mlp_gain))
    mlp_gain_sum, mlp_shift_sum = col_sum(grad_n2 * xhat2), col_sum(grad_n2)
    middle_low = grad_middle.astype(LOW)
    gml_ref[...] = middle_low
    grad_mixed = dot(middle_low, out_all, NT).astype(LOW)
    grad_n1 = 0.0
    for part, weight in enumerate(weights):
        for span in spans:
            own = grad_mixed[span, part * HEAD : (part + 1) * HEAD]
            found = attend_back(prob_scr[part, span], *qkv_of(part, span), own)
            gqkv_ref[part, span] = jnp.concatenate(found, 1)
        grad_n1 = grad_n1 + dot(gqkv_ref[part], weight[0:kinds])
    grad_stream = grad_middle + norm_back(grad_n1, xhat1, inverse1, vec(attn_gain))
    stream_low = grad_stream.astype(LOW)
    for chip, span in enumerate(spans):
        near = slice(chip * length, (chip + 1) * length)
        grad_latent_ref[near] = dot(chosen[chip], stream_low[span], TN).astype(LOW)
    seen_sum = col_sum(grad_stream * jnp.concatenate(seen, 0))
    vec_ref[...] = jnp.concatenate(
        [
            col_sum(grad_n1 * xhat1),
            col_sum(grad_n1),
            col_sum(grad_middle),
            mlp_gain_sum,
            mlp_shift_sum,
            col_sum(grad_out),
            seen_sum,
            col_sum(grad_stream) - seen_sum,
        ],
        0,
    )
    upvec_ref[...] = jnp.concatenate(up_sums + [jnp.zeros((8 - parts, units), F32)], 0)


def put_quarter(keep, sends, part, place, values):
    if part % 2 == 0:
        keep[part // 2, place] = values
        return
    half = sends[0].shape[0]
    put_block(sends[part - 1], sends[part], (), place, half, slice(None), slice(None), values)


def dec_up_kernel(
    place_ref, n2_ref, hid_ref, enc_low, latent, vec_ref, upvec_ref, keep, *sends
):
    parts, _, units = hid_ref.shape
    blocks = keep.shape[1]
    width, enc_width = n2_ref.shape[1], enc_low.shape[1]
    piece, enc_piece = width // blocks, enc_width // blocks
    column = latent.shape[1] // parts
    left = n2_ref[...].T
    left_proj = enc_low[...].T
    half_column = latent.shape[1] // parts // 2
    blank = jnp.zeros((half_column - 9, width), F32)
    for part in (1, 3, 0, 2):
        vectors = jnp.concatenate([vec_ref[...], upvec_ref[part : part + 1], blank], 0).T
        up = dot(left, hid_ref[part])
        spot = pl.multiple_of((place_ref[0] ^ part) * column, column)
        proj = dot(left_proj, latent[:, pl.ds(spot, column)])
        for block in range(blocks):
            first = block * enc_piece
            rest = proj[first + piece : first + enc_piece]
            rest = jnp.concatenate([rest[:, :half_column], rest[:, half_column:]], 0)
            values = jnp.concatenate(
                [
                    up[block * piece : (block + 1) * piece],
                    proj[first : first + piece],
                    rest,
                    vectors[block * piece : (block + 1) * piece],
                ],
                1,
            )
            place = spot_of(place_ref, block, blocks, UP)
            put_quarter(keep, sends, part, place, values.astype(LOW))


def dec_down_kernel(
    place_ref, cot_ref, act_ref, n1_ref, gqkv_ref, gml_ref, mixed_ref, keep, *sends
):
    parts = act_ref.shape[0]
    blocks = keep.shape[1]
    piece = n1_ref.shape[1] // blocks
    left_down, left_qkv, left_out = cot_ref[...].T, n1_ref[...].T, gml_ref[...].T
    for part in (1, 3, 0, 2):
        values = jnp.concatenate(
            [
                dot(left_down, act_ref[part]),
                dot(left_qkv, gqkv_ref[part]),
                dot(left_out, mixed_ref[part]),
            ],
            1,
        ).astype(LOW)
        for block in range(blocks):
            place = spot_of(place_ref, block, blocks, DOWN)
            put_quarter(keep, sends, part, place, values[block * piece : (block + 1) * piece])


def add_kernel(keep, got_0, got_1, out):
    half = got_0.shape[0]
    out[0:half] = (keep[0:half].astype(F32) + got_0[...].astype(F32)).astype(LOW)
    out[half:] = (keep[half:].astype(F32) + got_1[...].astype(F32)).astype(LOW)


def add_two_kernel(far_keep, far_got, near_keep, near_got, normed, far, near, early):
    early[...] = normed[...]
    far[...] = (far_keep[...].astype(F32) + far_got[...].astype(F32)).astype(LOW)
    near[...] = (near_keep[...].astype(F32) + near_got[...].astype(F32)).astype(LOW)


def add_with_kernel(keep, got_0, got_1, rest, out):
    rows = keep.shape[0]
    add_kernel(keep, got_0, got_1, out.at[0:rows])
    out[rows:] = rest[...]


def add_crossed_kernel(own, other, first, second):
    half = first.shape[0]
    first[...] = (own[0:half].astype(F32) + other[half : 2 * half].astype(F32)).astype(LOW)
    second[...] = (own[half : 2 * half].astype(F32) + other[0:half].astype(F32)).astype(LOW)


def assemble_kernel(place_ref, *refs):
    for sources, target in ((refs[0:4], refs[8]), (refs[4:8], refs[9])):
        for apart, source in enumerate(sources):
            rows = source.shape[0]
            spot = pl.multiple_of((place_ref[4] ^ apart) * rows, rows)
            target[pl.ds(spot, rows)] = source[...]


def copy_kernel(source, out):
    out[...] = source[...]


def pair_kernel(first, second, out):
    out[0] = first[...]
    out[1] = second[...]


def pick_kernel(place_ref, source, out):
    rows = out.shape[0]
    out[...] = source[pl.ds(pl.multiple_of(place_ref[4] * rows, rows), rows)]


class Behind:
    def __init__(self, array, places, rows):
        self.array, self.places, self.rows = array, places, rows

    def __getitem__(self, place):
        if len(self.array.shape) == 3:
            return self.array[place]
        first = self.array.shape[0] - (self.places - place) * self.rows
        return self.array[first : first + self.rows]


def total_of(arrays, place):
    total = arrays[0][place].astype(F32)
    for array in arrays[1:]:
        total = total + array[place].astype(F32)
    return total


def fold_kernel(*refs):
    arrays, (next_keep, next_send) = refs[:-2], refs[-2:]
    half = next_keep.shape[0]
    arrays = [Behind(array, 2 * half, arrays[0].shape[1]) for array in arrays]
    for place in range(half):
        next_send[place] = total_of(arrays, half + place).astype(LOW)
        next_keep[place] = total_of(arrays, place).astype(LOW)


def sum_kernel(*refs):
    for place in range(refs[-1].shape[0]):
        refs[-1][place] = total_of(refs[:-1], place).astype(LOW)


def split_kernel(keep, got_0, got_1, got_2, got_3, near_0, near_1, far_0, far_1):
    half = got_0.shape[0]
    pieces = ((0, got_0, near_0), (0, got_1, near_1), (1, got_2, far_0), (1, got_3, far_1))
    for number, (part, got, target) in enumerate(pieces):
        for place in range(half):
            first = keep[part, number % 2 * half + place].astype(F32)
            target[place] = (first + got[place].astype(F32)).astype(LOW)


def split_whole_kernel(keep, got_0, got_1, got_2, got_3, near, far):
    half = got_0.shape[0]
    split_kernel(
        keep, got_0, got_1, got_2, got_3,
        near.at[0:half], near.at[half:], far.at[0:half], far.at[half:],
    )


def enc_mlp_share_kernel(keep, got, up_ref, down_ref):
    piece, units = up_ref.shape
    total = total_of((keep, got), 0)
    up_ref[...] = total[:piece, :units]
    down_ref[...] = total[:piece, units:]


def enc_attn_share_kernel(keep, got, qkv_ref, out_ref, *vectors):
    total = total_of((keep, got), 0)
    inner, piece = out_ref.shape
    qkv_ref[...] = total[:piece, : 3 * inner].T
    out_ref[...] = total[:piece, 3 * inner :].T
    for row, vector in zip((10, 8, 9, 1, 0), vectors[:5], strict=True):
        vector[...] = total[total.shape[0] - VEC_ROWS + row, :piece]
    norms = total[total.shape[0] - VEC_ROWS :, :piece]
    vectors[5][...] = jnp.concatenate([norms[11:13], jnp.zeros((6, piece), F32)], 0)


def dec_up_share_kernel(keep, got, up_ref, proj_ref, *vectors):
    total = total_of((keep, got), 0)
    piece, units = up_ref.shape
    enc_piece, column = proj_ref.shape
    up_ref[...] = total[:, :units]
    rest = enc_piece - piece
    ends = total[:, units + column :]
    tail = jnp.concatenate([ends[:rest, : column // 2], ends[rest:, : column // 2]], 1)
    proj_ref[...] = jnp.concatenate([total[:, units : units + column], tail], 0).astype(LOW)
    rows = ends.T
    for row, vector in enumerate(vectors):
        vector[...] = rows[column // 2 + row, :piece]


def dec_down_share_kernel(keep, got, down_ref, qkv_ref, out_ref):
    total = total_of((keep, got), 0)
    units = down_ref.shape[1]
    inner = out_ref.shape[0]
    down_ref[...] = total[:, :units]
    qkv_ref[...] = total[:, units : units + 3 * inner].T
    out_ref[...] = total[:, units + 3 * inner :].T


def norm_share_kernel(own, core, far, far_core, gain_ref, shift_ref):
    total = own[...] + core[...] + far[...] + far_core[...]
    gain_ref[...] = total[0]
    shift_ref[...] = total[1]


def proj_kernel(place_ref, own, core, far, out):
    column = own.shape[1]
    for apart, part in enumerate((own[...], core[...], far[0], far[1])):
        spot = pl.multiple_of((place_ref[0] ^ apart) * column, column)
        out[:, pl.ds(spot, column)] = part.astype(F32)


def decoded_kernel(place_ref, keep, got, far, out):
    chips = keep.shape[1]
    for index in range(chips):
        pieces = (keep[0, index], got[0, index], far[0, index], far[1, index])
        for apart, piece in enumerate(pieces):
            out[(place_ref[0] ^ apart) * chips + index] = piece.astype(F32)


def swap(values, axis, apart):
    size = lax.axis_size(axis)
    return lax.ppermute(values, axis, [(i, i ^ apart) for i in range(size)])


class Chain:
    def __init__(self, line, keep, send, steps):
        self.line, self.keep, self.step = line, list(keep), 0
        self.steps = steps
        self.got = self.exchange(send)

    def exchange(self, send):
        return swap(send, DP, 1 << self.steps[self.step])

    def fold(self):
        half = self.places() // 2
        out = jax.ShapeDtypeStruct((half,) + self.got.shape[1:], LOW)
        self.step += 1
        keep, send = self.line.call(
            fold_kernel, [out, out], [*self.keep, self.got]
        )
        self.keep = [keep]
        self.got = self.exchange(send)

    def places(self):
        return self.got.shape[0]

    def advance(self):
        if self.places() == 1:
            return True
        self.fold()
        return False

    def addends(self):
        return [*self.keep, self.got]


class DecChain(Chain):
    def __init__(self, line, near, far, steps):
        self.line, self.near, self.far, self.step = line, near, far, 0
        self.steps, self.got = steps, None

    def advance(self):
        if self.got is not None:
            return super().advance()
        if len(self.near) == 1:
            out = jax.ShapeDtypeStruct((self.near[0].shape[0] // 2,) + self.near[0].shape[1:], LOW)
            keep, send = self.line.call(fold_kernel, [out, out], [self.near[0], self.far[0]])
            self.keep = [keep]
        else:
            out = jax.ShapeDtypeStruct(self.near[1].shape, LOW)
            send = self.line.call(sum_kernel, [out], [self.near[1], self.far[1]])[0]
            self.keep = [self.near[0], self.far[0]]
        self.got = self.exchange(send)
        return False


def body(
    band_patches,
    band_counts,
    visible_index,
    enc_attn_gain,
    enc_attn_shift,
    enc_qkv_weight,
    enc_out_weight,
    enc_out_bias,
    enc_mlp_gain,
    enc_mlp_shift,
    enc_up_weight,
    enc_up_bias,
    enc_down_weight,
    enc_down_bias,
    proj_weight,
    proj_bias,
    mask_token,
    dec_attn_gain,
    dec_attn_shift,
    dec_qkv_weight,
    dec_out_weight,
    dec_out_bias,
    dec_mlp_gain,
    dec_mlp_shift,
    dec_up_weight,
    dec_up_bias,
    dec_down_weight,
    dec_down_bias,
    cotangent,
):
    parts = lax.axis_size(TENSOR)
    blocks = lax.axis_size(DP)
    rank = lax.axis_index(TENSOR)
    number = lax.axis_index(DP)
    place = jnp.stack(
        [rank, *(place_of(number, blocks, kind) for kind in (Y, Z, PAIRED)), number % 4]
    ).astype(jnp.int32)
    chips, length = visible_index.shape
    band_total, own_patches = band_patches.shape[1:3]
    own_chips = chips // parts
    enc_width = band_patches.shape[3]
    patches, dec_width = cotangent.shape[1:]
    enc_inner = enc_out_weight.shape[0]
    enc_units = enc_up_weight.shape[1]
    dec_units = dec_up_weight.shape[1]
    dec_inner = dec_out_weight.shape[0]
    dec_kinds = 3 * dec_inner
    rows = chips * length
    shape = jax.ShapeDtypeStruct
    half_rows = shape((rows // 2, enc_width), LOW)
    quarter_rows = shape((rows // 4, enc_width), LOW)
    all_rows = shape((rows, enc_width), LOW)
    wide_rows = shape((rows, enc_width), F32)
    hidden_shape = shape((rows, enc_units), LOW)
    vec_shape = shape((8, enc_width), F32)
    part_shapes = [half_rows, quarter_rows, quarter_rows]

    line = Line()
    call = line.call

    def core(values):
        return swap(values, TENSOR, 1)

    def add_cores(parts, after=()):
        keep, *sends = parts
        return call(add_kernel, [half_rows], [keep, *map(core, sends)], after=after)[0]

    def cross(own, after=()):
        pair = call(
            add_crossed_kernel, [quarter_rows] * 2, [own, swap(own, TENSOR, 2)], after=after
        )
        return [*pair, *map(core, pair)]

    w_own = jnp.concatenate(
        [
            dec_qkv_weight.reshape(dec_kinds, dec_width),
            dec_out_weight,
            dec_up_weight,
            dec_down_weight,
        ],
        0,
    )
    angles = lax.broadcasted_iota(F32, (patches, dec_width // 2), 0) * jnp.exp(
        lax.broadcasted_iota(F32, (patches, dec_width // 2), 1)
        * (-math.log(10000.0) / (dec_width // 2))
    )
    position = jnp.concatenate([jnp.sin(angles), jnp.cos(angles)], 1)
    own_visible = lax.dynamic_slice_in_dim(visible_index, rank * own_chips, own_chips, 0)
    own_cotangent = lax.dynamic_slice_in_dim(cotangent, rank * own_chips, own_chips, 0)
    own_cotangent = own_cotangent.reshape(-1, dec_width)
    parts_here = call(
        functools.partial(band_mean_kernel, own_chips=own_chips),
        part_shapes,
        [InHbm(band_patches), visible_index],
        scalars=[place, band_counts],
        scratch=[pltpu.VMEM(band_patches.shape, LOW), pltpu.SemaphoreType.DMA((chips,))],
        vmem=50 * 1024 * 1024,
        after=[],
    )
    own = add_cores(parts_here)
    band_zeros = call(
        functools.partial(band_zero_kernel, own_chips=own_chips),
        [InHbm(shape(band_patches.shape, F32))],
        [],
        scalars=[place, band_counts],
        scratch=[
            pltpu.VMEM((own_patches, enc_width), F32),
            pltpu.SemaphoreType.DMA((chips, band_total)),
        ],
    )[0]
    tok = cross(own)

    w_core = core(w_own)
    w_rows = w_own.shape[0] // 4
    w_pick = call(
        pick_kernel, [shape((w_rows, dec_width), LOW)], [w_own], scalars=[place]
    )[0]
    w_fourths = [swap(w_pick, TENSOR, 2)]
    w_fourths.append(swap(w_fourths[0], DP, 1))
    w_fourths.append(swap(w_fourths[0], DP, 2))
    w_fourths.append(swap(w_fourths[2], DP, 1))

    qkv_w = enc_qkv_weight.reshape(3 * enc_inner, enc_width)
    *parts_here, enc_n1, enc_qkv, enc_mixed, enc_probs = call(
        functools.partial(enc_attn_kernel, length=length),
        part_shapes
        + [
            all_rows, shape((rows, 3 * enc_inner), LOW), shape((rows, enc_inner), LOW),
            shape((enc_inner // HEAD, rows, 2 * length), F32),
        ],
        [*tok, enc_attn_gain, enc_attn_shift, qkv_w, enc_out_weight],
        after=[position, own_cotangent, own_visible],
    )
    own = add_cores(parts_here, [w_fourths[0]])
    sums = cross(own, [w_fourths[1], w_fourths[2]])
    *parts_here, enc_n2, enc_act, enc_slope = call(
        enc_mlp_kernel,
        [quarter_rows] * 4 + [all_rows, hidden_shape, hidden_shape],
        [
            *tok, *sums, enc_out_bias, enc_mlp_gain, enc_mlp_shift,
            enc_up_weight, enc_up_bias, enc_down_weight,
        ],
    )
    far, near, early = call(
        add_two_kernel,
        [quarter_rows] * 2 + [all_rows],
        [parts_here[1], core(parts_here[3]), parts_here[0], core(parts_here[2]), enc_n2],
    )
    early = swap(early, DP, 2)
    w_x, w_diag = call(
        assemble_kernel,
        [shape(w_own.shape, LOW)] * 2,
        [*w_fourths, *map(core, w_fourths)],
        scalars=[place],
    )
    enc_low = call(
        enc_out_kernel,
        [quarter_rows],
        [tok[0], sums[0], enc_out_bias, near, swap(far, TENSOR, 2), enc_down_bias],
    )[0]

    dec_rows = own_chips * patches
    dec_all = shape((dec_rows, dec_width), LOW)
    dec_hidden = shape((parts, dec_rows, dec_units), LOW)
    dec_column = shape((parts // 2, own_chips, patches, dec_width // parts), LOW)
    (
        decoded_keep, decoded_send, grad_latent, dec_n1, dec_n2, dec_gml, dec_act, dec_hid,
        dec_gqkv, dec_mixed, dec_vec, dec_upvec,
    ) = call(
        dec_kernel,
        [
            dec_column, dec_column, shape((own_chips * length, dec_width), LOW), dec_all, dec_all,
            dec_all, dec_hidden, dec_hidden, shape((parts, dec_rows, 3 * HEAD), LOW),
            shape((parts, dec_rows, HEAD), LOW), shape((8, dec_width), F32), shape((8, dec_units), F32),
        ],
        [
            enc_low, proj_weight, proj_bias, mask_token, position, own_visible, dec_attn_gain,
            dec_attn_shift, dec_out_bias, dec_mlp_gain, dec_mlp_shift, dec_down_bias, dec_up_bias,
            w_own, w_core, w_x, w_diag, own_cotangent,
        ],
        scalars=[place],
        scratch=[
            pltpu.VMEM((parts, dec_rows, dec_units), LOW),
            pltpu.VMEM((parts, dec_rows, patches), F32),
            pltpu.VMEM((parts, dec_rows, 3 * HEAD), LOW),
        ],
    )
    lat_far = swap(grad_latent, TENSOR, 2)
    decoded_got = core(decoded_send)
    decoded_far = swap(jnp.stack([decoded_keep[1], decoded_got[1]]), TENSOR, 2)
    dec_piece = dec_width // blocks
    enc_piece = enc_width // blocks
    enc_rows = -(-enc_piece // 16) * 16
    proj_own = dec_width // parts
    enc_vector = shape((enc_piece,), F32)
    dec_vector = shape((dec_piece,), F32)
    have = types.SimpleNamespace()

    def dec_bundle(kernel, columns, args):
        sends = [shape((blocks // 2, dec_piece, columns), LOW)] * 4
        keep, *sends = call(
            kernel, [shape((2, blocks, dec_piece, columns), LOW)] + sends, args, scalars=[place]
        )
        return [keep, *map(core, sends)]

    def dec_up():
        args = [dec_n2, dec_hid, enc_low, grad_latent, dec_vec, dec_upvec]
        have.dec_up = dec_bundle(dec_up_kernel, dec_units + 2 * proj_own, args)

    def dec_down():
        args = [own_cotangent, dec_act, dec_n1, dec_gqkv, dec_gml, dec_mixed]
        have.dec_down = dec_bundle(dec_down_kernel, dec_units + 4 * dec_inner, args)

    def up_split():
        out = shape(have.dec_up[0].shape[1:], LOW)
        near, far = call(split_whole_kernel, [out] * 2, have.dec_up)
        have.dec_up = DecChain(line, [near], [swap(far, TENSOR, 2)], steps_of(blocks, UP))

    def down_split():
        out = shape((blocks // 2,) + have.dec_down[0].shape[2:], LOW)
        *near, far_0, far_1 = call(split_kernel, [out] * 4, have.dec_down)
        have.dec_down = DecChain(line, near, [far_0, swap(far_1, TENSOR, 2)], steps_of(blocks, DOWN))

    def pair():
        have.lat = call(
            pair_kernel, [shape((2,) + grad_latent.shape, LOW)], [grad_latent, lat_far]
        )[0]
        have.lat_core = core(have.lat)
        have.lat_z = swap(have.lat, DP, 2)

    def lat_core():
        have.lat_z = call(copy_kernel, [have.lat], [have.lat_z])[0]
        have.lat_z_core = core(have.lat_z)

    def mlp_back():
        *have.parts, have.out_grad, have.gol, have.hid, have.vec_mlp = call(
            enc_mlp_back_kernel,
            part_shapes + [wide_rows, all_rows, hidden_shape, vec_shape],
            [have.lat, have.lat_core, proj_weight, enc_slope, enc_up_weight, enc_down_weight],
        )

    def add_back():
        have.own = add_cores(have.parts)

    def cross_back():
        have.backs = cross(have.own)

    def mlp_early():
        have.early = call(
            enc_mlp_early_kernel,
            [hidden_shape] * 2,
            [early, enc_up_weight, enc_up_bias],
        )

    def mlp_weights():
        bundle = shape((blocks // 4, enc_rows, 2 * enc_units), LOW)
        keep, send = call(
            enc_mlp_weights_kernel,
            [bundle] * 2,
            [
                enc_n2, have.hid, have.gol, enc_act, early, *have.early,
                have.lat_z, have.lat_z_core,
                proj_weight, enc_down_weight,
            ],
            scalars=[place],
        )
        have.mlp = Chain(line, [keep], send, steps_of(blocks, PAIRED))

    def attn_back():
        *have.parts, have.mid, have.gml, have.gqkv, have.vec_attn = call(
            functools.partial(enc_attn_back_kernel, length=length),
            part_shapes + [wide_rows, all_rows, shape((rows, 3 * enc_inner), LOW), vec_shape],
            [
                *tok, *sums, *have.backs, enc_out_bias, enc_mlp_gain, have.out_grad, enc_qkv, qkv_w,
                enc_out_weight, enc_probs,
            ],
        )

    def attn_weights():
        bundle = shape((blocks // 2, enc_rows + VEC_ROWS, 4 * enc_inner), LOW)
        keep, send = call(
            enc_attn_weights_kernel,
            [bundle, bundle],
            [enc_n1, have.gqkv, have.gml, enc_mixed, have.vec_mlp, have.vec_attn],
            scalars=[place],
        )
        have.attn = Chain(line, [keep], send, steps_of(blocks, ATTN))

    def add_grad():
        keep, *sends = have.parts
        chain = have.dec_down
        rest = chain.far[0].reshape(-1, enc_width)
        have.own = call(
            add_with_kernel,
            [shape((rows // 2 + rest.shape[0], enc_width), LOW)],
            [keep, *map(core, sends), rest],
        )[0]
        have.far = chain.far[0] = swap(have.own, TENSOR, 2)

    def cross_grad():
        halves = call(
            add_crossed_kernel, [quarter_rows] * 2, [have.own, have.far]
        )
        have.grads = [*halves, *map(core, halves)]

    def band_grads():
        have.band_grad = call(
            functools.partial(band_grad_kernel, own_chips=own_chips),
            [InHbm(shape(band_patches.shape, F32))],
            [*tok, *have.grads, have.mid, enc_attn_gain, visible_index, InHbm(band_zeros)],
            scalars=[place, band_counts],
            scratch=[
                pltpu.VMEM((chips, own_patches, enc_width), F32),
                pltpu.SemaphoreType.DMA((chips, band_total)),
            ],
            in_place=True,
        )[0]

    def mlp():
        if have.mlp.advance():
            have.mlp = call(
                enc_mlp_share_kernel,
                [shape((enc_piece, enc_units), F32)] * 2,
                have.mlp.addends(),
            )

    def attn():
        if have.attn.advance():
            have.attn = call(
                enc_attn_share_kernel,
                [shape((3 * enc_inner, enc_piece), F32), shape((enc_inner, enc_piece), F32)]
                + [enc_vector] * 5
                + [shape((8, enc_piece), F32)],
                have.attn.addends(),
            )
            have.norm_core = core(have.attn[-1])
            have.norm_far = [swap(have.attn[-1], TENSOR, apart) for apart in (2, 3)]

    def up():
        if have.dec_up.advance():
            have.dec_up = call(
                dec_up_share_kernel,
                [shape((dec_piece, dec_units), F32), shape((enc_piece, proj_own), LOW)] + [dec_vector] * 9,
                have.dec_up.addends(),
            )
            have.proj_core = core(have.dec_up[1])

    def down():
        if have.dec_down.advance():
            have.dec_down = call(
                dec_down_share_kernel,
                [
                    shape((dec_piece, dec_units), F32),
                    shape((dec_kinds, dec_piece), F32),
                    shape((dec_inner, dec_piece), F32),
                ],
                have.dec_down.addends(),
            )

    def finish():
        while isinstance(have.mlp, Chain):
            mlp()
        while isinstance(have.attn, Chain):
            attn()
        while isinstance(have.dec_up, Chain):
            up()
        while isinstance(have.dec_down, Chain):
            down()

    def norm_share():
        own = have.attn[-1]
        parts = [own, have.norm_core, *have.norm_far]
        have.norm_grads = call(norm_share_kernel, [enc_vector] * 2, parts)

    def proj_far():
        have.proj_far = swap(jnp.stack([have.dec_up[1], have.proj_core]), TENSOR, 2)

    def proj_share():
        have.proj_grad = call(
            proj_kernel,
            [shape((enc_piece, dec_width), F32)],
            [have.dec_up[1], have.proj_core, have.proj_far],
            scalars=[place],
        )[0]

    def decoded_share():
        have.decoded = call(
            decoded_kernel,
            [shape((chips, patches, dec_width // parts), F32)],
            [decoded_keep, decoded_got, decoded_far],
            scalars=[place],
        )[0]

    order = (
        dec_up, pair, mlp_back, add_back, mlp_early, lat_core, up_split, mlp_weights, dec_down, cross_back,
        attn_back, down_split, attn_weights, add_grad, up, mlp, down, attn, mlp, up, up, cross_grad, down, up,
        attn, down, band_grads, down, attn, finish, proj_far, decoded_share, proj_share, norm_share,
    )
    for step in order:
        step()
    decoded, band_grad, norm_grads = have.decoded, have.band_grad, have.norm_grads
    enc_up_grad, enc_down_grad = have.mlp
    enc_qkv_grad, enc_out_grad, *enc_vecs = have.attn
    dec_up_grad, _, *dec_vecs = have.dec_up
    dec_down_grad, dec_qkv_grad, dec_out_grad = have.dec_down
    proj_grad = have.proj_grad
    return (
        decoded,
        band_grad,
        *norm_grads,
        enc_qkv_grad.reshape(3, enc_inner, enc_piece),
        enc_out_grad,
        enc_vecs[0],
        enc_vecs[1],
        enc_vecs[2],
        enc_up_grad,
        enc_vecs[3],
        enc_down_grad.T,
        enc_vecs[4],
        proj_grad,
        dec_vecs[6],
        dec_vecs[7],
        dec_vecs[0],
        dec_vecs[1],
        dec_qkv_grad.reshape(3, dec_inner, dec_piece),
        dec_out_grad,
        dec_vecs[2],
        dec_vecs[3],
        dec_vecs[4],
        dec_up_grad,
        dec_vecs[8],
        dec_down_grad.T,
        dec_vecs[5],
    )


def solution(mesh):
    in_specs = (
        P(DP, None, TENSOR, None),
        P(DP),
        P(DP, None),
        P(),
        P(),
        P(None, TENSOR, None),
        P(TENSOR, None),
        P(),
        P(),
        P(),
        P(None, TENSOR),
        P(TENSOR),
        P(TENSOR, None),
        P(),
        P(),
        P(),
        P(),
        P(),
        P(),
        P(None, TENSOR, None),
        P(TENSOR, None),
        P(),
        P(),
        P(),
        P(None, TENSOR),
        P(),
        P(TENSOR, None),
        P(),
        P(DP, None, None),
    )
    out_specs = (
        P(DP, None, TENSOR),
        P(DP, None, TENSOR, None),
        P(DP),
        P(DP),
        P(None, TENSOR, DP),
        P(TENSOR, DP),
        P(DP),
        P(DP),
        P(DP),
        P(DP, TENSOR),
        P((TENSOR, DP)),
        P(TENSOR, DP),
        P(DP),
        P(DP, None),
        P(DP),
        P(DP),
        P(DP),
        P(DP),
        P(None, TENSOR, DP),
        P(TENSOR, DP),
        P(DP),
        P(DP),
        P(DP),
        P(DP, TENSOR),
        P((TENSOR, DP)),
        P(TENSOR, DP),
        P(DP),
    )
    return jax.shard_map(body, mesh=mesh, in_specs=in_specs, out_specs=out_specs, check_vma=False)
```
